32 devices in a mesh: seq: 8 (over z, x), batch: 4 (over y, core).
Axes of the slice: x: 2, y: 2, z: 4, core: 2. Of those that a mesh axis runs over, the one named last changes fastest.
Arguments:
- tokens: bfloat16 [2048, 12, 576], P('seq', 'batch'), may hold values from -6 to 6
- positions: int32 [2048, 12], P('seq', 'batch'), may hold values from 0 to 2047, as said below
- norm_attn: float32 [576], replicated, may hold values from 0.5 to 1.5
- w_query: bfloat16 [576, 576], replicated, may hold values from -0.5 to 0.5
- w_key: bfloat16 [576, 192], replicated, may hold values from -0.25 to 0.25
- w_value: bfloat16 [576, 192], replicated, may hold values from -0.25 to 0.25
- w_out: bfloat16 [576, 576], replicated, may hold values from -1 to 1
- norm_mlp: float32 [576], replicated, may hold values from 0.5 to 1.5
- w_gate: bfloat16 [576, 1536], replicated, may hold values from -0.25 to 0.25
- w_up: bfloat16 [576, 1536], replicated, may hold values from -0.25 to 0.25
- w_down: bfloat16 [1536, 576], replicated, may hold values from -0.15625 to 0.15625
- cotangent: bfloat16 [2048, 12, 576], P('seq', 'batch'), may hold values from -6 to 6
Outputs:
- block_out: bfloat16 [2048, 12, 576], P('seq', 'batch')
- d_tokens: bfloat16 [2048, 12, 576], P('seq', 'batch')
- g_norm_attn: float32 [576], replicated
- g_query: float32 [576, 576], replicated
- g_key: float32 [576, 192], replicated
- g_value: float32 [576, 192], replicated
- g_out: float32 [576, 576], replicated
- g_norm_mlp: float32 [576], replicated
- g_gate: float32 [576, 1536], replicated
- g_up: float32 [576, 1536], replicated
- g_down: float32 [1536, 576], replicated
The draws below stay inside these ranges and needn't reach their ends.
Inputs may be any that keep to these rules, and one draw needn't show every extreme that they name: Along a sequence positions rise by one and return to 0 where a new document begins; sequence 0 is a single document.
All inputs are finite; a program needn't handle non-finite values.
Results may differ from the reference program's by a relative error of at most 0.019.
Values may be sent and summed in bfloat16 or wider, within the bound.
No kernel may reach another device: no remote copies, remote signals or barrier semaphores. Data moves between devices by JAX's collectives and lax.ppermute only.
A program may use at most 192 MiB of HBM per device.

```python
import math
import jax
import jax.numpy as jnp
from jax import lax

D = 576
HEADS = 9
KV_HEADS = 3
HEAD_DIM = 64
FF = 1536
LENGTH = 2048
SEQUENCES = 12


def draw_positions(key, part):
    key = jax.random.fold_in(key, 7)
    restart = jax.random.randint(key, (LENGTH, SEQUENCES), 0, 512) == 0
    token_index = jnp.arange(LENGTH, dtype=jnp.int32)[:, None] * jnp.ones((1, SEQUENCES), jnp.int32)
    column = jnp.arange(SEQUENCES, dtype=jnp.int32)[None, :]
    restart = restart & (column > 0)
    begins = jnp.where(restart, token_index, 0)
    doc_begin = lax.cummax(begins, axis=0)
    return (token_index - doc_begin).astype(jnp.int32)


def block_scale(stream_key, dims, cuts, least, largest):
    level = 1.0
    for axis_at, parts in cuts:
        heights = jax.random.uniform(jax.random.fold_in(jax.random.fold_in(stream_key, 6), axis_at), (parts,), jnp.float32, least / len(cuts), largest / len(cuts))
        level = level * jnp.repeat(jnp.exp(heights), dims[axis_at] // parts).reshape((-1,) + (1,) * (len(dims) - 1 - axis_at))
    return level


def noise(own_key, extent, spread, bound, split=(), held_as=jnp.bfloat16):
    gain = block_scale(own_key, extent, split, -0.22, 0.18) if split else 1.0
    array = jax.random.normal(own_key, extent, jnp.float32) * spread * gain
    return jnp.minimum(jnp.maximum(array, -bound), bound).astype(held_as)


def setup_inputs(seed: int = 0) -> dict:
    splits = jax.random.split(jax.random.key(seed), 13)
    return {
        "tokens": noise(splits[0], (LENGTH, SEQUENCES, D), 1.0, 6.0, ((0, 8), (1, 4))),
        "positions": draw_positions(jax.random.fold_in(splits[12], 71), 0),
        "norm_attn": jnp.clip(1.0 + 0.1 * jax.random.normal(splits[2], (D,), jnp.float32), 0.5, 1.5),
        "w_query": noise(splits[3], (D, D), (D // 4) ** -0.5, 0.5),
        "w_key": noise(splits[4], (D, KV_HEADS * HEAD_DIM), D ** -0.5, 0.25),
        "w_value": noise(splits[5], (D, KV_HEADS * HEAD_DIM), D ** -0.5, 0.25),
        "w_out": noise(splits[6], (D, D), (D // 16) ** -0.5, 1.0),
        "norm_mlp": jnp.clip(1.0 + 0.1 * jax.random.normal(splits[7], (D,), jnp.float32), 0.5, 1.5),
        "w_gate": noise(splits[8], (D, FF), D ** -0.5, 0.25),
        "w_up": noise(splits[9], (D, FF), D ** -0.5, 0.25),
        "w_down": noise(splits[10], (FF, D), FF ** -0.5, 0.15625),
        "cotangent": noise(splits[11], (LENGTH, SEQUENCES, D), 1.0, 6.0, ((0, 8), (1, 4))),
    }


@jax.custom_vjp
def low(v):
    return lax.optimization_barrier(v.astype(jnp.bfloat16)).astype(jnp.float32)

@jax.custom_vjp
def low_back(v):
    return v

def low_keep(v):
    return (low(v), None)

def low_pass(kept, grad):
    return (grad,)

def back_keep(v):
    return (v, None)

def back_low(kept, grad):
    return (low(grad),)
low.defvjp(low_keep, low_pass)
low_back.defvjp(back_keep, back_low)
eps_norm = 1e-05
mask_low = -1e+30
highest = lax.Precision.HIGHEST

def product(left, right):
    return jnp.dot(left, right, precision=highest)

def rope_tables(places, half_size):
    frequency = jnp.exp(jnp.arange(half_size, dtype=jnp.float32) * (-math.log(10000.0) / half_size))
    angles = places.astype(jnp.float32)[:, None] * frequency
    return (jnp.cos(angles)[:, None, :], jnp.sin(angles)[:, None, :])

def rotate(vector, cos_part, sin_part):
    half_size = vector.shape[-1] // 2
    lower_half = vector[..., :half_size]
    upper_half = vector[..., half_size:]
    return jnp.concatenate([lower_half * cos_part - upper_half * sin_part, upper_half * cos_part + lower_half * sin_part], axis=-1)

def rms_normed(hidden):
    return hidden * lax.rsqrt(lax.optimization_barrier(jnp.mean(hidden * hidden, axis=-1, keepdims=True)) + eps_norm)

def block_layer(hidden_in, places, norm_attn, w_query, w_key, w_value, w_out, norm_mlp, w_gate, w_up, w_down):
    length = hidden_in.shape[0]
    per_group = HEADS // KV_HEADS
    attn_in = low(rms_normed(hidden_in) * norm_attn)
    cos_part, sin_part = rope_tables(places, HEAD_DIM // 2)
    query_lin = low_back(product(attn_in, w_query)).reshape(length, HEADS, HEAD_DIM)
    queries = low(rotate(query_lin, cos_part, sin_part) * 0.125).reshape(length, KV_HEADS, per_group, HEAD_DIM)
    key_lin = low_back(product(attn_in, w_key)).reshape(length, KV_HEADS, HEAD_DIM)
    key_rot = low(rotate(key_lin, cos_part, sin_part))
    values = low(low_back(product(attn_in, w_value))).reshape(length, KV_HEADS, HEAD_DIM)
    query_block = min(512, length)
    key_index = jnp.arange(length, dtype=jnp.int32)

    def attend(block_index):
        first_row = block_index * query_block
        query_part = lax.dynamic_slice_in_dim(queries, first_row, query_block, 0)
        scores = low_back(jnp.einsum('qgrd,kgd->grqk', query_part, key_rot, precision=highest))
        query_index = first_row + jnp.arange(query_block, dtype=jnp.int32)
        visible_mask = key_index[None, :] <= query_index[:, None]
        scores = jnp.where(visible_mask, scores, mask_low)
        row_peak = lax.optimization_barrier(jnp.max(scores, axis=-1, keepdims=True))
        weights = jnp.exp(scores - row_peak)
        soft_probs = low(weights / lax.optimization_barrier(jnp.sum(weights, axis=-1, keepdims=True)))
        return jnp.einsum('grqk,kgd->qgrd', soft_probs, values, precision=highest)
    attended = lax.map(jax.checkpoint(attend), jnp.arange(length // query_block, dtype=jnp.int32))
    attn_out = low(low_back(attended.reshape(length, HEADS * HEAD_DIM)))
    hidden_mid = hidden_in + low_back(product(attn_out, w_out))
    mlp_in = low(rms_normed(hidden_mid) * norm_mlp)
    gate_proj = low_back(product(mlp_in, w_gate))
    up_proj = low_back(product(mlp_in, w_up))
    hidden_act = low(jax.nn.silu(gate_proj) * up_proj)
    return hidden_mid + product(hidden_act, w_down)

def reference(tokens, positions, norm_attn, w_query, w_key, w_value, w_out, norm_mlp, w_gate, w_up, w_down, cotangent):
    weights = (norm_attn.astype(jnp.float32), w_query.astype(jnp.float32), w_key.astype(jnp.float32), w_value.astype(jnp.float32), w_out.astype(jnp.float32), norm_mlp.astype(jnp.float32), w_gate.astype(jnp.float32), w_up.astype(jnp.float32), w_down.astype(jnp.float32))
    inputs_all = jnp.transpose(tokens.astype(jnp.float32), (1, 0, 2))
    places_all = jnp.transpose(positions, (1, 0))
    pulls_all = jnp.transpose(cotangent.astype(jnp.float32), (1, 0, 2))

    def one_sequence(totals, sequence_item):
        hidden_in, places_one, pull_one = sequence_item

        def layer_of(hidden, *params):
            return block_layer(hidden, places_one, *params)
        output, backward = jax.vjp(layer_of, hidden_in, *weights)
        gradients = backward(pull_one)
        totals = tuple((total_part + grad_part for total_part, grad_part in zip(totals, gradients[1:])))
        return (totals, (output, gradients[0]))
    initial = tuple((jnp.zeros(weight.shape, jnp.float32) for weight in weights))
    totals, (outputs, d_inputs) = lax.scan(one_sequence, initial, (inputs_all, places_all, pulls_all))
    return (jnp.transpose(outputs, (1, 0, 2)).astype(jnp.bfloat16), jnp.transpose(d_inputs, (1, 0, 2)).astype(jnp.bfloat16), totals[0], totals[1], totals[2], totals[3], totals[4], totals[5], totals[6], totals[7], totals[8])
```

```python
import functools
import math

import jax
import jax.numpy as jnp
from jax import lax
from jax.experimental import pallas as pl
from jax.experimental.pallas import tpu as pltpu
from jax.sharding import PartitionSpec as P

HEADS = 9
KV_HEADS = 3
HEAD_DIM = 64
PER = HEADS // KV_HEADS
LANES = 128

eps_norm = 1e-05
mask_low = -1e30
f32 = jnp.float32
bf16 = jnp.bfloat16

NN = (((1,), (0,)), ((), ()))
NT = (((1,), (1,)), ((), ()))
TN = (((0,), (0,)), ((), ()))
UNROLL = 4


def dot(left, right, dims=NN):
    return lax.dot_general(left, right, dims, preferred_element_type=f32)


def params(mib):
    return pltpu.CompilerParams(vmem_limit_bytes=mib * 1024 * 1024)


def full_spec(shape):
    zeros = (0,) * len(shape)
    return pl.BlockSpec(shape, lambda *_: zeros)


def lane_index(rows):
    return lax.broadcasted_iota(jnp.int32, (rows, LANES), 1)


def swap_halves(tile):
    half = HEAD_DIM // 2
    lane = lane_index(tile.shape[0])
    return jnp.where(
        lane % HEAD_DIM < half, pltpu.roll(tile, LANES - half, 1), pltpu.roll(tile, half, 1)
    )


def head_tiles(lin):
    rows, width = lin.shape
    if width % LANES:
        lin = jnp.concatenate([lin, jnp.zeros((rows, HEAD_DIM), lin.dtype)], axis=1)
    return [lin[:, at : at + LANES] for at in range(0, lin.shape[1], LANES)]


def pre_kernel(
    x_ref, norm_ref, wq_ref, wk_ref, wv_ref, cos_ref, sin_ref, a_ref, q_ref, kv_ref
):
    x = x_ref[0].T.astype(f32)
    rows, width = x.shape
    scale = lax.rsqrt(jnp.sum(x * x, axis=-1, keepdims=True) * (1.0 / width) + eps_norm)
    a = (x * scale * norm_ref[...]).astype(bf16)
    a_ref[0] = a
    cos, sin = cos_ref[0], sin_ref[0]
    low_half = lane_index(rows) < HEAD_DIM

    def turn(tile):
        return tile * cos + swap_halves(tile) * sin

    keys = [turn(tile) for tile in head_tiles(dot(a, wk_ref[...], NT))]
    values = head_tiles(dot(a, wv_ref[...], NT))
    for g in range(KV_HEADS):
        key, value = keys[g // 2], values[g // 2]
        if g % 2 == 0:
            value = pltpu.roll(value, HEAD_DIM, 1)
        else:
            key = pltpu.roll(key, HEAD_DIM, 1)
        kv_ref[0, :, g * LANES : (g + 1) * LANES] = jnp.where(low_half, key, value).astype(bf16)
    queries = [turn(tile) * 0.125 for tile in head_tiles(dot(a, wq_ref[...]))]
    for head in range(HEADS):
        tile = queries[head // 2]
        if head % 2:
            tile = pltpu.roll(tile, HEAD_DIM, 1)
        group, place = divmod(head, PER)
        q_ref[0, group, place * rows : (place + 1) * rows, :] = jnp.where(
            low_half, tile, 0.0
        ).astype(bf16)


def pre_call(x, norm, w_query, w_key, w_value, cos, sin):
    seqs, width, rows = x.shape
    row = lambda shape: pl.BlockSpec((1,) + shape, lambda s: (s,) + (0,) * len(shape))
    return pl.pallas_call(
        pre_kernel,
        grid=(seqs,),
        in_specs=[
            row((width, rows)),
            full_spec((1, width)),
            full_spec(w_query.shape),
            full_spec(w_key.shape),
            full_spec(w_value.shape),
            row((rows, LANES)),
            row((rows, LANES)),
        ],
        out_specs=[
            row((rows, width)),
            row((KV_HEADS, PER * rows, LANES)),
            row((rows, KV_HEADS * LANES)),
        ],
        out_shape=[
            jax.ShapeDtypeStruct((seqs, rows, width), bf16),
            jax.ShapeDtypeStruct((seqs, KV_HEADS, PER * rows, LANES), bf16),
            jax.ShapeDtypeStruct((seqs, rows, KV_HEADS * LANES), bf16),
        ],
        compiler_params=params(16),
        name="project",
    )(x, norm, w_query, w_key, w_value, cos, sin)


def causal_part(rows, heads):
    key = lax.broadcasted_iota(jnp.int32, (rows, rows), 0)
    query = lax.broadcasted_iota(jnp.int32, (rows, rows), 1)
    return jnp.concatenate([key <= query] * heads, axis=1)


def for_blocks(ids, me, seqs, own, pieces, counts, work, zeros=None):
    if own is not None:
        for s in range(seqs):
            work(s, own[s], None, (-1, s, s))
    first = 1
    for k, (parts, count) in enumerate(zip(pieces, counts)):
        least = ids[first]
        for n in range(1, seqs * count):
            least = jnp.minimum(least, ids[first + n])
        unroll = min(count, UNROLL)

        @pl.when(least < me)
        def _(parts=parts, first=first, count=count, k=k):
            def some(c, _):
                for s in range(seqs):
                    for u in range(unroll):
                        j = c * unroll + u
                        work(s, parts[s][j], ids[first + s * count + j] < me, (k, s, j))
                return 0

            if count == unroll:
                some(0, 0)
            else:
                lax.fori_loop(0, count // unroll, some, 0)

        if zeros is not None:

            @pl.when(least >= me)
            def _(k=k):
                zeros(k)

        first += seqs * count


def forward_kernel(counts, has_own, has_state, is_last, ids, *refs):
    refs = list(refs)
    q = refs.pop(0)
    seqs, rows = q.shape[0], q.shape[2] // PER
    own = refs.pop(0) if has_own else None
    pieces = [[refs.pop(0) for _ in range(seqs)] for _ in counts]
    if has_state:
        peak_in, total_in = refs.pop(0), refs.pop(0)
    outs, (peak, total) = refs[:-2], refs[-2:]
    me = ids[0]
    if has_state:
        peak[...] = peak_in[:, 0]
        total[...] = total_in[:, 0]
    low_half = lane_index(rows) < HEAD_DIM

    def attend(s, kv, seen):
        ones_values = jnp.where(low_half, jnp.ones((), bf16), kv)
        scores = dot(kv, q[s, 0], NT)
        if seen is None:
            scores = jnp.where(causal_part(rows, PER), scores, mask_low)
            new_peak = shift = jnp.max(scores, axis=0, keepdims=True)
        else:
            old_peak = peak[s]
            top = jnp.max(scores, axis=0, keepdims=True)
            new_peak = jnp.where(seen, jnp.maximum(old_peak, top), old_peak)
            shift = jnp.where(seen, new_peak, -mask_low)
        shares = jnp.exp(scores - shift).astype(bf16)
        added = dot(shares.T, ones_values)
        if seen is None:
            total[s] = added
        else:
            total[s] = total[s] * jnp.exp(old_peak - new_peak).T + added
        peak[s] = new_peak

    for_blocks(ids, me, seqs, own, pieces, counts, lambda s, kv, seen, store: attend(s, kv, seen))
    if is_last:
        attn, log_total = outs
        group = pl.program_id(0)
        for s in range(seqs):
            acc = total[s]
            normal = acc / pltpu.roll(acc, HEAD_DIM, 1)
            sums = acc.T[0:1]
            log_total[s, 0] = peak[s] + jnp.log(sums)
            values = normal[:, HEAD_DIM:].astype(bf16)
            for g in range(KV_HEADS):

                @pl.when(group == g)
                def _(values=values, s=s, g=g):
                    for h in range(PER):
                        at = (g * PER + h) * HEAD_DIM
                        attn[s, :, at : at + HEAD_DIM] = values[h * rows : (h + 1) * rows]

    else:
        outs[0][:, 0] = peak[...]
        outs[1][:, 0] = total[...]


def piece_spec(count, rows):
    return pl.BlockSpec((count, rows, LANES), lambda g, *_: (0, 0, g))


def group_spec(seqs, *shape):
    zeros = (0,) * len(shape)
    return pl.BlockSpec((seqs, 1) + shape, lambda g, *_: (0, g) + zeros)


def forward_call(ids, q, own, pieces, state, is_last):
    seqs, groups, wide, _ = q.shape
    rows = wide // PER
    counts = [parts[0].shape[0] for parts in pieces]
    arrays, specs = [q], [group_spec(seqs, wide, LANES)]
    if own is not None:
        arrays.append(own)
        specs.append(piece_spec(seqs, rows))
    for parts, count in zip(pieces, counts):
        arrays += parts
        specs += [piece_spec(count, rows)] * seqs
    row_spec, row_shape = group_spec(seqs, 1, wide), (seqs, groups, 1, wide)
    sum_spec, sum_shape = group_spec(seqs, wide, LANES), (seqs, groups, wide, LANES)
    if state is not None:
        arrays += list(state)
        specs += [row_spec, sum_spec]
    if is_last:
        attn_shape = (seqs, rows, HEADS * HEAD_DIM)
        out_shape = [
            jax.ShapeDtypeStruct(attn_shape, bf16),
            jax.ShapeDtypeStruct(row_shape, f32),
        ]
        out_specs = [full_spec(attn_shape), row_spec]
    else:
        out_shape = [
            jax.ShapeDtypeStruct(row_shape, f32),
            jax.ShapeDtypeStruct(sum_shape, f32),
        ]
        out_specs = [row_spec, sum_spec]
    return pl.pallas_call(
        functools.partial(
            forward_kernel, counts, own is not None, state is not None, is_last
        ),
        out_shape=out_shape,
        grid_spec=pltpu.PrefetchScalarGridSpec(
            num_scalar_prefetch=1,
            grid=(groups,),
            in_specs=specs,
            out_specs=out_specs,
            scratch_shapes=[
                pltpu.VMEM((seqs, 1, wide), f32),
                pltpu.VMEM((seqs, wide, LANES), f32),
            ],
        ),
        compiler_params=params(60),
        name="attend_forward",
    )(ids, *arrays)


def backward_kernel(counts, has_own, has_state, is_last, waits, ids, *refs):
    refs = list(refs)[waits:]
    q, d_out, log_total, delta = refs[:4]
    refs = refs[4:]
    seqs, rows = q.shape[0], q.shape[2] // PER
    own = refs.pop(0) if has_own else None
    pieces = [[refs.pop(0) for _ in range(seqs)] for _ in counts]
    d_query_in = refs.pop(0) if has_state else None
    cos, sin = (refs.pop(0), refs.pop(0)) if is_last else (None, None)
    d_own = refs.pop(0) if has_own else None
    d_pieces = [[refs.pop(0) for _ in range(seqs)] for _ in counts]
    d_query_out, d_query = refs
    me = ids[0]
    if has_state:
        d_query[...] = d_query_in[:, 0]
    else:
        d_query[...] = jnp.zeros_like(d_query)

    def back(s, kv, seen, place):
        q_all, d_all = q[s, 0], d_out[s, 0]
        scores = dot(kv, q_all, NT)
        if seen is None:
            probs = jnp.exp(scores - log_total[s, 0])
            probs = jnp.where(causal_part(rows, PER), probs, 0.0)
        else:
            probs = jnp.exp(scores - jnp.where(seen, log_total[s, 0], -mask_low))
        d_probs = dot(kv, d_all, NT)
        d_scores = (probs * (d_probs - delta[s, 0])).astype(bf16)
        d_query[s] += dot(d_scores.T, kv)
        terms = (dot(probs.astype(bf16), d_all) + dot(d_scores, q_all)).astype(bf16)
        piece, s, j = place
        if piece < 0:
            d_own[s] = terms
        else:
            d_pieces[piece][s][j] = terms

    def zeros(piece):
        for s in range(seqs):
            d_pieces[piece][s][...] = jnp.zeros(d_pieces[piece][s].shape, bf16)

    for_blocks(ids, me, seqs, own, pieces, counts, back, zeros)
    if is_last:
        group = pl.program_id(0)
        for s in range(seqs):
            turned = []
            for h in range(PER):
                tile = d_query[s, h * rows : (h + 1) * rows, :] * 0.125
                turned.append(
                    (tile * cos[s] - swap_halves(tile) * sin[s])[:, :HEAD_DIM].astype(bf16)
                )
            for g in range(KV_HEADS):

                @pl.when(group == g)
                def _(turned=turned, s=s, g=g):
                    for h in range(PER):
                        at = (g * PER + h) * HEAD_DIM
                        d_query_out[s, :, at : at + HEAD_DIM] = turned[h]

    else:
        d_query_out[:, 0] = d_query[...]


def backward_call(ids, q, d_out, log_total, delta, own, pieces, d_query, tables, after=()):
    seqs, groups, wide, _ = q.shape
    rows = wide // PER
    counts = [parts[0].shape[0] for parts in pieces]
    sum_spec, sum_shape = group_spec(seqs, wide, LANES), (seqs, groups, wide, LANES)
    row_spec = group_spec(seqs, 1, wide)
    arrays = [q, d_out, log_total, delta]
    specs = [sum_spec, sum_spec, row_spec, row_spec]
    out_shape, out_specs = [], []
    if own is not None:
        arrays.append(own)
        specs.append(piece_spec(seqs, rows))
        out_shape.append(jax.ShapeDtypeStruct(own.shape, bf16))
        out_specs.append(piece_spec(seqs, rows))
    for parts, count in zip(pieces, counts):
        arrays += parts
        specs += [piece_spec(count, rows)] * seqs
        out_shape += [jax.ShapeDtypeStruct(parts[0].shape, bf16)] * seqs
        out_specs += [piece_spec(count, rows)] * seqs
    if d_query is not None:
        arrays.append(d_query)
        specs.append(sum_spec)
    is_last = tables is not None
    if is_last:
        arrays += list(tables)
        specs += [full_spec((seqs, rows, LANES))] * 2
        shape = (seqs, rows, HEADS * HEAD_DIM)
        out_shape.append(jax.ShapeDtypeStruct(shape, bf16))
        out_specs.append(full_spec(shape))
    else:
        out_shape.append(jax.ShapeDtypeStruct(sum_shape, f32))
        out_specs.append(sum_spec)
    arrays = list(after) + arrays
    specs = [pl.BlockSpec(memory_space=pl.ANY)] * len(after) + specs
    outs = pl.pallas_call(
        functools.partial(
            backward_kernel, counts, own is not None, d_query is not None, is_last, len(after)
        ),
        out_shape=out_shape,
        grid_spec=pltpu.PrefetchScalarGridSpec(
            num_scalar_prefetch=1,
            grid=(groups,),
            in_specs=specs,
            out_specs=out_specs,
            scratch_shapes=[pltpu.VMEM((seqs, wide, LANES), f32)],
        ),
        compiler_params=params(60),
        name="attend_backward",
    )(ids, *arrays)
    d_own = None
    if own is not None:
        d_own, outs = outs[0], outs[1:]
    d_pieces = [list(outs[k * seqs : (k + 1) * seqs]) for k in range(len(counts))]
    return d_own, d_pieces, outs[-1]


def middle_kernel(
    x_ref,
    cot_ref,
    attn_ref,
    w_out_ref,
    norm_ref,
    w_gate_ref,
    w_up_ref,
    w_down_ref,
    out_ref,
    b_ref,
    hid_ref,
    d_gate_ref,
    d_up_ref,
    d_mid_ref,
    d_proj_ref,
    d_out_ref,
    delta_ref,
    g_norm_ref,
):
    x = x_ref[0].T.astype(f32)
    rows, width = x.shape
    cot = cot_ref[0].T
    attn = attn_ref[0]
    mid = x + dot(attn, w_out_ref[...])
    scale = lax.rsqrt(jnp.sum(mid * mid, axis=-1, keepdims=True) * (1.0 / width) + eps_norm)
    normed = mid * scale
    b = (normed * norm_ref[...]).astype(bf16)
    b_ref[0] = b
    gate = dot(b, w_gate_ref[...])
    up = dot(b, w_up_ref[...])
    sig = 1.0 / (1.0 + jnp.exp(-gate))
    active = gate * sig
    hid = (active * up).astype(bf16)
    hid_ref[0] = hid
    out_ref[0] = (mid + dot(hid, w_down_ref[...], NT)).astype(bf16).T
    d_hid = dot(cot, w_down_ref[...])
    d_gate = (d_hid * up * sig * (1.0 + gate * (1.0 - sig))).astype(bf16)
    d_up = (d_hid * active).astype(bf16)
    d_gate_ref[0] = d_gate
    d_up_ref[0] = d_up
    d_b = dot(d_gate, w_gate_ref[...], NT) + dot(d_up, w_up_ref[...], NT)
    g_norm = jnp.sum(d_b * normed, axis=0, keepdims=True)

    @pl.when(pl.program_id(0) == 0)
    def _():
        g_norm_ref[...] = g_norm

    @pl.when(pl.program_id(0) > 0)
    def _():
        g_norm_ref[...] += g_norm

    e = d_b * norm_ref[...]
    mean = jnp.sum(e * normed, axis=-1, keepdims=True) * (1.0 / width)
    d_mid = cot.astype(f32) + scale * (e - normed * mean)
    d_mid_ref[0] = d_mid
    d_proj = d_mid.astype(bf16)
    d_proj_ref[0] = d_proj
    d_attn = dot(d_proj, w_out_ref[...], NT).astype(bf16).astype(f32)
    both = d_attn * attn.astype(f32)
    high = both.astype(bf16)
    rest = (both - high.astype(f32)).astype(bf16)
    head = lax.broadcasted_iota(jnp.int32, (16, width), 0)
    feature = lax.broadcasted_iota(jnp.int32, (16, width), 1)
    picks = jnp.where(
        (feature >= head * HEAD_DIM) & (feature < (head + 1) * HEAD_DIM), 1.0, 0.0
    ).astype(bf16)
    sums = dot(picks, high, NT) + dot(picks, rest, NT)
    high_half = lane_index(rows) >= HEAD_DIM
    padded = jnp.concatenate([d_attn, jnp.zeros((rows, HEAD_DIM), f32)], axis=1)
    for k in range(HEADS):
        at = k // 2 * LANES
        tile = padded[:, at : at + LANES]
        if k % 2 == 0:
            tile = pltpu.roll(tile, HEAD_DIM, 1)
        group, place = divmod(k, PER)
        here = slice(place * rows, (place + 1) * rows)
        d_out_ref[0, group, here, :] = jnp.where(high_half, tile, 0.0).astype(bf16)
        delta_ref[0, group, 0:1, here] = sums[k : k + 1]


def middle_call(x, cot, attn, w_out, norm, w_gate, w_up, w_down):
    seqs, width, rows = x.shape
    hidden = w_gate.shape[1]
    row = lambda *shape: pl.BlockSpec((1,) + shape, lambda s: (s,) + (0,) * len(shape))
    wide = PER * rows
    shapes = [
        ((width, rows), bf16),
        ((rows, width), bf16),
        ((rows, hidden), bf16),
        ((rows, hidden), bf16),
        ((rows, hidden), bf16),
        ((rows, width), f32),
        ((rows, width), bf16),
        ((KV_HEADS, wide, LANES), bf16),
        ((KV_HEADS, 1, wide), f32),
    ]
    return pl.pallas_call(
        middle_kernel,
        grid=(seqs,),
        in_specs=[row(width, rows), row(width, rows), row(rows, width)]
        + [
            full_spec(w_out.shape),
            full_spec((1, width)),
            full_spec(w_gate.shape),
            full_spec(w_up.shape),
            full_spec(w_down.shape),
        ],
        out_specs=[row(*shape) for shape, _ in shapes] + [full_spec((1, width))],
        out_shape=[jax.ShapeDtypeStruct((seqs,) + shape, kind) for shape, kind in shapes]
        + [jax.ShapeDtypeStruct((1, width), f32)],
        compiler_params=params(60),
        name="feed_forward",
    )(x, cot, attn, w_out, norm, w_gate, w_up, w_down)


def ffn_place(k, t, tiles):
    if k < 2:
        return k, t
    return (0, tiles + t) if t < tiles // 2 else (1, tiles + t - tiles // 2)


def out_place(t, tiles, square):
    here = (square + 1) // 2
    return (0, tiles + tiles // 2 + t) if t < here else (1, tiles + tiles // 2 + t - here)


def half_rows(places, width, parts):
    unit = 16 * (parts // 2)
    return -(-places * width // unit) * unit


def put(out_ref, place, width, tile):
    half, at = place
    out_ref[half, at * width : (at + 1) * width, :] = tile


def with_column(tile, column):
    free = lane_index(tile.shape[0]) >= HEAD_DIM
    return jnp.where(free, column, tile)


def ffn_grad_kernel(
    b_ref, cot_ref, attn_ref, d_proj_ref, g_norm_ref, hid_ref, d_gate_ref, d_up_ref, out_ref,
    done_ref,
):
    done_ref[...] = jnp.zeros_like(done_ref)
    width = b_ref.shape[1]
    hidden = hid_ref.shape[1]
    tiles, square = hidden // LANES, -(-width // LANES)
    chunk = 2 * LANES
    b_turned = b_ref[...].T
    cot_turned = jnp.concatenate([cot_ref[s] for s in range(cot_ref.shape[0])], axis=1)
    for k, (left, right) in enumerate(
        ((b_turned, d_gate_ref), (b_turned, d_up_ref), (cot_turned, hid_ref))
    ):
        for c in range(hidden // chunk):
            product = dot(left, right[:, c * chunk : (c + 1) * chunk]).astype(bf16)
            for u in range(2):
                t = 2 * c + u
                put(
                    out_ref,
                    ffn_place(k, t, tiles),
                    width,
                    product[:, u * LANES : (u + 1) * LANES],
                )
    column = jnp.broadcast_to(g_norm_ref[...], (8, width)).T[:, :1]
    products = head_tiles(dot(attn_ref[...].T, d_proj_ref[...]))
    for t, tile in enumerate(products):
        if t == square - 1:
            tile = with_column(tile, column)
        put(out_ref, out_place(t, tiles, square), width, tile.astype(bf16))
    used = (tiles + tiles // 2) * width
    for half in range(2):
        here = used + (square + 1 - half) // 2 * width
        left_over = out_ref.shape[1] - here
        if left_over:
            out_ref[half, here:, :] = jnp.zeros((left_over, LANES), bf16)


def ffn_grad_call(b, cot, attn, d_proj, g_norm, hid, d_gate, d_up, parts):
    rows, width = b.shape
    tiles, square = hid.shape[1] // LANES, -(-width // LANES)
    places = tiles + tiles // 2 + (square + 1) // 2
    return pl.pallas_call(
        ffn_grad_kernel,
        out_shape=[
            jax.ShapeDtypeStruct((2, half_rows(places, width, parts), LANES), bf16),
            jax.ShapeDtypeStruct((8, LANES), f32),
        ],
        compiler_params=params(48),
        name="ffn_grads",
    )(b, cot, attn, d_proj, g_norm, hid, d_gate, d_up)


def ffn_unfold_kernel(side, mine, other, gate_ref, up_ref, down_ref, out_ref, norm_ref):
    width, hidden = gate_ref.shape
    tiles, square = hidden // LANES, -(-width // LANES)

    def spread(halves):
        def tile(place):
            half, at = place
            return halves[half][at * width : (at + 1) * width, :].astype(f32)

        for t in range(tiles):
            lanes = slice(t * LANES, (t + 1) * LANES)
            gate_ref[:, lanes] = tile(ffn_place(0, t, tiles))
            up_ref[:, lanes] = tile(ffn_place(1, t, tiles))
            down_ref[:, lanes] = tile(ffn_place(2, t, tiles))
        unfold_square([tile(out_place(t, tiles, square)) for t in range(square)], out_ref, norm_ref)

    @pl.when(side[0] == 0)
    def _():
        spread((mine, other))

    @pl.when(side[0] != 0)
    def _():
        spread((other, mine))


def unfold_square(products, out_ref, norm_ref):
    for t, product in enumerate(products):
        if t < len(products) - 1:
            out_ref[:, t * LANES : (t + 1) * LANES] = product
        else:
            out_ref[:, t * LANES :] = product[:, :HEAD_DIM]
            norm_ref[...] = product.T[HEAD_DIM : HEAD_DIM + 1, :]


def unfold_call(kernel, name, side, mine, other, shapes):
    smem = pl.BlockSpec(memory_space=pltpu.SMEM)
    vmem = pl.BlockSpec(memory_space=pltpu.VMEM)
    return pl.pallas_call(
        kernel,
        in_specs=[smem, vmem, vmem],
        out_shape=[jax.ShapeDtypeStruct(shape, f32) for shape in shapes],
        compiler_params=params(48),
        name=name,
    )(side, mine, other)


def query_grad_kernel(a_ref, d_q_ref, w_ref, out_ref, g_ref):
    for t, tile in enumerate(head_tiles(dot(a_ref[...].T, d_q_ref[...]))):
        g_ref[t] = tile.astype(bf16)
    out_ref[...] = dot(d_q_ref[...], w_ref[...], NT)


def query_grad_call(a, d_q, w_query):
    rows, width = a.shape
    return pl.pallas_call(
        query_grad_kernel,
        out_shape=[
            jax.ShapeDtypeStruct((rows, width), f32),
            jax.ShapeDtypeStruct((-(-width // LANES), width, LANES), bf16),
        ],
        compiler_params=params(32),
        name="query_grads",
    )(a, d_q, w_query)


def attn_place(t):
    return t % 2, t // 2


def last_kernel(
    x_ref, a_ref, norm_ref, wk_ref, wv_ref, cos_ref, sin_ref, d_kv_ref, d_aq_ref, d_mid_ref, g_q_ref,
    out_ref, g_ref, d_pairs, d_norm,
):
    step = pl.program_id(0)
    x = x_ref[0].T.astype(f32)
    rows, width = x.shape
    low_half = lane_index(rows) < HEAD_DIM
    scale = lax.rsqrt(jnp.sum(x * x, axis=-1, keepdims=True) * (1.0 / width) + eps_norm)
    normed = x * scale
    parts = []
    for g in range(KV_HEADS):
        tile = d_kv_ref[0, :, g * LANES : (g + 1) * LANES].astype(f32)
        turned = tile * cos_ref[0] - swap_halves(tile) * sin_ref[0]
        parts.append(jnp.where(low_half, turned, tile))
    moved = [pltpu.roll(part, HEAD_DIM, 1) for part in parts]
    d_key = jnp.concatenate(
        [jnp.where(low_half, parts[0], moved[1]), parts[2][:, :HEAD_DIM]], axis=1
    ).astype(bf16)
    d_value = jnp.concatenate(
        [jnp.where(low_half, moved[0], parts[1]), moved[2][:, :HEAD_DIM]], axis=1
    ).astype(bf16)
    g_pairs = dot(a_ref[0], jnp.concatenate(parts, axis=1).astype(bf16), TN)
    d_a = d_aq_ref[0] + dot(d_key, wk_ref[...]) + dot(d_value, wv_ref[...])
    g_norm = jnp.sum(d_a * normed, axis=0, keepdims=True)

    @pl.when(step == 0)
    def _():
        d_norm[...] = g_norm
        d_pairs[...] = g_pairs

    @pl.when(step > 0)
    def _():
        d_norm[...] += g_norm
        d_pairs[...] += g_pairs

    e = d_a * norm_ref[...]
    mean = jnp.sum(e * normed, axis=-1, keepdims=True) * (1.0 / width)
    out_ref[0] = (d_mid_ref[0] + scale * (e - normed * mean)).astype(bf16).T

    @pl.when(step == pl.num_programs(0) - 1)
    def _():
        square = g_q_ref.shape[0]
        column = jnp.broadcast_to(d_norm[...], (8, width)).T[:, :1]
        for t in range(square):
            tile = g_q_ref[t]
            if t == square - 1:
                tile = with_column(tile.astype(f32), column).astype(bf16)
            put(g_ref, attn_place(t), width, tile)
        for g in range(KV_HEADS):
            put(
                g_ref,
                attn_place(square + g),
                width,
                d_pairs[:, g * LANES : (g + 1) * LANES].astype(bf16),
            )
        used = (square + KV_HEADS) // 2 * width
        left_over = g_ref.shape[1] - used
        if left_over:
            g_ref[:, used:, :] = jnp.zeros((2, left_over, LANES), bf16)


def last_call(x, a, norm, w_key, w_value, cos, sin, d_kv, d_aq, d_mid, g_query, parts):
    seqs, width, rows = x.shape
    row = lambda *shape: pl.BlockSpec((1,) + shape, lambda s: (s,) + (0,) * len(shape))
    places = (g_query.shape[0] + KV_HEADS) // 2
    g_shape = (2, half_rows(places, width, parts), LANES)
    wide = KV_HEADS * LANES
    return pl.pallas_call(
        last_kernel,
        grid=(seqs,),
        in_specs=[
            row(width, rows),
            row(rows, width),
            full_spec((1, width)),
            full_spec(w_key.shape),
            full_spec(w_value.shape),
            row(rows, LANES),
            row(rows, LANES),
            row(rows, wide),
            row(rows, width),
            row(rows, width),
            full_spec(g_query.shape),
        ],
        out_specs=[row(width, rows), full_spec(g_shape)],
        out_shape=[
            jax.ShapeDtypeStruct((seqs, width, rows), bf16),
            jax.ShapeDtypeStruct(g_shape, bf16),
        ],
        scratch_shapes=[pltpu.VMEM((width, wide), f32), pltpu.VMEM((1, width), f32)],
        compiler_params=params(32),
        name="last_part",
    )(x, a, norm, w_key, w_value, cos, sin, d_kv, d_aq, d_mid, g_query)


def attn_unfold_kernel(side, mine, other, query_ref, key_ref, value_ref, norm_ref):
    width = query_ref.shape[0]
    square = -(-width // LANES)

    def spread(halves):
        def tile(t):
            half, at = attn_place(t)
            return halves[half][at * width : (at + 1) * width, :].astype(f32)

        unfold_square([tile(t) for t in range(square)], query_ref, norm_ref)
        for g in range(KV_HEADS):
            pair = tile(square + g)
            lanes = slice(g * HEAD_DIM, (g + 1) * HEAD_DIM)
            turned = pair.T
            key_ref[lanes, :] = turned[:HEAD_DIM]
            value_ref[lanes, :] = turned[HEAD_DIM:]

    @pl.when(side[0] == 0)
    def _():
        spread((mine, other))

    @pl.when(side[0] != 0)
    def _():
        spread((other, mine))


def device_stages(seq_count, batch_count):
    masks = [1 << k for k in range(batch_count.bit_length() - 1)]
    masks += [mask * batch_count for mask in exchange_masks(seq_count)]
    return [masks[:1]] + [masks[k : k + 2] for k in range(1, len(masks), 2)]


def stage_places(stages, index):
    bits = {}
    for mask in sorted((m for stage in stages for m in stage), reverse=True):
        bit = (index >> (mask.bit_length() - 1)) & 1
        bits[mask] = bit
        index = index ^ (bit * mask)
    return [sum(bits[mask] << k for k, mask in enumerate(stage)) for stage in stages]


def swap_with(value, mask, devices):
    return lax.ppermute(value, ("seq", "batch"), [(i, i ^ mask) for i in range(devices)])


def scatter_stage(value, stage, place, devices):
    group = 1 << len(stage)
    masks = span(stage)
    value = value.reshape((group, -1, LANES))
    pick = lambda k: lax.dynamic_index_in_dim(value, place ^ k, 0, False)
    got = [swap_with(pick(k), masks[k], devices) for k in range(1, group)]
    return sum((g.astype(f32) for g in got), pick(0).astype(f32)).astype(bf16)


def gather_stage(value, stage, place, devices):
    group = 1 << len(stage)
    masks = span(stage)
    parts = jnp.stack([value] + [swap_with(value, masks[k], devices) for k in range(1, group)])
    for k in range(len(stage)):
        shape = parts.shape
        split = parts.reshape((group >> (k + 1), 2, 1 << k) + shape[1:])
        parts = jnp.where((place >> k) & 1 == 1, split[:, ::-1], split).reshape(shape)
    return parts


def gather_order(value, order, stages, places, devices):
    done = []
    for k in order:
        value = gather_stage(value, stages[k], places[k], devices)
        done.insert(0, k)
    back = sorted(range(len(done)), key=lambda i: done[i])
    return jnp.transpose(value, back + [len(done), len(done) + 1])


def gather_sums(part, stages, places, devices, chains):
    late = list(range(1, len(stages)))[::-1]
    step = part.shape[0] // chains
    got = [
        gather_order(
            part[c * step : (c + 1) * step],
            late[c % len(late) :] + late[: c % len(late)],
            stages,
            places,
            devices,
        )
        for c in range(chains)
    ]
    half = got[0] if chains == 1 else jnp.concatenate(got, axis=-2)
    half = half.reshape(-1, LANES)
    return half, swap_with(half, stages[0][0], devices)


def exchange_masks(count):
    masks = [1 << k for k in range(count.bit_length() - 1)]
    if count == 8:
        masks[2] = 6
    return masks


def chain_order(masks, chain):
    shift = chain % len(masks)
    return masks[shift:] + masks[:shift]


def span(masks):
    ids = [0]
    for mask in masks:
        ids += [k ^ mask for k in ids]
    return ids


def gather_blocks(kv, count):
    me = lax.axis_index("seq")
    masks = exchange_masks(count)
    seqs, last = kv.shape[0], len(masks) - 1
    held = [kv[s : s + 1] for s in range(seqs)]
    rounds, numbers = [], []

    def send(s, r, value, known, is_last):
        mask = chain_order(masks, s)[r]
        pairs = [
            (i, i ^ mask)
            for i in range(count)
            if not is_last or min(i ^ k for k in known) < i ^ mask
        ]
        return lax.ppermute(value, "seq", pairs), [me ^ (mask ^ k) for k in known]

    def keep(sent):
        rounds.append([value for value, _ in sent])
        numbers.append([k for _, known in sent for k in known])

    early = []
    for r in range(last):
        known = [span(chain_order(masks, s)[:r]) for s in range(seqs)]
        if r == last - 1:
            early = [send(s, last, held[s], known[s], True) for s in range(seqs)]
        sent = [send(s, r, held[s], known[s], False) for s in range(seqs)]
        keep(sent)
        if r < last - 1:
            held = [jnp.concatenate([h, v], axis=0) for h, (v, _) in zip(held, sent)]
    keep(early)
    keep(
        [
            send(
                s,
                last,
                rounds[last - 1][s],
                [chain_order(masks, s)[last - 1] ^ k for k in known[s]],
                True,
            )
            for s in range(seqs)
        ]
    )
    return rounds, numbers


def add_low(*terms):
    return sum((t.astype(f32) for t in terms[1:]), terms[0].astype(f32)).astype(bf16)


def return_round(parts, r, count):
    masks = exchange_masks(count)
    got = []
    for s, part in enumerate(parts):
        order = chain_order(masks, s)
        mask, known = order[r], span(order[:r])
        pairs = [
            (i, i ^ mask)
            for i in range(count)
            if r < len(masks) - 1 or min(i ^ mask ^ k for k in known) < i
        ]
        got.append(lax.ppermute(part, "seq", pairs))
    return got


def beside(tile):
    rows = tile.shape[0]
    half = rows // 2
    return jnp.where(
        lane_index(half) < HEAD_DIM, tile[:half], pltpu.roll(tile[half:], HEAD_DIM, 1)
    )


def stacked(tile):
    return jnp.concatenate([tile, pltpu.roll(tile, HEAD_DIM, 1)], axis=0)


def other_half(tile):
    return pltpu.roll(tile, HEAD_DIM, 1)


def join(low, high):
    return jnp.where(lane_index(low.shape[0]) < HEAD_DIM, low, high)


def low_only(tile):
    return jnp.where(lane_index(tile.shape[0]) < HEAD_DIM, tile, 0.0)


def high_only(tile):
    return jnp.where(lane_index(tile.shape[0]) < HEAD_DIM, 0.0, tile)


def write_long(ref, at, parts, last_kv):
    rows = last_kv.shape[0]
    h0, h1, h2, key, value = parts
    moved = other_half(last_kv)
    ref[at, 0:rows] = join(h0, other_half(h1)).astype(bf16)
    ref[at, rows : 2 * rows] = join(h2, other_half(key)).astype(bf16)
    ref[at, 2 * rows : 3 * rows] = join(value, moved).astype(bf16)
    ref[at, 3 * rows :] = beside(moved).astype(bf16)


def read_long(message):
    rows = message.shape[0] * 2 // 7
    first = message[0:rows].astype(f32)
    second = message[rows : 2 * rows].astype(f32)
    third = message[2 * rows : 3 * rows].astype(f32)
    value = stacked(message[3 * rows :].astype(f32))
    moved = other_half(third)
    return (
        (first, other_half(first), second),
        join(other_half(second), moved),
        join(moved, other_half(value)),
    )


def write_short(ref, at, heads):
    rows = heads[0].shape[0]
    ref[at, 0:rows] = join(heads[0], other_half(heads[1])).astype(bf16)
    ref[at, rows:] = beside(heads[2]).astype(bf16)


def read_short(message):
    rows = message.shape[0] * 2 // 3
    first = message[0:rows].astype(f32)
    return first, other_half(first), stacked(message[rows:].astype(f32))


def pair_groups(count):
    left = {i: list(range(i)) for i in range(1, count)}
    groups = []
    while any(left.values()):
        order = sorted((i for i in left if left[i]), key=lambda i: -len(left[i]))[: count // 2]
        groups.append([(i, left[i].pop(0)) for i in order])
    return groups


def units_pre_kernel(
    ids, x_ref, norm_ref, wq_ref, wk_ref, wv_ref, cos_ref, sin_ref, a_ref, out_ref, q_ref, kept
):
    step = pl.program_id(0)
    count = out_ref.shape[0]
    me = ids[0]
    x = x_ref[0].T.astype(f32)
    rows, width = x.shape
    scale = lax.rsqrt(jnp.sum(x * x, axis=-1, keepdims=True) * (1.0 / width) + eps_norm)
    a = (x * scale * norm_ref[...]).astype(bf16)
    a_ref[0] = a
    cos, sin = cos_ref[0], sin_ref[0]

    def turn(tile):
        return tile * cos + swap_halves(tile) * sin

    def heads_of(tiles, many):
        return [tiles[h // 2] if h % 2 == 0 else other_half(tiles[h // 2]) for h in range(many)]

    queries = heads_of([turn(t) * 0.125 for t in head_tiles(dot(a, wq_ref[...]))], HEADS)
    keys = heads_of([turn(t) for t in head_tiles(dot(a, wk_ref[...], NT))], KV_HEADS)
    values = heads_of(head_tiles(dot(a, wv_ref[...], NT)), KV_HEADS)
    for g in range(KV_HEADS):
        parts = queries[g * PER : (g + 1) * PER] + [keys[g], values[g]]
        unit = step * KV_HEADS + g
        first, second, third = (
            join(parts[0], other_half(parts[1])),
            join(parts[2], other_half(parts[3])),
            parts[4],
        )

        @pl.when(unit < count)
        def _(first=first, second=second, third=third, unit=unit):
            at = lax.rem(unit - me + count, count)
            out_ref[at, 0:rows] = first.astype(bf16)
            out_ref[at, rows : 2 * rows] = second.astype(bf16)
            kept[at] = third

        @pl.when(unit == count)
        def _(parts=parts):
            for h in range(PER):
                q_ref[h * rows : (h + 1) * rows] = low_only(parts[h]).astype(bf16)
            last_key = other_half(parts[3])
            last_value = beside(parts[4]).astype(bf16)
            for at in range(count):
                out_ref[at, 2 * rows : 3 * rows] = join(kept[at], last_key).astype(bf16)
                out_ref[at, 3 * rows :] = last_value


def units_pre_call(ids, x, norm, w_query, w_key, w_value, cos, sin, count):
    seqs, width, rows = x.shape
    row = lambda shape: pl.BlockSpec((1,) + shape, lambda s, *_: (s,) + (0,) * len(shape))
    long_shape = (count, rows * 7 // 2, LANES)
    q_shape = (PER * rows, LANES)
    return pl.pallas_call(
        units_pre_kernel,
        grid_spec=pltpu.PrefetchScalarGridSpec(
            num_scalar_prefetch=1,
            grid=(seqs,),
            in_specs=[
                row((width, rows)),
                full_spec((1, width)),
                full_spec(w_query.shape),
                full_spec(w_key.shape),
                full_spec(w_value.shape),
                row((rows, LANES)),
                row((rows, LANES)),
            ],
            out_specs=[row((rows, width)), full_spec(long_shape), full_spec(q_shape)],
            scratch_shapes=[pltpu.VMEM((count, rows, LANES), f32)],
        ),
        out_shape=[
            jax.ShapeDtypeStruct((seqs, rows, width), bf16),
            jax.ShapeDtypeStruct(long_shape, bf16),
            jax.ShapeDtypeStruct(q_shape, bf16),
        ],
        compiler_params=params(24),
        name="project",
    )(ids, x, norm, w_query, w_key, w_value, cos, sin)


def attend_block(q, kv, peak, total, at, diagonal):
    rows = kv.shape[0]
    ones_values = jnp.where(lane_index(rows) < HEAD_DIM, jnp.ones((), bf16), kv)
    scores = dot(kv, q, NT)
    if diagonal:
        scores = jnp.where(causal_part(rows, PER), scores, mask_low)
    new_peak = jnp.max(scores, axis=0, keepdims=True)
    if not diagonal:
        old_peak = peak[at]
        new_peak = jnp.maximum(old_peak, new_peak)
    shares = jnp.exp(scores - new_peak).astype(bf16)
    added = dot(shares.T, ones_values)
    if not diagonal:
        added = total[at] * jnp.exp(old_peak - new_peak).T + added
    total[at] = added
    peak[at] = new_peak


def attend_result(peak, total):
    rows = total.shape[0] // PER
    moved = other_half(total)
    normal = moved / total
    log_total = peak + jnp.log(total.T[0:1])
    return [normal[h * rows : (h + 1) * rows] for h in range(PER)], log_total


def units_forward_kernel(ids, *refs):
    count = len(refs) - 7
    messages = refs[:count]
    out_ref, log_ref, q_ref, kv_ref, last_kv_ref, peak, total = refs[count:]
    rows = kv_ref.shape[1]
    me = ids[0]
    for t in range(count):
        block = lax.rem(me - t + count, count)
        heads, kv, last_kv = read_long(messages[t])
        for h in range(PER):
            q_ref[block, h * rows : (h + 1) * rows] = low_only(heads[h]).astype(bf16)
        kv_ref[block] = kv.astype(bf16)
        last_kv_ref[block] = last_kv.astype(bf16)
    unroll = count // 2

    def diagonal(c, _):
        for u in range(unroll):
            i = c * unroll + u
            attend_block(q_ref[i], kv_ref[i], peak, total, i, True)
        return 0

    lax.fori_loop(0, count // unroll, diagonal, 0)

    def some(c, _):
        for u in range(unroll):
            at = 1 + 2 * (c * unroll + u)
            i, j = ids[at], ids[at + 1]
            attend_block(q_ref[i], kv_ref[j], peak, total, i, False)
        return 0

    lax.fori_loop(0, (count - 1) * count // 2 // unroll, some, 0)

    def finish(i, _):
        heads, log_total = attend_result(peak[i], total[i])
        log_ref[i] = log_total
        write_short(out_ref, lax.rem(i - me + count, count), heads)
        return 0

    lax.fori_loop(0, count, finish, 0)


def units_forward_call(ids, messages):
    count = len(messages)
    rows = messages[0].shape[0] * 2 // 7
    wide = PER * rows
    vmem = pl.BlockSpec(memory_space=pltpu.VMEM)
    return pl.pallas_call(
        units_forward_kernel,
        in_specs=[pl.BlockSpec(memory_space=pltpu.SMEM)] + [vmem] * count,
        out_shape=[
            jax.ShapeDtypeStruct((count, rows * 3 // 2, LANES), bf16),
            jax.ShapeDtypeStruct((count, 1, wide), f32),
            jax.ShapeDtypeStruct((count, wide, LANES), bf16),
            jax.ShapeDtypeStruct((count, rows, LANES), bf16),
            jax.ShapeDtypeStruct((count, rows, LANES), bf16),
        ],
        scratch_shapes=[
            pltpu.VMEM((count, 1, wide), f32),
            pltpu.VMEM((count, wide, LANES), f32),
        ],
        compiler_params=params(48),
        name="units_forward",
    )(ids, *messages)


def last_unit_forward_kernel(ids, q_ref, kv_ref, out_ref, log_ref, peak, total):
    me = ids[0]
    attend_block(q_ref[...], kv_ref[me], peak, total, 0, True)

    def one(j, _):
        attend_block(q_ref[...], kv_ref[j], peak, total, 0, False)
        return 0

    lax.fori_loop(0, me, one, 0)
    heads, log_total = attend_result(peak[0], total[0])
    log_ref[...] = log_total
    write_short(out_ref, 0, heads)


def last_unit_forward_call(ids, q, kv):
    wide = q.shape[0]
    vmem = pl.BlockSpec(memory_space=pltpu.VMEM)
    return pl.pallas_call(
        last_unit_forward_kernel,
        in_specs=[pl.BlockSpec(memory_space=pltpu.SMEM), vmem, vmem],
        out_shape=[
            jax.ShapeDtypeStruct((1, wide // 2, LANES), bf16),
            jax.ShapeDtypeStruct((1, wide), f32),
        ],
        scratch_shapes=[pltpu.VMEM((1, 1, wide), f32), pltpu.VMEM((1, wide, LANES), f32)],
        compiler_params=params(16),
        name="last_unit_forward",
    )(ids, q, kv)


def attend_back(q, d_out, kv, log_total, delta, diagonal):
    rows = kv.shape[0]
    scores = dot(kv, q, NT)
    probs = jnp.exp(scores - log_total)
    if diagonal:
        probs = jnp.where(causal_part(rows, PER), probs, 0.0)
    d_probs = dot(kv, d_out, NT)
    d_scores = (probs * (d_probs - delta)).astype(bf16)
    return (
        dot(probs.astype(bf16), d_out) + dot(d_scores, q),
        dot(d_scores.T, kv),
    )


def unpack_out(message, attn):
    heads, values = read_short(message), read_short(attn)
    delta = [
        jnp.sum(low_only(d * o).T, axis=0, keepdims=True) for d, o in zip(heads, values)
    ]
    d_out = jnp.concatenate([high_only(other_half(d)) for d in heads], axis=0)
    return d_out.astype(bf16), jnp.concatenate(delta, axis=1)


def last_unit_backward_kernel(
    ids, q_ref, kv_ref, d_ref, attn_ref, log_ref, d_kv_ref, d_q_ref, d_out
):
    me = ids[0]
    count, rows = kv_ref.shape[0], kv_ref.shape[1]
    d_value, delta = unpack_out(d_ref[...], attn_ref[...])
    d_out[...] = d_value
    d_kv, d_q = attend_back(q_ref[...], d_out[...], kv_ref[me], log_ref[...], delta, True)
    d_kv_ref[me] = d_kv.astype(bf16)
    d_q_ref[...] = d_q

    def one(j, _):
        d_kv, d_q = attend_back(q_ref[...], d_out[...], kv_ref[j], log_ref[...], delta, False)
        d_kv_ref[j] = d_kv.astype(bf16)
        d_q_ref[...] += d_q
        return 0

    lax.fori_loop(0, me, one, 0)

    def none(j, _):
        d_kv_ref[j] = jnp.zeros((rows, LANES), bf16)
        return 0

    lax.fori_loop(me + 1, count, none, 0)


def last_unit_backward_call(ids, q, kv, d_message, attn, log_total):
    vmem = pl.BlockSpec(memory_space=pltpu.VMEM)
    return pl.pallas_call(
        last_unit_backward_kernel,
        in_specs=[pl.BlockSpec(memory_space=pltpu.SMEM)] + [vmem] * 5,
        out_shape=[
            jax.ShapeDtypeStruct(kv.shape, bf16),
            jax.ShapeDtypeStruct(q.shape, f32),
        ],
        scratch_shapes=[pltpu.VMEM(q.shape, bf16)],
        compiler_params=params(24),
        name="last_unit_backward",
    )(ids, q, kv, d_message, attn, log_total)


def units_backward_kernel(ids, *refs):
    count = len(refs) - 10
    messages = refs[:count]
    q_ref, kv_ref, attn_ref, log_ref, last_ref, out_ref, d_out, delta, d_q, d_kv = refs[count:]
    rows = kv_ref.shape[1]
    me = ids[0]
    for t in range(count):
        block = lax.rem(me - t + count, count)
        value, row = unpack_out(messages[t][...], attn_ref[(count - t) % count])
        d_out[block] = value
        delta[block] = row
    unroll = count // 2

    def diagonal(c, _):
        for u in range(unroll):
            i = c * unroll + u
            d_kv[i], d_q[i] = attend_back(
                q_ref[i], d_out[i], kv_ref[i], log_ref[i], delta[i], True
            )
        return 0

    lax.fori_loop(0, count // unroll, diagonal, 0)

    def some(c, _):
        for u in range(unroll):
            at = 1 + 2 * (c * unroll + u)
            i, j = ids[at], ids[at + 1]
            kv_term, q_term = attend_back(
                q_ref[i], d_out[i], kv_ref[j], log_ref[i], delta[i], False
            )
            d_kv[j] += kv_term
            d_q[i] += q_term
        return 0

    lax.fori_loop(0, (count - 1) * count // 2 // unroll, some, 0)

    def finish(i, _):
        tile = d_kv[i]
        heads = [d_q[i, h * rows : (h + 1) * rows, :] for h in range(PER)]
        write_long(
            out_ref,
            lax.rem(i - me + count, count),
            heads + [tile, other_half(tile)],
            last_ref[i].astype(f32),
        )
        return 0

    lax.fori_loop(0, count, finish, 0)


def units_backward_call(ids, messages, q, kv, attn, log_total, last_d_kv):
    count, rows, _ = kv.shape
    wide = PER * rows
    vmem = pl.BlockSpec(memory_space=pltpu.VMEM)
    return pl.pallas_call(
        units_backward_kernel,
        in_specs=[pl.BlockSpec(memory_space=pltpu.SMEM)] + [vmem] * (count + 5),
        out_shape=jax.ShapeDtypeStruct((count, rows * 7 // 2, LANES), bf16),
        scratch_shapes=[
            pltpu.VMEM((count, wide, LANES), bf16),
            pltpu.VMEM((count, 1, wide), f32),
            pltpu.VMEM((count, wide, LANES), f32),
            pltpu.VMEM((count, rows, LANES), f32),
        ],
        compiler_params=params(56),
        name="units_backward",
    )(ids, *messages, q, kv, attn, log_total, last_d_kv)


def units_middle_kernel(
    count,
    ids,
    x_ref,
    cot_ref,
    w_out_ref,
    norm_ref,
    w_gate_ref,
    w_up_ref,
    w_down_ref,
    *refs,
):
    messages, last_message = refs[:count], refs[count]
    (
        out_ref, b_ref, hid_ref, d_gate_ref, d_up_ref, d_mid_ref, d_proj_ref, attn_ref, d_out_ref,
        d_last_ref, g_norm_ref, units,
    ) = refs[count + 1 :]
    step = pl.program_id(0)
    me = ids[0]

    @pl.when(step == 0)
    def _():
        for t in range(count):
            units[lax.rem(me - t + count, count)] = messages[t][...]
        units[count] = last_message[0]

    heads = []
    for g in range(KV_HEADS):
        heads += read_short(units[step * KV_HEADS + g])
    tiles = [join(heads[h], other_half(heads[h + 1])) for h in range(0, HEADS - 1, 2)]
    attn = jnp.concatenate(tiles + [heads[HEADS - 1][:, :HEAD_DIM]], axis=1).astype(bf16)
    attn_ref[0] = attn
    x = x_ref[0].T.astype(f32)
    width = x.shape[1]
    cot = cot_ref[0].T
    mid = x + dot(attn, w_out_ref[...])
    scale = lax.rsqrt(jnp.sum(mid * mid, axis=-1, keepdims=True) * (1.0 / width) + eps_norm)
    normed = mid * scale
    b = (normed * norm_ref[...]).astype(bf16)
    b_ref[0] = b
    gate = dot(b, w_gate_ref[...])
    up = dot(b, w_up_ref[...])
    sig = 1.0 / (1.0 + jnp.exp(-gate))
    active = gate * sig
    hid = (active * up).astype(bf16)
    hid_ref[0] = hid
    out_ref[0] = (mid + dot(hid, w_down_ref[...], NT)).astype(bf16).T
    d_hid = dot(cot, w_down_ref[...])
    d_gate = (d_hid * up * sig * (1.0 + gate * (1.0 - sig))).astype(bf16)
    d_up = (d_hid * active).astype(bf16)
    d_gate_ref[0] = d_gate
    d_up_ref[0] = d_up
    d_b = dot(d_gate, w_gate_ref[...], NT) + dot(d_up, w_up_ref[...], NT)
    g_norm = jnp.sum(d_b * normed, axis=0, keepdims=True)

    @pl.when(step == 0)
    def _():
        g_norm_ref[...] = g_norm

    @pl.when(step > 0)
    def _():
        g_norm_ref[...] += g_norm

    e = d_b * norm_ref[...]
    mean = jnp.sum(e * normed, axis=-1, keepdims=True) * (1.0 / width)
    d_mid = cot.astype(f32) + scale * (e - normed * mean)
    d_mid_ref[0] = d_mid
    d_proj = d_mid.astype(bf16)
    d_proj_ref[0] = d_proj
    d_tiles = head_tiles(dot(d_proj, w_out_ref[...], NT))
    d_heads = [
        d_tiles[h // 2] if h % 2 == 0 else other_half(d_tiles[h // 2]) for h in range(HEADS)
    ]
    for g in range(KV_HEADS):
        unit = step * KV_HEADS + g

        @pl.when(unit < count)
        def _(g=g, unit=unit):
            at = lax.rem(unit - me + count, count)
            write_short(d_out_ref, at, d_heads[g * PER : (g + 1) * PER])

        @pl.when(unit == count)
        def _(g=g):
            write_short(d_last_ref, 0, d_heads[g * PER : (g + 1) * PER])


def units_middle_call(ids, x, cot, messages, last_message, w_out, norm, w_gate, w_up, w_down):
    seqs, width, rows = x.shape
    hidden = w_gate.shape[1]
    count = len(messages)
    row = lambda *shape: pl.BlockSpec((1,) + shape, lambda s, *_: (s,) + (0,) * len(shape))
    short = (rows * 3 // 2, LANES)
    shapes = [
        ((width, rows), bf16),
        ((rows, width), bf16),
        ((rows, hidden), bf16),
        ((rows, hidden), bf16),
        ((rows, hidden), bf16),
        ((rows, width), f32),
        ((rows, width), bf16),
        ((rows, width), bf16),
    ]
    whole = [((count,) + short, bf16), ((1,) + short, bf16), ((1, width), f32)]
    return pl.pallas_call(
        functools.partial(units_middle_kernel, count),
        grid_spec=pltpu.PrefetchScalarGridSpec(
            num_scalar_prefetch=1,
            grid=(seqs,),
            in_specs=[
                row(width, rows),
                row(width, rows),
                full_spec(w_out.shape),
                full_spec((1, width)),
                full_spec(w_gate.shape),
                full_spec(w_up.shape),
                full_spec(w_down.shape),
            ]
            + [full_spec(short)] * count
            + [full_spec((1,) + short)],
            out_specs=[row(*shape) for shape, _ in shapes] + [full_spec(sh) for sh, _ in whole],
            scratch_shapes=[pltpu.VMEM((count + 1,) + short, bf16)],
        ),
        out_shape=[jax.ShapeDtypeStruct((seqs,) + shape, kind) for shape, kind in shapes]
        + [jax.ShapeDtypeStruct(shape, kind) for shape, kind in whole],
        compiler_params=params(60),
        name="feed_forward",
    )(ids, x, cot, w_out, norm, w_gate, w_up, w_down, *messages, last_message)


def units_last_kernel(
    count, ids, x_ref, a_ref, norm_ref, wq_ref, wk_ref, wv_ref, cos_ref, sin_ref, d_mid_ref, last_q_ref,
    *refs,
):
    messages = refs[:count]
    out_ref, g_ref, units, last_kv, g_query, g_pairs, d_norm = refs[count:]
    step = pl.program_id(0)
    me = ids[0]
    x = x_ref[0].T.astype(f32)
    rows, width = x.shape

    @pl.when(step == 0)
    def _():
        total = None
        for t in range(count):
            units[lax.rem(me - t + count, count)] = messages[t][0 : 3 * rows]
            third = other_half(messages[t][2 * rows : 3 * rows].astype(f32))
            value = stacked(messages[t][3 * rows :].astype(f32))
            term = join(third, other_half(value))
            total = term if total is None else total + term
        last_kv[...] = total
        units[count] = jnp.zeros_like(units[count])
        heads = [last_q_ref[h * rows : (h + 1) * rows] for h in range(PER)]
        units[count, 0:rows] = join(heads[0], other_half(heads[1])).astype(bf16)
        units[count, rows : 2 * rows] = join(heads[2], other_half(total)).astype(bf16)
        units[count, 2 * rows :] = other_half(total).astype(bf16)

    cos, sin = cos_ref[0], sin_ref[0]

    def turn(tile):
        return tile * cos - swap_halves(tile) * sin

    heads, keys, values = [], [], []
    for g in range(KV_HEADS):
        message = units[step * KV_HEADS + g].astype(f32)
        first, second, third = (message[k * rows : (k + 1) * rows] for k in range(3))
        heads += [first, other_half(first), second]
        keys.append(other_half(second))
        values.append(third)

    def in_tiles(parts, scale):
        tiles = [
            join(parts[h], other_half(parts[h + 1])) for h in range(0, len(parts) - 1, 2)
        ] + [parts[-1]]
        return tiles if scale is None else [turn(t) * scale for t in tiles]

    def flat(tiles):
        return jnp.concatenate(tiles[:-1] + [tiles[-1][:, :HEAD_DIM]], axis=1).astype(bf16)

    d_query = flat(in_tiles(heads, 0.125))
    key_tiles = in_tiles(keys, 1.0)
    d_key, d_value = flat(key_tiles), flat(in_tiles(values, None))
    turned = [key_tiles[g // 2] if g % 2 == 0 else other_half(key_tiles[g // 2]) for g in range(KV_HEADS)]
    pairs = jnp.concatenate(
        [join(turned[g], other_half(values[g])) for g in range(KV_HEADS)], axis=1
    ).astype(bf16)
    a_turned = a_ref[0].T
    query_term = dot(a_turned, d_query)
    pair_term = dot(a_turned, pairs)
    d_a = (
        dot(d_query, wq_ref[...], NT) + dot(d_key, wk_ref[...]) + dot(d_value, wv_ref[...])
    )
    scale = lax.rsqrt(jnp.sum(x * x, axis=-1, keepdims=True) * (1.0 / width) + eps_norm)
    normed = x * scale
    norm_term = jnp.sum(d_a * normed, axis=0, keepdims=True)

    @pl.when(step == 0)
    def _():
        d_norm[...] = norm_term
        g_query[...] = query_term
        g_pairs[...] = pair_term

    @pl.when(step > 0)
    def _():
        d_norm[...] += norm_term
        g_query[...] += query_term
        g_pairs[...] += pair_term

    e = d_a * norm_ref[...]
    mean = jnp.sum(e * normed, axis=-1, keepdims=True) * (1.0 / width)
    out_ref[0] = (d_mid_ref[0] + scale * (e - normed * mean)).astype(bf16).T

    @pl.when(step == pl.num_programs(0) - 1)
    def _():
        square = -(-width // LANES)
        column = jnp.broadcast_to(d_norm[...], (8, width)).T[:, :1]
        for t, tile in enumerate(head_tiles(g_query[...])):
            if t == square - 1:
                tile = with_column(tile, column)
            put(g_ref, attn_place(t), width, tile.astype(bf16))
        for g in range(KV_HEADS):
            tile = g_pairs[:, g * LANES : (g + 1) * LANES]
            put(g_ref, attn_place(square + g), width, tile.astype(bf16))
        used = (square + KV_HEADS) // 2 * width
        left_over = g_ref.shape[1] - used
        if left_over:
            g_ref[:, used:, :] = jnp.zeros((2, left_over, LANES), bf16)


def units_last_call(
    ids, x, a, norm, w_query, w_key, w_value, cos, sin, d_mid, last_d_q, messages, parts
):
    seqs, width, rows = x.shape
    count = len(messages)
    row = lambda *shape: pl.BlockSpec((1,) + shape, lambda s, *_: (s,) + (0,) * len(shape))
    places = (-(-width // LANES) + KV_HEADS) // 2
    g_shape = (2, half_rows(places, width, parts), LANES)
    return pl.pallas_call(
        functools.partial(units_last_kernel, count),
        grid_spec=pltpu.PrefetchScalarGridSpec(
            num_scalar_prefetch=1,
            grid=(seqs,),
            in_specs=[
                row(width, rows),
                row(rows, width),
                full_spec((1, width)),
                full_spec(w_query.shape),
                full_spec(w_key.shape),
                full_spec(w_value.shape),
                row(rows, LANES),
                row(rows, LANES),
                row(rows, width),
                full_spec(last_d_q.shape),
            ]
            + [full_spec(m.shape) for m in messages],
            out_specs=[row(width, rows), full_spec(g_shape)],
            scratch_shapes=[
                pltpu.VMEM((count + 1, 3 * rows, LANES), bf16),
                pltpu.VMEM((rows, LANES), f32),
                pltpu.VMEM((width, width), f32),
                pltpu.VMEM((width, KV_HEADS * LANES), f32),
                pltpu.VMEM((1, width), f32),
            ],
        ),
        out_shape=[
            jax.ShapeDtypeStruct((seqs, width, rows), bf16),
            jax.ShapeDtypeStruct(g_shape, bf16),
        ],
        compiler_params=params(40),
        name="last_part",
    )(ids, x, a, norm, w_query, w_key, w_value, cos, sin, d_mid, last_d_q, *messages)


def to_all(messages):
    count = messages.shape[0]
    return [messages[0]] + [
        lax.ppermute(messages[t], "seq", [(i, (i + t) % count) for i in range(count)])
        for t in range(1, count)
    ]


def rope_tables(positions):
    half = HEAD_DIM // 2
    lane = jnp.arange(LANES, dtype=jnp.int32)
    frequency = jnp.exp((lane % half).astype(f32) * (-math.log(10000.0) / half))
    angles = positions.T.astype(f32)[..., None] * frequency
    return jnp.cos(angles), jnp.where(lane % HEAD_DIM < half, -1.0, 1.0) * jnp.sin(angles)


def spread_layer(
    x, cot, cos, sin, norm_one, norm_two, w_query, wk_turned, wv_turned, w_out, w_gate, w_up,
    w_down_turned, count, devices, sum_over, places_ok,
):
    seqs, width, rows = x.shape
    me = lax.axis_index("seq")
    a, q, kv = pre_call(x, norm_one, w_query, wk_turned, wv_turned, cos, sin)
    rounds, numbers = gather_blocks(kv, count)
    last = len(rounds) - 2

    def ids_of(picked):
        return jnp.stack([me] + [k for part in picked for k in part]).astype(jnp.int32)

    state = forward_call(ids_of(numbers[:last]), q, kv, rounds[:last], None, False)
    far, far_ids = rounds[last:], ids_of(numbers[last:])
    attn, log_total = forward_call(far_ids, q, None, far, state, True)
    (block_out, b, hid, d_gate, d_up, d_mid, d_proj, d_out, delta, g_norm_mlp) = middle_call(
        x, cot, attn, w_out, norm_two, w_gate, w_up, w_down_turned
    )
    flat = lambda t: t.reshape(seqs * rows, t.shape[-1])
    g_ffn, done = ffn_grad_call(
        flat(b), cot, flat(attn), flat(d_proj), g_norm_mlp,
        flat(hid), flat(d_gate), flat(d_up), devices,
    )
    g_ffn = lax.psum(g_ffn, ("seq", "batch"))
    common = (q, d_out, log_total, delta)
    _, far_terms, d_query = backward_call(far_ids, *common, None, far, None, None, (done,))
    far_terms = [jnp.concatenate([t, u], axis=0) for t, u in zip(*far_terms)]
    got = [return_round(far_terms, last, count)]
    _, mid_terms, d_query = backward_call(
        ids_of(numbers[last - 1 : last]), *common, None, rounds[last - 1 : last], d_query, None
    )
    half = far_terms[0].shape[0] // 2
    mid_terms = [add_low(t, g[half:]) for t, g in zip(mid_terms[0], got[0])]
    got.append(return_round(mid_terms, last - 1, count))
    own_terms, near_terms, d_q = backward_call(
        ids_of(numbers[: last - 1]), *common, kv, rounds[: last - 1], d_query, (cos, sin),
        tuple(mid_terms),
    )
    for r in reversed(range(last - 1)):
        size = 1 << r
        terms = [
            add_low(t, *(g[s][size : 2 * size] for g in got)) for s, t in enumerate(near_terms[r])
        ]
        got.append(return_round(terms, r, count))
    d_kv = jnp.concatenate(
        [add_low(own_terms[s : s + 1], *(g[s][:1] for g in got)) for s in range(seqs)], axis=0
    )
    d_aq, g_query = query_grad_call(flat(a), flat(d_q), w_query)
    d_tokens, g_attn = last_call(
        x, a, norm_one, wk_turned, wv_turned, cos, sin, d_kv,
        d_aq.reshape(seqs, rows, width), d_mid, g_query, devices,
    )
    return block_out, d_tokens, g_ffn, sum_over(g_attn)


def units_layer(
    x, cot, cos, sin, norm_one, norm_two, w_query, wk_turned, wv_turned, w_out, w_gate, w_up,
    w_down_turned, count, devices, sum_over, places_ok,
):
    seqs, width, rows = x.shape
    flat = lambda t: t.reshape(seqs * rows, t.shape[-1])
    order = [k for group in pair_groups(count) for pair in group for k in pair]
    me = lax.axis_index("seq").astype(jnp.int32)
    ids = jnp.concatenate([me.reshape(1), jnp.array(order, jnp.int32)])
    a, messages, last_q = units_pre_call(
        ids, x, norm_one, w_query, wk_turned, wv_turned, cos, sin, count
    )
    attn_out, log_total, q, kv, last_kv = units_forward_call(ids, to_all(messages))
    last_attn, last_log = last_unit_forward_call(ids, last_q, last_kv)
    (
        block_out, b, hid, d_gate, d_up, d_mid, d_proj, attn, d_messages, d_last, g_norm_mlp,
    ) = units_middle_call(
        ids, x, cot, to_all(attn_out), last_attn, w_out, norm_two, w_gate, w_up, w_down_turned
    )
    g_ffn, _ = ffn_grad_call(
        flat(b), cot, flat(attn), flat(d_proj), g_norm_mlp,
        flat(hid), flat(d_gate), flat(d_up), devices,
    )
    g_ffn = lax.psum(g_ffn, ("seq", "batch"))

    def backward(d_messages, d_last, q, kv, attn_out, log_total, last_attn, last_log, d_mid, a):
        last_d_kv, last_d_q = last_unit_backward_call(
            ids, last_q, last_kv, d_last[0], last_attn[0], last_log
        )
        d_all = units_backward_call(
            ids, to_all(d_messages), q, kv, attn_out, log_total, last_d_kv
        )
        d_tokens, g_attn = units_last_call(
            ids, x, a, norm_one, w_query, wk_turned, wv_turned, cos, sin, d_mid, last_d_q,
            to_all(d_all), devices,
        )
        return (d_tokens,) + sum_over(g_attn)

    d_tokens, *attn_sums = in_one_piece(
        places_ok,
        backward,
        (d_messages, d_last, q, kv, attn_out, log_total, last_attn, last_log, d_mid, a),
    )
    return block_out, d_tokens, g_ffn, attn_sums


def in_one_piece(always, part, operands):
    shapes = jax.eval_shape(part, *operands)

    def never(*_):
        return jax.tree.map(lambda t: jnp.zeros(t.shape, t.dtype), shapes)

    return lax.cond(always, part, never, *operands)


def on_device(
    tokens,
    positions,
    norm_attn,
    w_query,
    w_key,
    w_value,
    w_out,
    norm_mlp,
    w_gate,
    w_up,
    w_down,
    cotangent,
):
    rows, seqs, width = tokens.shape
    hidden = w_gate.shape[1]
    kv_width = KV_HEADS * HEAD_DIM
    count, batches = lax.axis_size("seq"), lax.axis_size("batch")
    me = lax.axis_index("seq")
    devices = count * batches
    stages = device_stages(count, batches)
    places = stage_places(stages, me * batches + lax.axis_index("batch"))
    x = jnp.transpose(tokens, (1, 2, 0))
    cot = jnp.transpose(cotangent, (1, 2, 0))
    wk_turned, wv_turned, w_down_turned = w_key.T, w_value.T, w_down.T
    cos, sin = rope_tables(positions)
    norm_one, norm_two = norm_attn[None], norm_mlp[None]
    def sum_over(value):
        for stage, place in zip(stages, places):
            value = scatter_stage(value, stage, place, devices)
        return gather_sums(value, stages, places, devices, 1)

    layer = units_layer if count == seqs * KV_HEADS - 1 else spread_layer
    block_out, d_tokens, g_ffn, attn_sums = layer(
        x, cot, cos, sin, norm_one, norm_two, w_query, wk_turned, wv_turned, w_out, w_gate, w_up,
        w_down_turned, count, devices, sum_over, positions[0, 0] >= 0,
    )
    side = places[0].reshape(1).astype(jnp.int32)
    g_gate, g_up, g_down, g_out, g_norm_mlp = unfold_call(
        ffn_unfold_kernel,
        "ffn_unfold",
        jnp.zeros_like(side),
        g_ffn[0],
        g_ffn[1],
        [(width, hidden)] * 3 + [(width, width), (1, width)],
    )
    g_query, g_key, g_value, g_norm_attn = unfold_call(
        attn_unfold_kernel,
        "attn_unfold",
        side,
        *attn_sums,
        [(width, width), (kv_width, width), (kv_width, width), (1, width)],
    )
    return (
        jnp.transpose(block_out, (2, 0, 1)),
        jnp.transpose(d_tokens, (2, 0, 1)),
        g_norm_attn[0],
        g_query,
        g_key.T,
        g_value.T,
        g_out,
        g_norm_mlp[0],
        g_gate,
        g_up,
        g_down.T,
    )


def solution(mesh):
    split = P("seq", "batch", None)
    return jax.shard_map(
        on_device,
        mesh=mesh,
        in_specs=(split, P("seq", "batch")) + (P(),) * 9 + (split,),
        out_specs=(split, split) + (P(),) * 9,
        check_vma=False,
    )
```

```python
import functools
import math

import jax
import jax.numpy as jnp
from jax import lax
from jax.experimental import pallas as pl
from jax.experimental.pallas import tpu as pltpu
from jax.sharding import PartitionSpec as P

HEADS = 9
KV_HEADS = 3
HEAD_DIM = 64
PER = HEADS // KV_HEADS
LANES = 128

eps_norm = 1e-05
mask_low = -1e30
f32 = jnp.float32
bf16 = jnp.bfloat16

NN = (((1,), (0,)), ((), ()))
NT = (((1,), (1,)), ((), ()))
TN = (((0,), (0,)), ((), ()))
UNROLL = 4


def dot(left, right, dims=NN):
    return lax.dot_general(left, right, dims, preferred_element_type=f32)


def params(mib):
    return pltpu.CompilerParams(vmem_limit_bytes=mib * 1024 * 1024)


def full_spec(shape):
    zeros = (0,) * len(shape)
    return pl.BlockSpec(shape, lambda *_: zeros)


def lane_index(rows):
    return lax.broadcasted_iota(jnp.int32, (rows, LANES), 1)


def swap_halves(tile):
    half = HEAD_DIM // 2
    lane = lane_index(tile.shape[0])
    return jnp.where(
        lane % HEAD_DIM < half, pltpu.roll(tile, LANES - half, 1), pltpu.roll(tile, half, 1)
    )


def head_tiles(lin):
    rows, width = lin.shape
    if width % LANES:
        lin = jnp.concatenate([lin, jnp.zeros((rows, HEAD_DIM), lin.dtype)], axis=1)
    return [lin[:, at : at + LANES] for at in range(0, lin.shape[1], LANES)]


def pre_kernel(
    x_ref, norm_ref, wq_ref, wk_ref, wv_ref, cos_ref, sin_ref, a_ref, q_ref, kv_ref
):
    x = x_ref[0].T.astype(f32)
    rows, width = x.shape
    scale = lax.rsqrt(jnp.sum(x * x, axis=-1, keepdims=True) * (1.0 / width) + eps_norm)
    a = (x * scale * norm_ref[...]).astype(bf16)
    a_ref[0] = a
    cos, sin = cos_ref[0], sin_ref[0]
    low_half = lane_index(rows) < HEAD_DIM

    def turn(tile):
        return tile * cos + swap_halves(tile) * sin

    keys = [turn(tile) for tile in head_tiles(dot(a, wk_ref[...], NT))]
    values = head_tiles(dot(a, wv_ref[...], NT))
    for g in range(KV_HEADS):
        key, value = keys[g // 2], values[g // 2]
        if g % 2 == 0:
            value = pltpu.roll(value, HEAD_DIM, 1)
        else:
            key = pltpu.roll(key, HEAD_DIM, 1)
        kv_ref[0, :, g * LANES : (g + 1) * LANES] = jnp.where(low_half, key, value).astype(bf16)
    queries = [turn(tile) * 0.125 for tile in head_tiles(dot(a, wq_ref[...]))]
    for head in range(HEADS):
        tile = queries[head // 2]
        if head % 2:
            tile = pltpu.roll(tile, HEAD_DIM, 1)
        group, place = divmod(head, PER)
        q_ref[0, group, place * rows : (place + 1) * rows, :] = jnp.where(
            low_half, tile, 0.0
        ).astype(bf16)


def pre_call(x, norm, w_query, w_key, w_value, cos, sin):
    seqs, width, rows = x.shape
    row = lambda shape: pl.BlockSpec((1,) + shape, lambda s: (s,) + (0,) * len(shape))
    return pl.pallas_call(
        pre_kernel,
        grid=(seqs,),
        in_specs=[
            row((width, rows)),
            full_spec((1, width)),
            full_spec(w_query.shape),
            full_spec(w_key.shape),
            full_spec(w_value.shape),
            row((rows, LANES)),
            row((rows, LANES)),
        ],
        out_specs=[
            row((rows, width)),
            row((KV_HEADS, PER * rows, LANES)),
            row((rows, KV_HEADS * LANES)),
        ],
        out_shape=[
            jax.ShapeDtypeStruct((seqs, rows, width), bf16),
            jax.ShapeDtypeStruct((seqs, KV_HEADS, PER * rows, LANES), bf16),
            jax.ShapeDtypeStruct((seqs, rows, KV_HEADS * LANES), bf16),
        ],
        compiler_params=params(16),
        name="project",
    )(x, norm, w_query, w_key, w_value, cos, sin)


def causal_part(rows, heads):
    key = lax.broadcasted_iota(jnp.int32, (rows, rows), 0)
    query = lax.broadcasted_iota(jnp.int32, (rows, rows), 1)
    return jnp.concatenate([key <= query] * heads, axis=1)


def for_blocks(ids, me, seqs, own, pieces, counts, work, zeros=None):
    if own is not None:
        for s in range(seqs):
            work(s, own[s], None, (-1, s, s))
    first = 1
    for k, (parts, count) in enumerate(zip(pieces, counts)):
        least = ids[first]
        for n in range(1, seqs * count):
            least = jnp.minimum(least, ids[first + n])
        unroll = min(count, UNROLL)

        @pl.when(least < me)
        def _(parts=parts, first=first, count=count, k=k):
            def some(c, _):
                for s in range(seqs):
                    for u in range(unroll):
                        j = c * unroll + u
                        work(s, parts[s][j], ids[first + s * count + j] < me, (k, s, j))
                return 0

            if count == unroll:
                some(0, 0)
            else:
                lax.fori_loop(0, count // unroll, some, 0)

        if zeros is not None:

            @pl.when(least >= me)
            def _(k=k):
                zeros(k)

        first += seqs * count


def forward_kernel(counts, has_own, has_state, is_last, ids, *refs):
    refs = list(refs)
    q = refs.pop(0)
    seqs, rows = q.shape[0], q.shape[2] // PER
    own = refs.pop(0) if has_own else None
    pieces = [[refs.pop(0) for _ in range(seqs)] for _ in counts]
    if has_state:
        peak_in, total_in = refs.pop(0), refs.pop(0)
    outs, (peak, total) = refs[:-2], refs[-2:]
    me = ids[0]
    if has_state:
        peak[...] = peak_in[:, 0]
        total[...] = total_in[:, 0]
    low_half = lane_index(rows) < HEAD_DIM

    def attend(s, kv, seen):
        ones_values = jnp.where(low_half, jnp.ones((), bf16), kv)
        scores = dot(kv, q[s, 0], NT)
        if seen is None:
            scores = jnp.where(causal_part(rows, PER), scores, mask_low)
            new_peak = shift = jnp.max(scores, axis=0, keepdims=True)
        else:
            old_peak = peak[s]
            top = jnp.max(scores, axis=0, keepdims=True)
            new_peak = jnp.where(seen, jnp.maximum(old_peak, top), old_peak)
            shift = jnp.where(seen, new_peak, -mask_low)
        shares = jnp.exp(scores - shift).astype(bf16)
        added = dot(shares.T, ones_values)
        if seen is None:
            total[s] = added
        else:
            total[s] = total[s] * jnp.exp(old_peak - new_peak).T + added
        peak[s] = new_peak

    for_blocks(ids, me, seqs, own, pieces, counts, lambda s, kv, seen, store: attend(s, kv, seen))
    if is_last:
        attn, log_total = outs
        group = pl.program_id(0)
        for s in range(seqs):
            acc = total[s]
            normal = acc / pltpu.roll(acc, HEAD_DIM, 1)
            sums = acc.T[0:1]
            log_total[s, 0] = peak[s] + jnp.log(sums)
            values = normal[:, HEAD_DIM:].astype(bf16)
            for g in range(KV_HEADS):

                @pl.when(group == g)
                def _(values=values, s=s, g=g):
                    for h in range(PER):
                        at = (g * PER + h) * HEAD_DIM
                        attn[s, :, at : at + HEAD_DIM] = values[h * rows : (h + 1) * rows]

    else:
        outs[0][:, 0] = peak[...]
        outs[1][:, 0] = total[...]


def piece_spec(count, rows):
    return pl.BlockSpec((count, rows, LANES), lambda g, *_: (0, 0, g))


def group_spec(seqs, *shape):
    zeros = (0,) * len(shape)
    return pl.BlockSpec((seqs, 1) + shape, lambda g, *_: (0, g) + zeros)


def forward_call(ids, q, own, pieces, state, is_last):
    seqs, groups, wide, _ = q.shape
    rows = wide // PER
    counts = [parts[0].shape[0] for parts in pieces]
    arrays, specs = [q], [group_spec(seqs, wide, LANES)]
    if own is not None:
        arrays.append(own)
        specs.append(piece_spec(seqs, rows))
    for parts, count in zip(pieces, counts):
        arrays += parts
        specs += [piece_spec(count, rows)] * seqs
    row_spec, row_shape = group_spec(seqs, 1, wide), (seqs, groups, 1, wide)
    sum_spec, sum_shape = group_spec(seqs, wide, LANES), (seqs, groups, wide, LANES)
    if state is not None:
        arrays += list(state)
        specs += [row_spec, sum_spec]
    if is_last:
        attn_shape = (seqs, rows, HEADS * HEAD_DIM)
        out_shape = [
            jax.ShapeDtypeStruct(attn_shape, bf16),
            jax.ShapeDtypeStruct(row_shape, f32),
        ]
        out_specs = [full_spec(attn_shape), row_spec]
    else:
        out_shape = [
            jax.ShapeDtypeStruct(row_shape, f32),
            jax.ShapeDtypeStruct(sum_shape, f32),
        ]
        out_specs = [row_spec, sum_spec]
    return pl.pallas_call(
        functools.partial(
            forward_kernel, counts, own is not None, state is not None, is_last
        ),
        out_shape=out_shape,
        grid_spec=pltpu.PrefetchScalarGridSpec(
            num_scalar_prefetch=1,
            grid=(groups,),
            in_specs=specs,
            out_specs=out_specs,
            scratch_shapes=[
                pltpu.VMEM((seqs, 1, wide), f32),
                pltpu.VMEM((seqs, wide, LANES), f32),
            ],
        ),
        compiler_params=params(60),
        name="attend_forward",
    )(ids, *arrays)


def backward_kernel(counts, has_own, has_state, is_last, waits, ids, *refs):
    refs = list(refs)[waits:]
    q, d_out, log_total, delta = refs[:4]
    refs = refs[4:]
    seqs, rows = q.shape[0], q.shape[2] // PER
    own = refs.pop(0) if has_own else None
    pieces = [[refs.pop(0) for _ in range(seqs)] for _ in counts]
    d_query_in = refs.pop(0) if has_state else None
    cos, sin = (refs.pop(0), refs.pop(0)) if is_last else (None, None)
    d_own = refs.pop(0) if has_own else None
    d_pieces = [[refs.pop(0) for _ in range(seqs)] for _ in counts]
    d_query_out, d_query = refs
    me = ids[0]
    if has_state:
        d_query[...] = d_query_in[:, 0]
    else:
        d_query[...] = jnp.zeros_like(d_query)

    def back(s, kv, seen, place):
        q_all, d_all = q[s, 0], d_out[s, 0]
        scores = dot(kv, q_all, NT)
        if seen is None:
            probs = jnp.exp(scores - log_total[s, 0])
            probs = jnp.where(causal_part(rows, PER), probs, 0.0)
        else:
            probs = jnp.exp(scores - jnp.where(seen, log_total[s, 0], -mask_low))
        d_probs = dot(kv, d_all, NT)
        d_scores = (probs * (d_probs - delta[s, 0])).astype(bf16)
        d_query[s] += dot(d_scores.T, kv)
        terms = (dot(probs.astype(bf16), d_all) + dot(d_scores, q_all)).astype(bf16)
        piece, s, j = place
        if piece < 0:
            d_own[s] = terms
        else:
            d_pieces[piece][s][j] = terms

    def zeros(piece):
        for s in range(seqs):
            d_pieces[piece][s][...] = jnp.zeros(d_pieces[piece][s].shape, bf16)

    for_blocks(ids, me, seqs, own, pieces, counts, back, zeros)
    if is_last:
        group = pl.program_id(0)
        for s in range(seqs):
            turned = []
            for h in range(PER):
                tile = d_query[s, h * rows : (h + 1) * rows, :] * 0.125
                turned.append(
                    (tile * cos[s] - swap_halves(tile) * sin[s])[:, :HEAD_DIM].astype(bf16)
                )
            for g in range(KV_HEADS):

                @pl.when(group == g)
                def _(turned=turned, s=s, g=g):
                    for h in range(PER):
                        at = (g * PER + h) * HEAD_DIM
                        d_query_out[s, :, at : at + HEAD_DIM] = turned[h]

    else:
        d_query_out[:, 0] = d_query[...]


def backward_call(ids, q, d_out, log_total, delta, own, pieces, d_query, tables, after=()):
    seqs, groups, wide, _ = q.shape
    rows = wide // PER
    counts = [parts[0].shape[0] for parts in pieces]
    sum_spec, sum_shape = group_spec(seqs, wide, LANES), (seqs, groups, wide, LANES)
    row_spec = group_spec(seqs, 1, wide)
    arrays = [q, d_out, log_total, delta]
    specs = [sum_spec, sum_spec, row_spec, row_spec]
    out_shape, out_specs = [], []
    if own is not None:
        arrays.append(own)
        specs.append(piece_spec(seqs, rows))
        out_shape.append(jax.ShapeDtypeStruct(own.shape, bf16))
        out_specs.append(piece_spec(seqs, rows))
    for parts, count in zip(pieces, counts):
        arrays += parts
        specs += [piece_spec(count, rows)] * seqs
        out_shape += [jax.ShapeDtypeStruct(parts[0].shape, bf16)] * seqs
        out_specs += [piece_spec(count, rows)] * seqs
    if d_query is not None:
        arrays.append(d_query)
        specs.append(sum_spec)
    is_last = tables is not None
    if is_last:
        arrays += list(tables)
        specs += [full_spec((seqs, rows, LANES))] * 2
        shape = (seqs, rows, HEADS * HEAD_DIM)
        out_shape.append(jax.ShapeDtypeStruct(shape, bf16))
        out_specs.append(full_spec(shape))
    else:
        out_shape.append(jax.ShapeDtypeStruct(sum_shape, f32))
        out_specs.append(sum_spec)
    arrays = list(after) + arrays
    specs = [pl.BlockSpec(memory_space=pl.ANY)] * len(after) + specs
    outs = pl.pallas_call(
        functools.partial(
            backward_kernel, counts, own is not None, d_query is not None, is_last, len(after)
        ),
        out_shape=out_shape,
        grid_spec=pltpu.PrefetchScalarGridSpec(
            num_scalar_prefetch=1,
            grid=(groups,),
            in_specs=specs,
            out_specs=out_specs,
            scratch_shapes=[pltpu.VMEM((seqs, wide, LANES), f32)],
        ),
        compiler_params=params(60),
        name="attend_backward",
    )(ids, *arrays)
    d_own = None
    if own is not None:
        d_own, outs = outs[0], outs[1:]
    d_pieces = [list(outs[k * seqs : (k + 1) * seqs]) for k in range(len(counts))]
    return d_own, d_pieces, outs[-1]


def middle_kernel(
    x_ref,
    cot_ref,
    attn_ref,
    w_out_ref,
    norm_ref,
    w_gate_ref,
    w_up_ref,
    w_down_ref,
    out_ref,
    b_ref,
    hid_ref,
    d_gate_ref,
    d_up_ref,
    d_mid_ref,
    d_proj_ref,
    d_out_ref,
    delta_ref,
    g_norm_ref,
):
    x = x_ref[0].T.astype(f32)
    rows, width = x.shape
    cot = cot_ref[0].T
    attn = attn_ref[0]
    mid = x + dot(attn, w_out_ref[...])
    scale = lax.rsqrt(jnp.sum(mid * mid, axis=-1, keepdims=True) * (1.0 / width) + eps_norm)
    normed = mid * scale
    b = (normed * norm_ref[...]).astype(bf16)
    b_ref[0] = b
    gate = dot(b, w_gate_ref[...])
    up = dot(b, w_up_ref[...])
    sig = 1.0 / (1.0 + jnp.exp(-gate))
    active = gate * sig
    hid = (active * up).astype(bf16)
    hid_ref[0] = hid
    out_ref[0] = (mid + dot(hid, w_down_ref[...], NT)).astype(bf16).T
    d_hid = dot(cot, w_down_ref[...])
    d_gate = (d_hid * up * sig * (1.0 + gate * (1.0 - sig))).astype(bf16)
    d_up = (d_hid * active).astype(bf16)
    d_gate_ref[0] = d_gate
    d_up_ref[0] = d_up
    d_b = dot(d_gate, w_gate_ref[...], NT) + dot(d_up, w_up_ref[...], NT)
    g_norm = jnp.sum(d_b * normed, axis=0, keepdims=True)

    @pl.when(pl.program_id(0) == 0)
    def _():
        g_norm_ref[...] = g_norm

    @pl.when(pl.program_id(0) > 0)
    def _():
        g_norm_ref[...] += g_norm

    e = d_b * norm_ref[...]
    mean = jnp.sum(e * normed, axis=-1, keepdims=True) * (1.0 / width)
    d_mid = cot.astype(f32) + scale * (e - normed * mean)
    d_mid_ref[0] = d_mid
    d_proj = d_mid.astype(bf16)
    d_proj_ref[0] = d_proj
    d_attn = dot(d_proj, w_out_ref[...], NT).astype(bf16).astype(f32)
    both = d_attn * attn.astype(f32)
    high = both.astype(bf16)
    rest = (both - high.astype(f32)).astype(bf16)
    head = lax.broadcasted_iota(jnp.int32, (16, width), 0)
    feature = lax.broadcasted_iota(jnp.int32, (16, width), 1)
    picks = jnp.where(
        (feature >= head * HEAD_DIM) & (feature < (head + 1) * HEAD_DIM), 1.0, 0.0
    ).astype(bf16)
    sums = dot(picks, high, NT) + dot(picks, rest, NT)
    high_half = lane_index(rows) >= HEAD_DIM
    padded = jnp.concatenate([d_attn, jnp.zeros((rows, HEAD_DIM), f32)], axis=1)
    for k in range(HEADS):
        at = k // 2 * LANES
        tile = padded[:, at : at + LANES]
        if k % 2 == 0:
            tile = pltpu.roll(tile, HEAD_DIM, 1)
        group, place = divmod(k, PER)
        here = slice(place * rows, (place + 1) * rows)
        d_out_ref[0, group, here, :] = jnp.where(high_half, tile, 0.0).astype(bf16)
        delta_ref[0, group, 0:1, here] = sums[k : k + 1]


def middle_call(x, cot, attn, w_out, norm, w_gate, w_up, w_down):
    seqs, width, rows = x.shape
    hidden = w_gate.shape[1]
    row = lambda *shape: pl.BlockSpec((1,) + shape, lambda s: (s,) + (0,) * len(shape))
    wide = PER * rows
    shapes = [
        ((width, rows), bf16),
        ((rows, width), bf16),
        ((rows, hidden), bf16),
        ((rows, hidden), bf16),
        ((rows, hidden), bf16),
        ((rows, width), f32),
        ((rows, width), bf16),
        ((KV_HEADS, wide, LANES), bf16),
        ((KV_HEADS, 1, wide), f32),
    ]
    return pl.pallas_call(
        middle_kernel,
        grid=(seqs,),
        in_specs=[row(width, rows), row(width, rows), row(rows, width)]
        + [
            full_spec(w_out.shape),
            full_spec((1, width)),
            full_spec(w_gate.shape),
            full_spec(w_up.shape),
            full_spec(w_down.shape),
        ],
        out_specs=[row(*shape) for shape, _ in shapes] + [full_spec((1, width))],
        out_shape=[jax.ShapeDtypeStruct((seqs,) + shape, kind) for shape, kind in shapes]
        + [jax.ShapeDtypeStruct((1, width), f32)],
        compiler_params=params(60),
        name="feed_forward",
    )(x, cot, attn, w_out, norm, w_gate, w_up, w_down)


def ffn_place(k, t, tiles):
    if k < 2:
        return k, t
    return (0, tiles + t) if t < tiles // 2 else (1, tiles + t - tiles // 2)


def half_rows(places, width, parts):
    unit = 16 * (parts // 2)
    return -(-places * width // unit) * unit


def put(out_ref, place, width, tile):
    half, at = place
    out_ref[half, at * width : (at + 1) * width, :] = tile


def with_column(tile, column):
    free = lane_index(tile.shape[0]) >= HEAD_DIM
    return jnp.where(free, column, tile)


def ffn_grad_kernel(b_ref, cot_ref, hid_ref, d_gate_ref, d_up_ref, out_ref):
    width = b_ref.shape[1]
    hidden = hid_ref.shape[1]
    tiles = hidden // LANES
    chunk = 2 * LANES
    b_turned = b_ref[...].T
    cot_turned = jnp.concatenate([cot_ref[s] for s in range(cot_ref.shape[0])], axis=1)
    for k, (left, right) in enumerate(
        ((b_turned, d_gate_ref), (b_turned, d_up_ref), (cot_turned, hid_ref))
    ):
        for c in range(hidden // chunk):
            product = dot(left, right[:, c * chunk : (c + 1) * chunk]).astype(bf16)
            for u in range(2):
                put(
                    out_ref,
                    ffn_place(k, 2 * c + u, tiles),
                    width,
                    product[:, u * LANES : (u + 1) * LANES],
                )


def ffn_grad_call(b, cot, hid, d_gate, d_up):
    width = b.shape[1]
    tiles = hid.shape[1] // LANES
    return pl.pallas_call(
        ffn_grad_kernel,
        out_shape=jax.ShapeDtypeStruct((2, (tiles + tiles // 2) * width, LANES), bf16),
        compiler_params=params(60),
        name="ffn_grads",
    )(b, cot, hid, d_gate, d_up)


def ffn_unfold_kernel(gate_in, up_in, down_in, gate_ref, up_ref, down_ref):
    for source, target in ((gate_in, gate_ref), (up_in, up_ref), (down_in, down_ref)):
        for u in range(source.shape[1]):
            target[:, u * LANES : (u + 1) * LANES] = source[0, u].astype(f32)


def ffn_unfold_call(sums, width, hidden):
    tiles = hidden // LANES
    chunk = 2
    steps = tiles // chunk
    sums = sums.reshape(2, tiles + tiles // 2, width, LANES)
    block = (1, chunk, width, LANES)
    return pl.pallas_call(
        ffn_unfold_kernel,
        grid=(steps,),
        in_specs=[
            pl.BlockSpec(block, lambda i: (0, i, 0, 0)),
            pl.BlockSpec(block, lambda i: (1, i, 0, 0)),
            pl.BlockSpec(block, lambda i: (i // (steps // 2), steps + i % (steps // 2), 0, 0)),
        ],
        out_specs=[pl.BlockSpec((width, chunk * LANES), lambda i: (0, i))] * 3,
        out_shape=[jax.ShapeDtypeStruct((width, hidden), f32)] * 3,
        compiler_params=params(60),
        name="ffn_unfold",
    )(sums, sums, sums)


def unfold_square(products, out_ref, norm_ref):
    for t, product in enumerate(products):
        if t < len(products) - 1:
            out_ref[:, t * LANES : (t + 1) * LANES] = product
        else:
            out_ref[:, t * LANES :] = product[:, :HEAD_DIM]
            norm_ref[...] = product.T[HEAD_DIM : HEAD_DIM + 1, :]


def unfold_call(kernel, name, arrays, shapes):
    smem = pl.BlockSpec(memory_space=pltpu.SMEM)
    vmem = pl.BlockSpec(memory_space=pltpu.VMEM)
    return pl.pallas_call(
        kernel,
        in_specs=[smem if t.ndim == 1 else vmem for t in arrays],
        out_shape=[jax.ShapeDtypeStruct(shape, f32) for shape in shapes],
        compiler_params=params(48),
        name=name,
    )(*arrays)


def query_grad_kernel(
    a_ref, attn_ref, d_proj_ref, d_q_ref, g_norm_ref, w_ref, out_ref, g_ref, g_out_ref
):
    for t, tile in enumerate(head_tiles(dot(a_ref[...].T, d_q_ref[...]))):
        g_ref[t] = tile.astype(bf16)
    width = a_ref.shape[1]
    column = jnp.broadcast_to(g_norm_ref[...], (8, width)).T[:, :1]
    for t, tile in enumerate(head_tiles(dot(attn_ref[...].T, d_proj_ref[...]))):
        if t == g_out_ref.shape[0] - 1:
            tile = with_column(tile, column)
        g_out_ref[t] = tile.astype(bf16)
    out_ref[...] = dot(d_q_ref[...], w_ref[...], NT)


def query_grad_call(a, attn, d_proj, d_q, g_norm, w_query):
    rows, width = a.shape
    tiles = jax.ShapeDtypeStruct((-(-width // LANES), width, LANES), bf16)
    return pl.pallas_call(
        query_grad_kernel,
        out_shape=[jax.ShapeDtypeStruct((rows, width), f32), tiles, tiles],
        compiler_params=params(32),
        name="query_grads",
    )(a, attn, d_proj, d_q, g_norm, w_query)


def attn_place(t):
    return t % 2, t // 2


def last_kernel(
    x_ref, a_ref, norm_ref, wk_ref, wv_ref, cos_ref, sin_ref, d_kv_ref, d_aq_ref, d_mid_ref, g_q_ref,
    g_out_ref, out_ref, g_ref, d_pairs, d_norm,
):
    step = pl.program_id(0)
    x = x_ref[0].T.astype(f32)
    rows, width = x.shape
    low_half = lane_index(rows) < HEAD_DIM
    scale = lax.rsqrt(jnp.sum(x * x, axis=-1, keepdims=True) * (1.0 / width) + eps_norm)
    normed = x * scale
    parts = []
    for g in range(KV_HEADS):
        tile = d_kv_ref[0, :, g * LANES : (g + 1) * LANES].astype(f32)
        turned = tile * cos_ref[0] - swap_halves(tile) * sin_ref[0]
        parts.append(jnp.where(low_half, turned, tile))
    moved = [pltpu.roll(part, HEAD_DIM, 1) for part in parts]
    d_key = jnp.concatenate(
        [jnp.where(low_half, parts[0], moved[1]), parts[2][:, :HEAD_DIM]], axis=1
    ).astype(bf16)
    d_value = jnp.concatenate(
        [jnp.where(low_half, moved[0], parts[1]), moved[2][:, :HEAD_DIM]], axis=1
    ).astype(bf16)
    g_pairs = dot(a_ref[0], jnp.concatenate(parts, axis=1).astype(bf16), TN)
    d_a = d_aq_ref[0] + dot(d_key, wk_ref[...]) + dot(d_value, wv_ref[...])
    g_norm = jnp.sum(d_a * normed, axis=0, keepdims=True)

    @pl.when(step == 0)
    def _():
        d_norm[...] = g_norm
        d_pairs[...] = g_pairs

    @pl.when(step > 0)
    def _():
        d_norm[...] += g_norm
        d_pairs[...] += g_pairs

    e = d_a * norm_ref[...]
    mean = jnp.sum(e * normed, axis=-1, keepdims=True) * (1.0 / width)
    out_ref[0] = (d_mid_ref[0] + scale * (e - normed * mean)).astype(bf16).T

    @pl.when(step == pl.num_programs(0) - 1)
    def _():
        square = g_q_ref.shape[0]
        column = jnp.broadcast_to(d_norm[...], (8, width)).T[:, :1]
        for t in range(square):
            tile = g_q_ref[t]
            if t == square - 1:
                tile = with_column(tile.astype(f32), column).astype(bf16)
            put(g_ref, attn_place(t), width, tile)
        for g in range(KV_HEADS):
            put(
                g_ref,
                attn_place(square + g),
                width,
                d_pairs[:, g * LANES : (g + 1) * LANES].astype(bf16),
            )
        for t in range(square):
            put(g_ref, attn_place(square + KV_HEADS + t), width, g_out_ref[t])
        clear_rest(g_ref, 2 * square + KV_HEADS, width)


def last_call(x, a, norm, w_key, w_value, cos, sin, d_kv, d_aq, d_mid, g_query, g_out, parts):
    seqs, width, rows = x.shape
    row = lambda *shape: pl.BlockSpec((1,) + shape, lambda s: (s,) + (0,) * len(shape))
    places = -(-(2 * g_query.shape[0] + KV_HEADS) // 2)
    g_shape = (2, half_rows(places, width, parts), LANES)
    wide = KV_HEADS * LANES
    return pl.pallas_call(
        last_kernel,
        grid=(seqs,),
        in_specs=[
            row(width, rows),
            row(rows, width),
            full_spec((1, width)),
            full_spec(w_key.shape),
            full_spec(w_value.shape),
            row(rows, LANES),
            row(rows, LANES),
            row(rows, wide),
            row(rows, width),
            row(rows, width),
            full_spec(g_query.shape),
            full_spec(g_out.shape),
        ],
        out_specs=[row(width, rows), full_spec(g_shape)],
        out_shape=[
            jax.ShapeDtypeStruct((seqs, width, rows), bf16),
            jax.ShapeDtypeStruct(g_shape, bf16),
        ],
        scratch_shapes=[pltpu.VMEM((width, wide), f32), pltpu.VMEM((1, width), f32)],
        compiler_params=params(32),
        name="last_part",
    )(x, a, norm, w_key, w_value, cos, sin, d_kv, d_aq, d_mid, g_query, g_out)


def attn_unfold_kernel(
    side, mine, other, query_ref, key_ref, value_ref, norm_ref, out_ref, norm_two_ref
):
    width = query_ref.shape[0]
    square = -(-width // LANES)

    def spread(halves):
        def tile(t):
            half, at = attn_place(t)
            return halves[half][at * width : (at + 1) * width, :].astype(f32)

        unfold_square([tile(t) for t in range(square)], query_ref, norm_ref)
        for g in range(KV_HEADS):
            pair = tile(square + g)
            lanes = slice(g * HEAD_DIM, (g + 1) * HEAD_DIM)
            turned = pair.T
            key_ref[lanes, :] = turned[:HEAD_DIM]
            value_ref[lanes, :] = turned[HEAD_DIM:]
        first = square + KV_HEADS
        unfold_square([tile(first + t) for t in range(square)], out_ref, norm_two_ref)

    @pl.when(side[0] == 0)
    def _():
        spread((mine, other))

    @pl.when(side[0] != 0)
    def _():
        spread((other, mine))


def device_stages(seq_count, batch_count):
    masks = [1 << k for k in range(batch_count.bit_length() - 1)]
    masks += [mask * batch_count for mask in exchange_masks(seq_count)]
    return [masks[:1]] + [masks[k : k + 2] for k in range(1, len(masks), 2)]


def stage_places(stages, index):
    bits = {}
    for mask in sorted((m for stage in stages for m in stage), reverse=True):
        bit = (index >> (mask.bit_length() - 1)) & 1
        bits[mask] = bit
        index = index ^ (bit * mask)
    return [sum(bits[mask] << k for k, mask in enumerate(stage)) for stage in stages]


def swap_with(value, mask, devices):
    return lax.ppermute(value, ("seq", "batch"), [(i, i ^ mask) for i in range(devices)])


def scatter_stage(value, stage, place, devices):
    group = 1 << len(stage)
    masks = span(stage)
    value = value.reshape((group, -1, LANES))
    pick = lambda k: lax.dynamic_index_in_dim(value, place ^ k, 0, False)
    got = [swap_with(pick(k), masks[k], devices) for k in range(1, group)]
    return sum((g.astype(f32) for g in got), pick(0).astype(f32)).astype(bf16)


def gather_stage(value, stage, place, devices):
    group = 1 << len(stage)
    masks = span(stage)
    parts = jnp.stack([value] + [swap_with(value, masks[k], devices) for k in range(1, group)])
    for k in range(len(stage)):
        shape = parts.shape
        split = parts.reshape((group >> (k + 1), 2, 1 << k) + shape[1:])
        parts = jnp.where((place >> k) & 1 == 1, split[:, ::-1], split).reshape(shape)
    return parts


def gather_order(value, order, stages, places, devices):
    done = []
    for k in order:
        value = gather_stage(value, stages[k], places[k], devices)
        done.insert(0, k)
    back = sorted(range(len(done)), key=lambda i: done[i])
    return jnp.transpose(value, back + [len(done), len(done) + 1])


def gather_sums(part, stages, places, devices, chains):
    late = list(range(1, len(stages)))[::-1]
    step = part.shape[0] // chains
    got = [
        gather_order(
            part[c * step : (c + 1) * step],
            late[c % len(late) :] + late[: c % len(late)],
            stages,
            places,
            devices,
        )
        for c in range(chains)
    ]
    half = got[0] if chains == 1 else jnp.concatenate(got, axis=-2)
    half = half.reshape(-1, LANES)
    return half, swap_with(half, stages[0][0], devices)


def exchange_masks(count):
    masks = [1 << k for k in range(count.bit_length() - 1)]
    if count == 8:
        masks[2] = 6
    return masks


def chain_order(masks, chain):
    shift = chain % len(masks)
    return masks[shift:] + masks[:shift]


def span(masks):
    ids = [0]
    for mask in masks:
        ids += [k ^ mask for k in ids]
    return ids


def gather_blocks(kv, count):
    me = lax.axis_index("seq")
    masks = exchange_masks(count)
    seqs, last = kv.shape[0], len(masks) - 1
    held = [kv[s : s + 1] for s in range(seqs)]
    rounds, numbers = [], []

    def send(s, r, value, known, is_last):
        mask = chain_order(masks, s)[r]
        pairs = [
            (i, i ^ mask)
            for i in range(count)
            if not is_last or min(i ^ k for k in known) < i ^ mask
        ]
        return lax.ppermute(value, "seq", pairs), [me ^ (mask ^ k) for k in known]

    def keep(sent):
        rounds.append([value for value, _ in sent])
        numbers.append([k for _, known in sent for k in known])

    early = []
    for r in range(last):
        known = [span(chain_order(masks, s)[:r]) for s in range(seqs)]
        if r == last - 1:
            early = [send(s, last, held[s], known[s], True) for s in range(seqs)]
        sent = [send(s, r, held[s], known[s], False) for s in range(seqs)]
        keep(sent)
        if r < last - 1:
            held = [jnp.concatenate([h, v], axis=0) for h, (v, _) in zip(held, sent)]
    keep(early)
    keep(
        [
            send(
                s,
                last,
                rounds[last - 1][s],
                [chain_order(masks, s)[last - 1] ^ k for k in known[s]],
                True,
            )
            for s in range(seqs)
        ]
    )
    return rounds, numbers


def add_low(*terms):
    return sum((t.astype(f32) for t in terms[1:]), terms[0].astype(f32)).astype(bf16)


def return_round(parts, r, count):
    masks = exchange_masks(count)
    got = []
    for s, part in enumerate(parts):
        order = chain_order(masks, s)
        mask, known = order[r], span(order[:r])
        pairs = [
            (i, i ^ mask)
            for i in range(count)
            if r < len(masks) - 1 or min(i ^ mask ^ k for k in known) < i
        ]
        got.append(lax.ppermute(part, "seq", pairs))
    return got


def beside(tile):
    rows = tile.shape[0]
    half = rows // 2
    return jnp.where(
        lane_index(half) < HEAD_DIM, tile[:half], pltpu.roll(tile[half:], HEAD_DIM, 1)
    )


def stacked(tile):
    return jnp.concatenate([tile, pltpu.roll(tile, HEAD_DIM, 1)], axis=0)


def other_half(tile):
    return pltpu.roll(tile, HEAD_DIM, 1)


def join(low, high):
    return jnp.where(lane_index(low.shape[0]) < HEAD_DIM, low, high)


def low_only(tile):
    return jnp.where(lane_index(tile.shape[0]) < HEAD_DIM, tile, 0.0)


def high_only(tile):
    return jnp.where(lane_index(tile.shape[0]) < HEAD_DIM, 0.0, tile)


def write_long(ref, at, parts, more=None):
    h0, h1, h2, key, value = parts
    rows = key.shape[0]
    ref[at, 0:rows] = join(h0, other_half(h1)).astype(bf16)
    ref[at, rows : 2 * rows] = join(h2, other_half(key)).astype(bf16)
    ref[at, 2 * rows : rows * 5 // 2] = beside(value).astype(bf16)
    if more is not None:
        ref[at, rows * 5 // 2 :] = more


def read_long(message, rows):
    first = message[0:rows].astype(f32)
    second = message[rows : 2 * rows].astype(f32)
    value = stacked(message[2 * rows : rows * 5 // 2].astype(f32))
    return (first, other_half(first), second), join(other_half(second), other_half(value))


def write_short(ref, at, heads):
    rows = heads[0].shape[0]
    ref[at, 0:rows] = join(heads[0], other_half(heads[1])).astype(bf16)
    ref[at, rows:] = beside(heads[2]).astype(bf16)


def read_short(message):
    rows = message.shape[0] * 2 // 3
    first = message[0:rows].astype(f32)
    return first, other_half(first), stacked(message[rows:].astype(f32))


def units_pre_kernel(
    ids, x_ref, norm_ref, wq_ref, wk_ref, wv_ref, cos_ref, sin_ref, a_ref, out_ref, q_ref, kv_ref
):
    step = pl.program_id(0)
    count = out_ref.shape[0]
    me = ids[0]
    x = x_ref[0].T.astype(f32)
    rows, width = x.shape
    scale = lax.rsqrt(jnp.sum(x * x, axis=-1, keepdims=True) * (1.0 / width) + eps_norm)
    a = (x * scale * norm_ref[...]).astype(bf16)
    a_ref[0] = a
    cos, sin = cos_ref[0], sin_ref[0]

    def turn(tile):
        return tile * cos + swap_halves(tile) * sin

    def heads_of(tiles, many):
        return [tiles[h // 2] if h % 2 == 0 else other_half(tiles[h // 2]) for h in range(many)]

    queries = heads_of([turn(t) * 0.125 for t in head_tiles(dot(a, wq_ref[...]))], HEADS)
    keys = heads_of([turn(t) for t in head_tiles(dot(a, wk_ref[...], NT))], KV_HEADS)
    values = heads_of(head_tiles(dot(a, wv_ref[...], NT)), KV_HEADS)
    for g in range(KV_HEADS):
        parts = queries[g * PER : (g + 1) * PER] + [keys[g], values[g]]
        unit = step * KV_HEADS + g

        @pl.when(unit < count)
        def _(parts=parts, unit=unit):
            write_long(out_ref, lax.rem(unit - me + count, count), parts)

        @pl.when(unit == count)
        def _(parts=parts):
            for h in range(PER):
                q_ref[h * rows : (h + 1) * rows] = low_only(parts[h]).astype(bf16)
            kv_ref[0] = join(parts[3], other_half(parts[4])).astype(bf16)


def units_pre_call(ids, x, norm, w_query, w_key, w_value, cos, sin, count):
    seqs, width, rows = x.shape
    row = lambda shape: pl.BlockSpec((1,) + shape, lambda s, *_: (s,) + (0,) * len(shape))
    long_shape = (count, rows * 5 // 2, LANES)
    q_shape = (PER * rows, LANES)
    kv_shape = (1, rows, LANES)
    return pl.pallas_call(
        units_pre_kernel,
        grid_spec=pltpu.PrefetchScalarGridSpec(
            num_scalar_prefetch=1,
            grid=(seqs,),
            in_specs=[
                row((width, rows)),
                full_spec((1, width)),
                full_spec(w_query.shape),
                full_spec(w_key.shape),
                full_spec(w_value.shape),
                row((rows, LANES)),
                row((rows, LANES)),
            ],
            out_specs=[row((rows, width))]
            + [full_spec(shape) for shape in (long_shape, q_shape, kv_shape)],
        ),
        out_shape=[
            jax.ShapeDtypeStruct((seqs, rows, width), bf16),
            jax.ShapeDtypeStruct(long_shape, bf16),
            jax.ShapeDtypeStruct(q_shape, bf16),
            jax.ShapeDtypeStruct(kv_shape, bf16),
        ],
        compiler_params=params(60),
        name="project",
    )(ids, x, norm, w_query, w_key, w_value, cos, sin)


def attend_row(q, blocks, seen=None):
    rows = blocks[0].shape[0]
    peak = sums = None
    for first in range(0, len(blocks), UNROLL):
        part = blocks[first : first + UNROLL]
        scores = [dot(kv, q, NT) for kv in part]
        if first + len(part) == len(blocks):
            scores[-1] = jnp.where(causal_part(rows, PER), scores[-1], mask_low)
        tops = [jnp.max(sc, axis=0, keepdims=True) for sc in scores]
        flags = [None] * len(part)
        if seen is not None:
            flags = (seen + [None])[first : first + UNROLL]
            tops = [t if f is None else jnp.where(f, t, mask_low) for t, f in zip(tops, flags)]
        new_peak = functools.reduce(jnp.maximum, tops if peak is None else tops + [peak])
        shifts = [new_peak if f is None else jnp.where(f, new_peak, -mask_low) for f in flags]
        shares = [jnp.exp(sc - sh).astype(bf16).T for sc, sh in zip(scores, shifts)]
        ones = lane_index(rows) < HEAD_DIM
        values = [jnp.where(ones, jnp.ones((), bf16), kv) for kv in part]
        added = dot(jnp.concatenate(shares, axis=1), jnp.concatenate(values, axis=0))
        if peak is not None:
            fading = jnp.broadcast_to(jnp.exp(peak - new_peak), (LANES, peak.shape[1])).T
            added = sums * fading + added
        peak, sums = new_peak, added
    return peak, sums


def attend_result(peak, total):
    rows = total.shape[0] // PER
    moved = other_half(total)
    normal = moved / total
    log_total = peak + jnp.log(total.T[0:1])
    return [normal[h * rows : (h + 1) * rows] for h in range(PER)], log_total


def units_forward_kernel(count, ids, *refs):
    messages = refs[:count]
    out_ref, log_ref, q_ref, kv_ref = refs[-4:]
    rows = kv_ref.shape[1]
    me = ids[0]
    for t in range(count):
        block = lax.rem(me - t + count, count)
        heads, kv = read_long(messages[t], rows)
        for h in range(PER):
            q_ref[block, h * rows : (h + 1) * rows] = low_only(heads[h]).astype(bf16)
        kv_ref[block] = kv.astype(bf16)
    for i in range(count):
        new_peak, sums = attend_row(q_ref[i], [kv_ref[j] for j in range(i + 1)])
        heads, log_total = attend_result(new_peak, sums)
        log_ref[i] = log_total
        write_short(out_ref, lax.rem(i - me + count, count), heads)


def units_forward_call(ids, messages, after):
    count = len(messages)
    rows = messages[0].shape[0] * 2 // 5
    wide = PER * rows
    vmem = pl.BlockSpec(memory_space=pltpu.VMEM)
    return pl.pallas_call(
        functools.partial(units_forward_kernel, count),
        in_specs=[pl.BlockSpec(memory_space=pltpu.SMEM)]
        + [vmem] * count
        + [pl.BlockSpec(memory_space=pl.ANY)] * len(after),
        out_shape=[
            jax.ShapeDtypeStruct((count, rows * 3 // 2, LANES), bf16),
            jax.ShapeDtypeStruct((count, 1, wide), f32),
            jax.ShapeDtypeStruct((count, wide, LANES), bf16),
            jax.ShapeDtypeStruct((count, rows, LANES), bf16),
        ],
        compiler_params=params(48),
        name="units_forward",
    )(ids, *messages, *after)


def last_unit_forward_kernel(ids, q_ref, kv_ref, out_ref, log_ref):
    me = ids[0]
    count = kv_ref.shape[0]
    others = span(exchange_masks(count))[1:]
    blocks = [kv_ref[p] for p in range(1, count)] + [kv_ref[0]]
    heads, log_total = attend_result(
        *attend_row(q_ref[...], blocks, [(me ^ k) < me for k in others])
    )
    log_ref[...] = log_total
    write_short(out_ref, 0, heads)


def last_unit_forward_call(ids, q, kv):
    wide = q.shape[0]
    vmem = pl.BlockSpec(memory_space=pltpu.VMEM)
    return pl.pallas_call(
        last_unit_forward_kernel,
        in_specs=[pl.BlockSpec(memory_space=pltpu.SMEM), vmem, vmem],
        out_shape=[
            jax.ShapeDtypeStruct((1, wide // 2, LANES), bf16),
            jax.ShapeDtypeStruct((1, wide), f32),
        ],
        compiler_params=params(32),
        name="last_unit_forward",
    )(ids, q, kv)


def attend_back(q, d_out, kv, log_total, delta, diagonal):
    rows = kv.shape[0]
    scores = dot(kv, q, NT)
    probs = jnp.exp(scores - log_total)
    if diagonal:
        probs = jnp.where(causal_part(rows, PER), probs, 0.0)
    d_probs = dot(kv, d_out, NT)
    d_scores = (probs * (d_probs - delta)).astype(bf16)
    return (
        dot(probs.astype(bf16), d_out) + dot(d_scores, q),
        dot(d_scores.T, kv),
    )


def unpack_out(message, attn):
    heads, values = read_short(message), read_short(attn)
    delta = [
        jnp.sum(low_only(d * o).T, axis=0, keepdims=True) for d, o in zip(heads, values)
    ]
    d_out = jnp.concatenate([high_only(other_half(d)) for d in heads], axis=0)
    return d_out.astype(bf16), jnp.concatenate(delta, axis=1)


def last_unit_backward_kernel(
    ids, q_ref, kv_ref, d_ref, attn_ref, log_ref, d_kv_ref, d_q_ref, d_out
):
    me = ids[0]
    count = kv_ref.shape[0]
    d_value, delta = unpack_out(d_ref[...], attn_ref[...])
    d_out[...] = d_value
    log_total = log_ref[...]
    total = None
    for p, k in list(enumerate(span(exchange_masks(count))))[1:]:
        shift = jnp.where((me ^ k) < me, log_total, -mask_low)
        d_kv, d_q = attend_back(q_ref[...], d_out[...], kv_ref[p], shift, delta, False)
        d_kv_ref[me ^ k] = d_kv.astype(bf16)
        total = d_q if total is None else total + d_q
    d_kv, d_q = attend_back(q_ref[...], d_out[...], kv_ref[0], log_total, delta, True)
    d_kv_ref[me] = d_kv.astype(bf16)
    d_q_ref[...] = total + d_q


def last_unit_backward_call(ids, q, kv, d_message, attn, log_total):
    vmem = pl.BlockSpec(memory_space=pltpu.VMEM)
    return pl.pallas_call(
        last_unit_backward_kernel,
        in_specs=[pl.BlockSpec(memory_space=pltpu.SMEM)] + [vmem] * 5,
        out_shape=[
            jax.ShapeDtypeStruct(kv.shape, bf16),
            jax.ShapeDtypeStruct(q.shape, f32),
        ],
        scratch_shapes=[pltpu.VMEM(q.shape, bf16)],
        compiler_params=params(24),
        name="last_unit_backward",
    )(ids, q, kv, d_message, attn, log_total)


def units_backward_kernel(count, ids, *refs):
    messages, refs = refs[:count], refs[count:]
    q_ref, kv_ref, attn_ref, log_ref, last_ref, out_ref, d_out, delta, d_kv = refs
    rows = kv_ref.shape[1]
    me = ids[0]
    for t in range(count):
        block = lax.rem(me - t + count, count)
        value, row = unpack_out(messages[t][...], attn_ref[(count - t) % count])
        d_out[block] = value
        delta[block] = row
    for i in reversed(range(count)):
        d_query = None
        for first in range(0, i + 1, 2):
            places = list(range(first, min(first + 2, i + 1)))
            blocks = [kv_ref[j] for j in places]
            probs, d_scores = [], []
            for j, kv in zip(places, blocks):
                prob = jnp.exp(dot(kv, q_ref[i], NT) - log_ref[i])
                if j == i:
                    prob = jnp.where(causal_part(rows, PER), prob, 0.0)
                d_prob = dot(kv, d_out[i], NT)
                d_scores.append((prob * (d_prob - delta[i])).astype(bf16))
                probs.append(prob.astype(bf16))
            for j, prob, d_score in zip(places, probs, d_scores):
                term = dot(prob, d_out[i]) + dot(d_score, q_ref[i])
                d_kv[j] = term if i == count - 1 else d_kv[j] + term
            term = dot(jnp.concatenate([d.T for d in d_scores], axis=1), jnp.concatenate(blocks, axis=0))
            d_query = term if d_query is None else d_query + term
        tile = d_kv[i]
        write_long(
            out_ref,
            lax.rem(i - me + count, count),
            [d_query[h * rows : (h + 1) * rows] for h in range(PER)] + [tile, other_half(tile)],
            last_ref[i],
        )


def units_backward_call(ids, messages, q, kv, attn, log_total, last_d_kv):
    count, rows, _ = kv.shape
    wide = PER * rows
    vmem = pl.BlockSpec(memory_space=pltpu.VMEM)
    return pl.pallas_call(
        functools.partial(units_backward_kernel, count),
        in_specs=[pl.BlockSpec(memory_space=pltpu.SMEM)]
        + [vmem] * (count + 5),
        out_shape=jax.ShapeDtypeStruct((count, rows * 7 // 2, LANES), bf16),
        scratch_shapes=[
            pltpu.VMEM((count, wide, LANES), bf16),
            pltpu.VMEM((count, 1, wide), f32),
            pltpu.VMEM((count, rows, LANES), f32),
        ],
        compiler_params=params(56),
        name="units_backward",
    )(ids, *messages, q, kv, attn, log_total, last_d_kv)


def units_ffn_kernel(
    count,
    ids,
    x_ref,
    cot_ref,
    norm_ref,
    w_out_ref,
    w_gate_hbm,
    w_up_hbm,
    w_down_hbm,
    *refs,
):
    messages, last_message = refs[:count], refs[count]
    (
        mid_ref, attn, hid_hbm, d_gate_hbm, d_up_hbm, g_hbm,
        units, w_gate, w_up, w_down, cot, b, hid, d_gate, d_up, g_buf, w_sems, h_sems, g_sems,
    ) = refs[count + 1 :]
    me = ids[0]
    seqs, width, rows = x_ref.shape
    hidden = w_gate.shape[1]
    tiles = hidden // LANES
    loads = [
        pltpu.make_async_copy(source, target, w_sems.at[k])
        for k, (source, target) in enumerate(
            ((w_gate_hbm, w_gate), (w_up_hbm, w_up), (w_down_hbm, w_down))
        )
    ]
    for load in loads:
        load.start()
    for t in range(count):
        units[lax.rem(me - t + count, count)] = messages[t][...]
    units[count] = last_message[0]
    for s in range(seqs):
        here = slice(s * rows, (s + 1) * rows)
        heads = []
        for g in range(KV_HEADS):
            heads += read_short(units[s * KV_HEADS + g])
        parts = [join(heads[h], other_half(heads[h + 1])) for h in range(0, HEADS - 1, 2)]
        attn_rows = jnp.concatenate(parts + [heads[HEADS - 1][:, :HEAD_DIM]], axis=1).astype(bf16)
        attn[s] = attn_rows
        cot[here] = cot_ref[s].T
        mid_rows = x_ref[s].T.astype(f32) + dot(attn_rows, w_out_ref[...])
        scale = lax.rsqrt(
            jnp.sum(mid_rows * mid_rows, axis=-1, keepdims=True) * (1.0 / width) + eps_norm
        )
        mid_ref[s] = mid_rows
        b[here] = (mid_rows * scale * norm_ref[...]).astype(bf16)
    for load in loads:
        load.wait()
    chunk = 2 * LANES
    stores = []

    def store(source, target, sem):
        copy = pltpu.make_async_copy(source, target, sem)
        copy.start()
        stores.append(copy)

    for c in range(hidden // chunk):
        lanes = pl.ds(c * chunk, chunk)
        gate = dot(b[...], w_gate[:, lanes])
        up = dot(b[...], w_up[:, lanes])
        d_hid = dot(cot[...], w_down[:, lanes])
        sig = 1.0 / (1.0 + jnp.exp(-gate))
        active = gate * sig
        hid[:, lanes] = (active * up).astype(bf16)
        d_gate[:, lanes] = (d_hid * up * sig * (1.0 + gate * (1.0 - sig))).astype(bf16)
        d_up[:, lanes] = (d_hid * active).astype(bf16)
    for k, (source, target) in enumerate(((hid, hid_hbm), (d_gate, d_gate_hbm), (d_up, d_up_hbm))):
        store(source, target, h_sems.at[k])
    b_turned = b[...].T
    cot_turned = jnp.concatenate([cot_ref[s] for s in range(seqs)], axis=1)
    for k, (left, right) in enumerate(((b_turned, d_gate), (b_turned, d_up), (cot_turned, hid))):
        for c in range(hidden // chunk):
            product = dot(left, right[:, c * chunk : (c + 1) * chunk]).astype(bf16)
            for u in range(2):
                t = 2 * c + u
                half, at = ffn_place(k, t, tiles)
                here = pl.ds(at * width, width)
                g_buf[half, here, :] = product[:, u * LANES : (u + 1) * LANES]
                store(g_buf.at[half, here], g_hbm.at[half, here], g_sems.at[k * tiles + t])
    for copy in stores:
        copy.wait()


def units_ffn_call(ids, x, cot, messages, last_message, w_out, norm, w_gate, w_up, w_down):
    seqs, width, rows = x.shape
    hidden = w_gate.shape[1]
    count = len(messages)
    tokens = seqs * rows
    short = (rows * 3 // 2, LANES)
    tiles = hidden // LANES
    g_shape = (2, (tiles + tiles // 2) * width, LANES)
    vmem = pl.BlockSpec(memory_space=pltpu.VMEM)
    hbm = pl.BlockSpec(memory_space=pl.ANY)
    wide = (tokens, hidden)
    return pl.pallas_call(
        functools.partial(units_ffn_kernel, count),
        in_specs=[pl.BlockSpec(memory_space=pltpu.SMEM)]
        + [vmem] * 4
        + [hbm] * 3
        + [vmem] * (count + 1),
        out_specs=[vmem] * 2 + [hbm] * 4,
        out_shape=[
            jax.ShapeDtypeStruct((seqs, rows, width), f32),
            jax.ShapeDtypeStruct((seqs, rows, width), bf16),
            jax.ShapeDtypeStruct(wide, bf16),
            jax.ShapeDtypeStruct(wide, bf16),
            jax.ShapeDtypeStruct(wide, bf16),
            jax.ShapeDtypeStruct(g_shape, bf16),
        ],
        scratch_shapes=[
            pltpu.VMEM((count + 1,) + short, bf16),
            pltpu.VMEM(w_gate.shape, bf16),
            pltpu.VMEM(w_up.shape, bf16),
            pltpu.VMEM(w_down.shape, bf16),
            pltpu.VMEM((tokens, width), bf16),
            pltpu.VMEM((tokens, width), bf16),
            pltpu.VMEM(wide, bf16),
            pltpu.VMEM(wide, bf16),
            pltpu.VMEM(wide, bf16),
            pltpu.VMEM(g_shape, bf16),
            pltpu.SemaphoreType.DMA((3,)),
            pltpu.SemaphoreType.DMA((3,)),
            pltpu.SemaphoreType.DMA((3 * tiles,)),
        ],
        compiler_params=params(60),
        name="feed_forward",
    )(ids, x, cot, norm, w_out, w_gate, w_up, w_down, *messages, last_message)


def units_back_kernel(
    count,
    ids,
    mid_ref,
    cot_ref,
    d_gate_ref,
    d_up_ref,
    norm_ref,
    w_out_ref,
    w_gate_ref,
    w_up_ref,
    d_mid_ref,
    d_out_ref,
    d_last_ref,
    g_norm_ref,
):
    step = pl.program_id(0)
    me = ids[0]
    mid = mid_ref[0]
    rows, width = mid.shape
    cot = cot_ref[0].T
    scale = lax.rsqrt(jnp.sum(mid * mid, axis=-1, keepdims=True) * (1.0 / width) + eps_norm)
    normed = mid * scale
    d_b = dot(d_gate_ref[...], w_gate_ref[...], NT) + dot(d_up_ref[...], w_up_ref[...], NT)
    norm_term = jnp.sum(d_b * normed, axis=0, keepdims=True)
    e = d_b * norm_ref[...]
    mean = jnp.sum(e * normed, axis=-1, keepdims=True) * (1.0 / width)
    d_mid = cot.astype(f32) + scale * (e - normed * mean)
    d_mid_ref[0] = d_mid
    d_proj = d_mid.astype(bf16)
    d_tiles = head_tiles(dot(d_proj, w_out_ref[...], NT))
    d_heads = [
        d_tiles[h // 2] if h % 2 == 0 else other_half(d_tiles[h // 2]) for h in range(HEADS)
    ]
    for g in range(KV_HEADS):
        unit = step * KV_HEADS + g

        @pl.when(unit < count)
        def _(g=g, unit=unit):
            at = lax.rem(unit - me + count, count)
            write_short(d_out_ref, at, d_heads[g * PER : (g + 1) * PER])

        @pl.when(unit == count)
        def _(g=g):
            write_short(d_last_ref, 0, d_heads[g * PER : (g + 1) * PER])

    @pl.when(step == 0)
    def _():
        g_norm_ref[...] = norm_term

    @pl.when(step > 0)
    def _():
        g_norm_ref[...] += norm_term


def units_back_call(ids, mid, cot, d_gate, d_up, norm, w_out, w_gate, w_up, count):
    seqs, rows, width = mid.shape
    hidden = w_gate.shape[1]
    row = lambda *shape: pl.BlockSpec((1,) + shape, lambda s, *_: (s,) + (0,) * len(shape))
    part = pl.BlockSpec((rows, hidden), lambda s, *_: (s, 0))
    short = (rows * 3 // 2, LANES)
    return pl.pallas_call(
        functools.partial(units_back_kernel, count),
        grid_spec=pltpu.PrefetchScalarGridSpec(
            num_scalar_prefetch=1,
            grid=(seqs,),
            in_specs=[row(rows, width), row(width, rows), part, part, full_spec((1, width))]
            + [full_spec(w_out.shape), full_spec(w_gate.shape), full_spec(w_up.shape)],
            out_specs=[
                row(rows, width),
                full_spec((count,) + short),
                full_spec((1,) + short),
                full_spec((1, width)),
            ],
        ),
        out_shape=[
            jax.ShapeDtypeStruct((seqs, rows, width), f32),
            jax.ShapeDtypeStruct((count,) + short, bf16),
            jax.ShapeDtypeStruct((1,) + short, bf16),
            jax.ShapeDtypeStruct((1, width), f32),
        ],
        compiler_params=params(60),
        name="feed_back",
    )(ids, mid, cot, d_gate, d_up, norm, w_out, w_gate, w_up)


def units_out_kernel(
    mid_ref, attn_ref, hid_ref, d_mid_ref, g_norm_ref, w_down_ref, out_ref, g_ref, g_out
):
    step = pl.program_id(0)
    out_ref[0] = (mid_ref[0] + dot(hid_ref[...], w_down_ref[...], NT)).astype(bf16).T
    term = dot(attn_ref[0].T, d_mid_ref[0].astype(bf16))

    @pl.when(step == 0)
    def _():
        g_out[...] = term

    @pl.when(step > 0)
    def _():
        g_out[...] += term

    @pl.when(step == pl.num_programs(0) - 1)
    def _():
        column = jnp.broadcast_to(g_norm_ref[...], (8, g_norm_ref.shape[1])).T[:, :1]
        for t, tile in enumerate(head_tiles(g_out[...])):
            if t == g_ref.shape[0] - 1:
                tile = with_column(tile, column)
            g_ref[t] = tile.astype(bf16)


def units_out_call(mid, attn, hid, d_mid, g_norm, w_down):
    seqs, rows, width = mid.shape
    hidden = w_down.shape[1]
    row = lambda *shape: pl.BlockSpec((1,) + shape, lambda s: (s,) + (0,) * len(shape))
    g_shape = (-(-width // LANES), width, LANES)
    return pl.pallas_call(
        units_out_kernel,
        grid=(seqs,),
        in_specs=[
            row(rows, width),
            row(rows, width),
            pl.BlockSpec((rows, hidden), lambda s: (s, 0)),
            row(rows, width),
            full_spec((1, width)),
            full_spec(w_down.shape),
        ],
        out_specs=[row(width, rows), full_spec(g_shape)],
        out_shape=[
            jax.ShapeDtypeStruct((seqs, width, rows), bf16),
            jax.ShapeDtypeStruct(g_shape, bf16),
        ],
        scratch_shapes=[pltpu.VMEM((width, width), f32)],
        compiler_params=params(60),
        name="feed_out",
    )(mid, attn, hid, d_mid, g_norm, w_down)


def units_last_kernel(
    count, ids, x_ref, a_ref, norm_ref, wq_ref, wk_ref, wv_ref, cos_ref, sin_ref, d_mid_ref, last_q_ref,
    g_out_ref, *refs,
):
    messages = refs[:count]
    out_ref, g_ref, units, g_query, g_pairs, d_norm = refs[count:]
    step = pl.program_id(0)
    me = ids[0]
    x = x_ref[0].T.astype(f32)
    rows, width = x.shape

    @pl.when(step == 0)
    def _():
        for t in range(count):
            units[lax.rem(me - t + count, count)] = messages[t][: rows * 5 // 2]
        last_kv = sum(messages[t][rows * 5 // 2 :].astype(f32) for t in range(count))
        heads = [last_q_ref[h * rows : (h + 1) * rows] for h in range(PER)]
        write_long(units, count, heads + [last_kv, other_half(last_kv)])

    cos, sin = cos_ref[0], sin_ref[0]

    def turn(tile):
        return tile * cos - swap_halves(tile) * sin

    heads, keys, values = [], [], []
    for g in range(KV_HEADS):
        parts, kv = read_long(units[step * KV_HEADS + g], rows)
        heads += parts
        keys.append(kv)
        values.append(other_half(kv))

    def in_tiles(parts, scale):
        tiles = [
            join(parts[h], other_half(parts[h + 1])) for h in range(0, len(parts) - 1, 2)
        ] + [parts[-1]]
        return tiles if scale is None else [turn(t) * scale for t in tiles]

    def flat(tiles):
        return jnp.concatenate(tiles[:-1] + [tiles[-1][:, :HEAD_DIM]], axis=1).astype(bf16)

    d_query = flat(in_tiles(heads, 0.125))
    key_tiles = in_tiles(keys, 1.0)
    d_key, d_value = flat(key_tiles), flat(in_tiles(values, None))
    turned = [key_tiles[g // 2] if g % 2 == 0 else other_half(key_tiles[g // 2]) for g in range(KV_HEADS)]
    pairs = jnp.concatenate(
        [join(turned[g], other_half(values[g])) for g in range(KV_HEADS)], axis=1
    ).astype(bf16)
    a_turned = a_ref[0].T
    query_term = dot(a_turned, d_query)
    pair_term = dot(a_turned, pairs)
    d_a = (
        dot(d_query, wq_ref[...], NT) + dot(d_key, wk_ref[...]) + dot(d_value, wv_ref[...])
    )
    scale = lax.rsqrt(jnp.sum(x * x, axis=-1, keepdims=True) * (1.0 / width) + eps_norm)
    normed = x * scale
    norm_term = jnp.sum(d_a * normed, axis=0, keepdims=True)

    @pl.when(step == 0)
    def _():
        d_norm[...] = norm_term
        g_query[...] = query_term
        g_pairs[...] = pair_term

    @pl.when(step > 0)
    def _():
        d_norm[...] += norm_term
        g_query[...] += query_term
        g_pairs[...] += pair_term

    e = d_a * norm_ref[...]
    mean = jnp.sum(e * normed, axis=-1, keepdims=True) * (1.0 / width)
    out_ref[0] = (d_mid_ref[0] + scale * (e - normed * mean)).astype(bf16).T

    @pl.when(step == pl.num_programs(0) - 1)
    def _():
        square = -(-width // LANES)
        column = jnp.broadcast_to(d_norm[...], (8, width)).T[:, :1]
        for t, tile in enumerate(head_tiles(g_query[...])):
            if t == square - 1:
                tile = with_column(tile, column)
            put(g_ref, attn_place(t), width, tile.astype(bf16))
        for g in range(KV_HEADS):
            tile = g_pairs[:, g * LANES : (g + 1) * LANES]
            put(g_ref, attn_place(square + g), width, tile.astype(bf16))
        for t in range(square):
            put(g_ref, attn_place(square + KV_HEADS + t), width, g_out_ref[t])
        clear_rest(g_ref, 2 * square + KV_HEADS, width)


def clear_rest(g_ref, places, width):
    for half in range(2):
        used = (places + 1 - half) // 2 * width
        left_over = g_ref.shape[1] - used
        if left_over:
            g_ref[half, used:, :] = jnp.zeros((left_over, LANES), bf16)


def units_last_call(
    ids, x, a, norm, w_query, w_key, w_value, cos, sin, d_mid, last_d_q, g_out, messages, parts
):
    seqs, width, rows = x.shape
    count = len(messages)
    row = lambda *shape: pl.BlockSpec((1,) + shape, lambda s, *_: (s,) + (0,) * len(shape))
    places = -(-(2 * -(-width // LANES) + KV_HEADS) // 2)
    g_shape = (2, half_rows(places, width, parts), LANES)
    return pl.pallas_call(
        functools.partial(units_last_kernel, count),
        grid_spec=pltpu.PrefetchScalarGridSpec(
            num_scalar_prefetch=1,
            grid=(seqs,),
            in_specs=[
                row(width, rows),
                row(rows, width),
                full_spec((1, width)),
                full_spec(w_query.shape),
                full_spec(w_key.shape),
                full_spec(w_value.shape),
                row(rows, LANES),
                row(rows, LANES),
                row(rows, width),
                full_spec(last_d_q.shape),
                full_spec(g_out.shape),
            ]
            + [full_spec(m.shape) for m in messages],
            out_specs=[row(width, rows), full_spec(g_shape)],
            scratch_shapes=[
                pltpu.VMEM((count + 1, rows * 5 // 2, LANES), bf16),
                pltpu.VMEM((width, width), f32),
                pltpu.VMEM((width, KV_HEADS * LANES), f32),
                pltpu.VMEM((1, width), f32),
            ],
        ),
        out_shape=[
            jax.ShapeDtypeStruct((seqs, width, rows), bf16),
            jax.ShapeDtypeStruct(g_shape, bf16),
        ],
        compiler_params=params(60),
        name="last_part",
    )(ids, x, a, norm, w_query, w_key, w_value, cos, sin, d_mid, last_d_q, g_out, *messages)


def to_all(messages):
    count = messages.shape[0]
    return [messages[0]] + [
        lax.ppermute(messages[t], "seq", [(i, (i + t) % count) for i in range(count)])
        for t in range(1, count)
    ]


def rope_tables(positions):
    half = HEAD_DIM // 2
    lane = jnp.arange(LANES, dtype=jnp.int32)
    frequency = jnp.exp((lane % half).astype(f32) * (-math.log(10000.0) / half))
    angles = positions.T.astype(f32)[..., None] * frequency
    return jnp.cos(angles), jnp.where(lane % HEAD_DIM < half, -1.0, 1.0) * jnp.sin(angles)


def spread_layer(
    x, cot, cos, sin, norm_one, norm_two, w_query, wk_turned, wv_turned, w_out, w_gate, w_up,
    w_down_turned, count, devices, sum_over, places_ok,
):
    seqs, width, rows = x.shape
    me = lax.axis_index("seq")
    a, q, kv = pre_call(x, norm_one, w_query, wk_turned, wv_turned, cos, sin)
    rounds, numbers = gather_blocks(kv, count)
    last = len(rounds) - 2

    def ids_of(picked):
        return jnp.stack([me] + [k for part in picked for k in part]).astype(jnp.int32)

    state = forward_call(ids_of(numbers[:last]), q, kv, rounds[:last], None, False)
    far, far_ids = rounds[last:], ids_of(numbers[last:])
    attn, log_total = forward_call(far_ids, q, None, far, state, True)
    (block_out, b, hid, d_gate, d_up, d_mid, d_proj, d_out, delta, g_norm_mlp) = middle_call(
        x, cot, attn, w_out, norm_two, w_gate, w_up, w_down_turned
    )
    flat = lambda t: t.reshape(seqs * rows, t.shape[-1])
    g_ffn = ffn_grad_call(flat(b), cot, flat(hid), flat(d_gate), flat(d_up))
    g_ffn = lax.psum(g_ffn, ("seq", "batch"))
    common = (q, d_out, log_total, delta)
    _, far_terms, d_query = backward_call(far_ids, *common, None, far, None, None)
    far_terms = [jnp.concatenate([t, u], axis=0) for t, u in zip(*far_terms)]
    got = [return_round(far_terms, last, count)]
    _, mid_terms, d_query = backward_call(
        ids_of(numbers[last - 1 : last]), *common, None, rounds[last - 1 : last], d_query, None
    )
    half = far_terms[0].shape[0] // 2
    mid_terms = [add_low(t, g[half:]) for t, g in zip(mid_terms[0], got[0])]
    got.append(return_round(mid_terms, last - 1, count))
    own_terms, near_terms, d_q = backward_call(
        ids_of(numbers[: last - 1]), *common, kv, rounds[: last - 1], d_query, (cos, sin),
        tuple(mid_terms),
    )
    for r in reversed(range(last - 1)):
        size = 1 << r
        terms = [
            add_low(t, *(g[s][size : 2 * size] for g in got)) for s, t in enumerate(near_terms[r])
        ]
        got.append(return_round(terms, r, count))
    d_kv = jnp.concatenate(
        [add_low(own_terms[s : s + 1], *(g[s][:1] for g in got)) for s in range(seqs)], axis=0
    )
    d_aq, g_query, g_out = query_grad_call(
        flat(a), flat(attn), flat(d_proj), flat(d_q), g_norm_mlp, w_query
    )
    d_tokens, g_attn = last_call(
        x, a, norm_one, wk_turned, wv_turned, cos, sin, d_kv,
        d_aq.reshape(seqs, rows, width), d_mid, g_query, g_out, devices,
    )
    return block_out, d_tokens, g_ffn, sum_over(g_attn)


def units_layer(
    x, cot, cos, sin, norm_one, norm_two, w_query, wk_turned, wv_turned, w_out, w_gate, w_up,
    w_down_turned, count, devices, sum_over, places_ok,
):
    seqs, width, rows = x.shape
    flat = lambda t: t.reshape(seqs * rows, t.shape[-1])
    ids = lax.axis_index("seq").astype(jnp.int32).reshape(1)
    a, messages, last_q, last_kv = units_pre_call(
        ids, x, norm_one, w_query, wk_turned, wv_turned, cos, sin, count
    )
    masks = exchange_masks(count)
    swap = lambda part, mask: lax.ppermute(part, "seq", [(i, i ^ mask) for i in range(count)])
    arrived = to_all(messages)
    for mask in masks[:-1]:
        last_kv = jnp.concatenate([last_kv, swap(last_kv, mask)], axis=0)
    attn_out, log_total, q, kv = units_forward_call(ids, arrived, (last_kv,))
    last_kv = jnp.concatenate([last_kv, swap(last_kv, masks[-1])], axis=0)
    last_attn, last_log = last_unit_forward_call(ids, last_q, last_kv)
    mid, attn, hid, d_gate, d_up, g_ffn = units_ffn_call(
        ids, x, cot, to_all(attn_out), last_attn, w_out, norm_two, w_gate, w_up, w_down_turned
    )
    g_ffn = lax.psum(g_ffn, ("seq", "batch"))

    def backward(mid, attn, hid, d_gate, d_up, q, kv, attn_out, log_total, last_attn, last_log, a):
        d_mid, d_messages, d_last, g_norm_mlp = units_back_call(
            ids, mid, cot, d_gate, d_up, norm_two, w_out, w_gate, w_up, count
        )
        block_out, g_out = units_out_call(mid, attn, hid, d_mid, g_norm_mlp, w_down_turned)
        last_d_kv, last_d_q = last_unit_backward_call(
            ids, last_q, last_kv, d_last[0], last_attn[0], last_log
        )
        d_all = units_backward_call(
            ids, to_all(d_messages), q, kv, attn_out, log_total, last_d_kv
        )
        d_tokens, g_attn = units_last_call(
            ids, x, a, norm_one, w_query, wk_turned, wv_turned, cos, sin, d_mid, last_d_q, g_out,
            to_all(d_all), devices,
        )
        return (block_out, d_tokens) + sum_over(g_attn)

    block_out, d_tokens, *attn_sums = in_one_piece(
        places_ok,
        backward,
        (mid, attn, hid, d_gate, d_up, q, kv, attn_out, log_total, last_attn, last_log, a),
    )
    return block_out, d_tokens, g_ffn, attn_sums


def in_one_piece(always, part, operands):
    shapes = jax.eval_shape(part, *operands)

    def never(*_):
        return jax.tree.map(lambda t: jnp.zeros(t.shape, t.dtype), shapes)

    return lax.cond(always, part, never, *operands)


def on_device(
    tokens,
    positions,
    norm_attn,
    w_query,
    w_key,
    w_value,
    w_out,
    norm_mlp,
    w_gate,
    w_up,
    w_down,
    cotangent,
):
    rows, seqs, width = tokens.shape
    hidden = w_gate.shape[1]
    kv_width = KV_HEADS * HEAD_DIM
    count, batches = lax.axis_size("seq"), lax.axis_size("batch")
    me = lax.axis_index("seq")
    devices = count * batches
    stages = device_stages(count, batches)
    places = stage_places(stages, me * batches + lax.axis_index("batch"))
    x = jnp.transpose(tokens, (1, 2, 0))
    cot = jnp.transpose(cotangent, (1, 2, 0))
    wk_turned, wv_turned, w_down_turned = w_key.T, w_value.T, w_down.T
    cos, sin = rope_tables(positions)
    norm_one, norm_two = norm_attn[None], norm_mlp[None]
    def sum_over(value):
        for stage, place in zip(stages, places):
            value = scatter_stage(value, stage, place, devices)
        return gather_sums(value, stages, places, devices, 1)

    layer = units_layer if count == seqs * KV_HEADS - 1 else spread_layer
    block_out, d_tokens, g_ffn, attn_sums = layer(
        x, cot, cos, sin, norm_one, norm_two, w_query, wk_turned, wv_turned, w_out, w_gate, w_up,
        w_down_turned, count, devices, sum_over, positions[0, 0] >= 0,
    )
    side = places[0].reshape(1).astype(jnp.int32)
    g_gate, g_up, g_down = ffn_unfold_call(g_ffn, width, hidden)
    g_query, g_key, g_value, g_norm_attn, g_out, g_norm_mlp = unfold_call(
        attn_unfold_kernel,
        "attn_unfold",
        (side, *attn_sums),
        [(width, width), (kv_width, width), (kv_width, width), (1, width)]
        + [(width, width), (1, width)],
    )
    return (
        jnp.transpose(block_out, (2, 0, 1)),
        jnp.transpose(d_tokens, (2, 0, 1)),
        g_norm_attn[0],
        g_query,
        g_key.T,
        g_value.T,
        g_out,
        g_norm_mlp[0],
        g_gate,
        g_up,
        g_down.T,
    )


def solution(mesh):
    split = P("seq", "batch", None)
    return jax.shard_map(
        on_device,
        mesh=mesh,
        in_specs=(split, P("seq", "batch")) + (P(),) * 9 + (split,),
        out_specs=(split, split) + (P(),) * 9,
        check_vma=False,
    )
```

```python
import functools
import math

import jax
import jax.numpy as jnp
from jax import lax
from jax.experimental import pallas as pl
from jax.experimental.pallas import tpu as pltpu
from jax.sharding import PartitionSpec as P

HEADS = 9
KV_HEADS = 3
HEAD_DIM = 64
PER = HEADS // KV_HEADS
LANES = 128

eps_norm = 1e-05
mask_low = -1e30
f32 = jnp.float32
bf16 = jnp.bfloat16

NN = (((1,), (0,)), ((), ()))
NT = (((1,), (1,)), ((), ()))
TN = (((0,), (0,)), ((), ()))
UNROLL = 4


def dot(left, right, dims=NN):
    return lax.dot_general(left, right, dims, preferred_element_type=f32)


def params(mib):
    return pltpu.CompilerParams(vmem_limit_bytes=mib * 1024 * 1024)


def as_row(ref):
    return ref[...].reshape(1, ref.shape[0])


def full_spec(shape):
    zeros = (0,) * len(shape)
    return pl.BlockSpec(shape, lambda *_: zeros)


def lane_index(rows):
    return lax.broadcasted_iota(jnp.int32, (rows, LANES), 1)


def swap_halves(tile):
    half = HEAD_DIM // 2
    lane = lane_index(tile.shape[0])
    return jnp.where(
        lane % HEAD_DIM < half, pltpu.roll(tile, LANES - half, 1), pltpu.roll(tile, half, 1)
    )


def head_tiles(lin):
    rows, width = lin.shape
    if width % LANES:
        lin = jnp.concatenate([lin, jnp.zeros((rows, HEAD_DIM), lin.dtype)], axis=1)
    return [lin[:, at : at + LANES] for at in range(0, lin.shape[1], LANES)]


def pre_kernel(
    x_ref, norm_ref, wq_ref, wk_ref, wv_ref, cos_ref, sin_ref, a_ref, q_ref, kv_ref
):
    x = x_ref[0].T.astype(f32)
    rows, width = x.shape
    scale = lax.rsqrt(jnp.sum(x * x, axis=-1, keepdims=True) * (1.0 / width) + eps_norm)
    a = (x * scale * as_row(norm_ref)).astype(bf16)
    a_ref[0] = a
    cos, sin = cos_ref[0], sin_ref[0]
    low_half = lane_index(rows) < HEAD_DIM

    def turn(tile):
        return tile * cos + swap_halves(tile) * sin

    keys = [turn(tile) for tile in head_tiles(dot(a, wk_ref[...], NT))]
    values = head_tiles(dot(a, wv_ref[...], NT))
    for g in range(KV_HEADS):
        key, value = keys[g // 2], values[g // 2]
        if g % 2 == 0:
            value = pltpu.roll(value, HEAD_DIM, 1)
        else:
            key = pltpu.roll(key, HEAD_DIM, 1)
        kv_ref[0, :, g * LANES : (g + 1) * LANES] = jnp.where(low_half, key, value).astype(bf16)
    queries = [turn(tile) * 0.125 for tile in head_tiles(dot(a, wq_ref[...]))]
    for head in range(HEADS):
        tile = queries[head // 2]
        if head % 2:
            tile = pltpu.roll(tile, HEAD_DIM, 1)
        group, place = divmod(head, PER)
        q_ref[0, group, place * rows : (place + 1) * rows, :] = jnp.where(
            low_half, tile, 0.0
        ).astype(bf16)


def pre_call(x, norm, w_query, w_key, w_value, cos, sin):
    seqs, width, rows = x.shape
    row = lambda shape: pl.BlockSpec((1,) + shape, lambda s: (s,) + (0,) * len(shape))
    return pl.pallas_call(
        pre_kernel,
        grid=(seqs,),
        in_specs=[
            row((width, rows)),
            full_spec((width,)),
            full_spec(w_query.shape),
            full_spec(w_key.shape),
            full_spec(w_value.shape),
            row((rows, LANES)),
            row((rows, LANES)),
        ],
        out_specs=[
            row((rows, width)),
            row((KV_HEADS, PER * rows, LANES)),
            row((rows, KV_HEADS * LANES)),
        ],
        out_shape=[
            jax.ShapeDtypeStruct((seqs, rows, width), bf16),
            jax.ShapeDtypeStruct((seqs, KV_HEADS, PER * rows, LANES), bf16),
            jax.ShapeDtypeStruct((seqs, rows, KV_HEADS * LANES), bf16),
        ],
        compiler_params=params(16),
        name="project",
    )(x, norm, w_query, w_key, w_value, cos, sin)


def causal_part(rows, heads):
    key = lax.broadcasted_iota(jnp.int32, (rows, rows), 0)
    query = lax.broadcasted_iota(jnp.int32, (rows, rows), 1)
    return jnp.concatenate([key <= query] * heads, axis=1)


def for_blocks(ids, me, seqs, own, pieces, counts, work, zeros=None):
    if own is not None:
        for s in range(seqs):
            work(s, own[s], None, (-1, s, s))
    first = 1
    for k, (parts, count) in enumerate(zip(pieces, counts)):
        least = ids[first]
        for n in range(1, seqs * count):
            least = jnp.minimum(least, ids[first + n])
        unroll = min(count, UNROLL)

        @pl.when(least < me)
        def _(parts=parts, first=first, count=count, k=k):
            def some(c, _):
                for s in range(seqs):
                    for u in range(unroll):
                        j = c * unroll + u
                        work(s, parts[s][j], ids[first + s * count + j] < me, (k, s, j))
                return 0

            if count == unroll:
                some(0, 0)
            else:
                lax.fori_loop(0, count // unroll, some, 0)

        if zeros is not None:

            @pl.when(least >= me)
            def _(k=k):
                zeros(k)

        first += seqs * count


def forward_kernel(counts, has_own, has_state, is_last, ids, *refs):
    refs = list(refs)
    q = refs.pop(0)
    seqs, rows = q.shape[0], q.shape[2] // PER
    own = refs.pop(0) if has_own else None
    pieces = [[refs.pop(0) for _ in range(seqs)] for _ in counts]
    if has_state:
        peak_in, total_in = refs.pop(0), refs.pop(0)
    outs, (peak, total) = refs[:-2], refs[-2:]
    me = ids[0]
    if has_state:
        peak[...] = peak_in[:, 0]
        total[...] = total_in[:, 0]
    low_half = lane_index(rows) < HEAD_DIM

    def attend(s, kv, seen):
        ones_values = jnp.where(low_half, jnp.ones((), bf16), kv)
        scores = dot(kv, q[s, 0], NT)
        if seen is None:
            scores = jnp.where(causal_part(rows, PER), scores, mask_low)
            new_peak = shift = jnp.max(scores, axis=0, keepdims=True)
        else:
            old_peak = peak[s]
            top = jnp.max(scores, axis=0, keepdims=True)
            new_peak = jnp.where(seen, jnp.maximum(old_peak, top), old_peak)
            shift = jnp.where(seen, new_peak, -mask_low)
        shares = jnp.exp(scores - shift).astype(bf16)
        added = dot(shares.T, ones_values)
        if seen is None:
            total[s] = added
        else:
            total[s] = total[s] * jnp.exp(old_peak - new_peak).T + added
        peak[s] = new_peak

    for_blocks(ids, me, seqs, own, pieces, counts, lambda s, kv, seen, store: attend(s, kv, seen))
    if is_last:
        attn, log_total = outs
        group = pl.program_id(0)
        for s in range(seqs):
            acc = total[s]
            normal = acc / pltpu.roll(acc, HEAD_DIM, 1)
            sums = acc.T[0:1]
            log_total[s, 0] = peak[s] + jnp.log(sums)
            values = normal[:, HEAD_DIM:].astype(bf16)
            for g in range(KV_HEADS):

                @pl.when(group == g)
                def _(values=values, s=s, g=g):
                    for h in range(PER):
                        at = (g * PER + h) * HEAD_DIM
                        attn[s, :, at : at + HEAD_DIM] = values[h * rows : (h + 1) * rows]

    else:
        outs[0][:, 0] = peak[...]
        outs[1][:, 0] = total[...]


def piece_spec(count, rows):
    return pl.BlockSpec((count, rows, LANES), lambda g, *_: (0, 0, g))


def group_spec(seqs, *shape):
    zeros = (0,) * len(shape)
    return pl.BlockSpec((seqs, 1) + shape, lambda g, *_: (0, g) + zeros)


def forward_call(ids, q, own, pieces, state, is_last):
    seqs, groups, wide, _ = q.shape
    rows = wide // PER
    counts = [parts[0].shape[0] for parts in pieces]
    arrays, specs = [q], [group_spec(seqs, wide, LANES)]
    if own is not None:
        arrays.append(own)
        specs.append(piece_spec(seqs, rows))
    for parts, count in zip(pieces, counts):
        arrays += parts
        specs += [piece_spec(count, rows)] * seqs
    row_spec, row_shape = group_spec(seqs, 1, wide), (seqs, groups, 1, wide)
    sum_spec, sum_shape = group_spec(seqs, wide, LANES), (seqs, groups, wide, LANES)
    if state is not None:
        arrays += list(state)
        specs += [row_spec, sum_spec]
    if is_last:
        attn_shape = (seqs, rows, HEADS * HEAD_DIM)
        out_shape = [
            jax.ShapeDtypeStruct(attn_shape, bf16),
            jax.ShapeDtypeStruct(row_shape, f32),
        ]
        out_specs = [full_spec(attn_shape), row_spec]
    else:
        out_shape = [
            jax.ShapeDtypeStruct(row_shape, f32),
            jax.ShapeDtypeStruct(sum_shape, f32),
        ]
        out_specs = [row_spec, sum_spec]
    return pl.pallas_call(
        functools.partial(
            forward_kernel, counts, own is not None, state is not None, is_last
        ),
        out_shape=out_shape,
        grid_spec=pltpu.PrefetchScalarGridSpec(
            num_scalar_prefetch=1,
            grid=(groups,),
            in_specs=specs,
            out_specs=out_specs,
            scratch_shapes=[
                pltpu.VMEM((seqs, 1, wide), f32),
                pltpu.VMEM((seqs, wide, LANES), f32),
            ],
        ),
        compiler_params=params(60),
        name="attend_forward",
    )(ids, *arrays)


def backward_kernel(counts, has_own, has_state, is_last, waits, ids, *refs):
    refs = list(refs)[waits:]
    q, d_out, log_total, delta = refs[:4]
    refs = refs[4:]
    seqs, rows = q.shape[0], q.shape[2] // PER
    own = refs.pop(0) if has_own else None
    pieces = [[refs.pop(0) for _ in range(seqs)] for _ in counts]
    d_query_in = refs.pop(0) if has_state else None
    cos, sin = (refs.pop(0), refs.pop(0)) if is_last else (None, None)
    d_own = refs.pop(0) if has_own else None
    d_pieces = [[refs.pop(0) for _ in range(seqs)] for _ in counts]
    d_query_out, d_query = refs
    me = ids[0]
    if has_state:
        d_query[...] = d_query_in[:, 0]
    else:
        d_query[...] = jnp.zeros_like(d_query)

    def back(s, kv, seen, place):
        q_all, d_all = q[s, 0], d_out[s, 0]
        scores = dot(kv, q_all, NT)
        if seen is None:
            probs = jnp.exp(scores - log_total[s, 0])
            probs = jnp.where(causal_part(rows, PER), probs, 0.0)
        else:
            probs = jnp.exp(scores - jnp.where(seen, log_total[s, 0], -mask_low))
        d_probs = dot(kv, d_all, NT)
        d_scores = (probs * (d_probs - delta[s, 0])).astype(bf16)
        d_query[s] += dot(d_scores.T, kv)
        terms = (dot(probs.astype(bf16), d_all) + dot(d_scores, q_all)).astype(bf16)
        piece, s, j = place
        if piece < 0:
            d_own[s] = terms
        else:
            d_pieces[piece][s][j] = terms

    def zeros(piece):
        for s in range(seqs):
            d_pieces[piece][s][...] = jnp.zeros(d_pieces[piece][s].shape, bf16)

    for_blocks(ids, me, seqs, own, pieces, counts, back, zeros)
    if is_last:
        group = pl.program_id(0)
        for s in range(seqs):
            turned = []
            for h in range(PER):
                tile = d_query[s, h * rows : (h + 1) * rows, :] * 0.125
                turned.append(
                    (tile * cos[s] - swap_halves(tile) * sin[s])[:, :HEAD_DIM].astype(bf16)
                )
            for g in range(KV_HEADS):

                @pl.when(group == g)
                def _(turned=turned, s=s, g=g):
                    for h in range(PER):
                        at = (g * PER + h) * HEAD_DIM
                        d_query_out[s, :, at : at + HEAD_DIM] = turned[h]

    else:
        d_query_out[:, 0] = d_query[...]


def backward_call(ids, q, d_out, log_total, delta, own, pieces, d_query, tables, after=()):
    seqs, groups, wide, _ = q.shape
    rows = wide // PER
    counts = [parts[0].shape[0] for parts in pieces]
    sum_spec, sum_shape = group_spec(seqs, wide, LANES), (seqs, groups, wide, LANES)
    row_spec = group_spec(seqs, 1, wide)
    arrays = [q, d_out, log_total, delta]
    specs = [sum_spec, sum_spec, row_spec, row_spec]
    out_shape, out_specs = [], []
    if own is not None:
        arrays.append(own)
        specs.append(piece_spec(seqs, rows))
        out_shape.append(jax.ShapeDtypeStruct(own.shape, bf16))
        out_specs.append(piece_spec(seqs, rows))
    for parts, count in zip(pieces, counts):
        arrays += parts
        specs += [piece_spec(count, rows)] * seqs
        out_shape += [jax.ShapeDtypeStruct(parts[0].shape, bf16)] * seqs
        out_specs += [piece_spec(count, rows)] * seqs
    if d_query is not None:
        arrays.append(d_query)
        specs.append(sum_spec)
    is_last = tables is not None
    if is_last:
        arrays += list(tables)
        specs += [full_spec((seqs, rows, LANES))] * 2
        shape = (seqs, rows, HEADS * HEAD_DIM)
        out_shape.append(jax.ShapeDtypeStruct(shape, bf16))
        out_specs.append(full_spec(shape))
    else:
        out_shape.append(jax.ShapeDtypeStruct(sum_shape, f32))
        out_specs.append(sum_spec)
    arrays = list(after) + arrays
    specs = [pl.BlockSpec(memory_space=pl.ANY)] * len(after) + specs
    outs = pl.pallas_call(
        functools.partial(
            backward_kernel, counts, own is not None, d_query is not None, is_last, len(after)
        ),
        out_shape=out_shape,
        grid_spec=pltpu.PrefetchScalarGridSpec(
            num_scalar_prefetch=1,
            grid=(groups,),
            in_specs=specs,
            out_specs=out_specs,
            scratch_shapes=[pltpu.VMEM((seqs, wide, LANES), f32)],
        ),
        compiler_params=params(60),
        name="attend_backward",
    )(ids, *arrays)
    d_own = None
    if own is not None:
        d_own, outs = outs[0], outs[1:]
    d_pieces = [list(outs[k * seqs : (k + 1) * seqs]) for k in range(len(counts))]
    return d_own, d_pieces, outs[-1]


def middle_kernel(
    x_ref,
    cot_ref,
    attn_ref,
    w_out_ref,
    norm_ref,
    w_gate_ref,
    w_up_ref,
    w_down_ref,
    out_ref,
    b_ref,
    hid_ref,
    d_gate_ref,
    d_up_ref,
    d_mid_ref,
    d_proj_ref,
    d_out_ref,
    delta_ref,
    g_norm_ref,
):
    x = x_ref[0].T.astype(f32)
    rows, width = x.shape
    cot = cot_ref[0].T
    attn = attn_ref[0]
    mid = x + dot(attn, w_out_ref[...])
    scale = lax.rsqrt(jnp.sum(mid * mid, axis=-1, keepdims=True) * (1.0 / width) + eps_norm)
    normed = mid * scale
    b = (normed * as_row(norm_ref)).astype(bf16)
    b_ref[0] = b
    gate = dot(b, w_gate_ref[...])
    up = dot(b, w_up_ref[...])
    sig = 1.0 / (1.0 + jnp.exp(-gate))
    active = gate * sig
    hid = (active * up).astype(bf16)
    hid_ref[0] = hid
    out_ref[0] = (mid + dot(hid, w_down_ref[...], NT)).astype(bf16).T
    d_hid = dot(cot, w_down_ref[...])
    d_gate = (d_hid * up * sig * (1.0 + gate * (1.0 - sig))).astype(bf16)
    d_up = (d_hid * active).astype(bf16)
    d_gate_ref[0] = d_gate
    d_up_ref[0] = d_up
    d_b = dot(d_gate, w_gate_ref[...], NT) + dot(d_up, w_up_ref[...], NT)
    g_norm = jnp.sum(d_b * normed, axis=0, keepdims=True)

    @pl.when(pl.program_id(0) == 0)
    def _():
        g_norm_ref[...] = g_norm

    @pl.when(pl.program_id(0) > 0)
    def _():
        g_norm_ref[...] += g_norm

    e = d_b * as_row(norm_ref)
    mean = jnp.sum(e * normed, axis=-1, keepdims=True) * (1.0 / width)
    d_mid = cot.astype(f32) + scale * (e - normed * mean)
    d_mid_ref[0] = d_mid
    d_proj = d_mid.astype(bf16)
    d_proj_ref[0] = d_proj
    d_attn = dot(d_proj, w_out_ref[...], NT).astype(bf16).astype(f32)
    both = d_attn * attn.astype(f32)
    high = both.astype(bf16)
    rest = (both - high.astype(f32)).astype(bf16)
    head = lax.broadcasted_iota(jnp.int32, (16, width), 0)
    feature = lax.broadcasted_iota(jnp.int32, (16, width), 1)
    picks = jnp.where(
        (feature >= head * HEAD_DIM) & (feature < (head + 1) * HEAD_DIM), 1.0, 0.0
    ).astype(bf16)
    sums = dot(picks, high, NT) + dot(picks, rest, NT)
    high_half = lane_index(rows) >= HEAD_DIM
    padded = jnp.concatenate([d_attn, jnp.zeros((rows, HEAD_DIM), f32)], axis=1)
    for k in range(HEADS):
        at = k // 2 * LANES
        tile = padded[:, at : at + LANES]
        if k % 2 == 0:
            tile = pltpu.roll(tile, HEAD_DIM, 1)
        group, place = divmod(k, PER)
        here = slice(place * rows, (place + 1) * rows)
        d_out_ref[0, group, here, :] = jnp.where(high_half, tile, 0.0).astype(bf16)
        delta_ref[0, group, 0:1, here] = sums[k : k + 1]


def middle_call(x, cot, attn, w_out, norm, w_gate, w_up, w_down):
    seqs, width, rows = x.shape
    hidden = w_gate.shape[1]
    row = lambda *shape: pl.BlockSpec((1,) + shape, lambda s: (s,) + (0,) * len(shape))
    wide = PER * rows
    shapes = [
        ((width, rows), bf16),
        ((rows, width), bf16),
        ((rows, hidden), bf16),
        ((rows, hidden), bf16),
        ((rows, hidden), bf16),
        ((rows, width), f32),
        ((rows, width), bf16),
        ((KV_HEADS, wide, LANES), bf16),
        ((KV_HEADS, 1, wide), f32),
    ]
    return pl.pallas_call(
        middle_kernel,
        grid=(seqs,),
        in_specs=[row(width, rows), row(width, rows), row(rows, width)]
        + [
            full_spec(w_out.shape),
            full_spec((width,)),
            full_spec(w_gate.shape),
            full_spec(w_up.shape),
            full_spec(w_down.shape),
        ],
        out_specs=[row(*shape) for shape, _ in shapes] + [full_spec((1, width))],
        out_shape=[jax.ShapeDtypeStruct((seqs,) + shape, kind) for shape, kind in shapes]
        + [jax.ShapeDtypeStruct((1, width), f32)],
        compiler_params=params(60),
        name="feed_forward",
    )(x, cot, attn, w_out, norm, w_gate, w_up, w_down)


def ffn_place(k, t, tiles):
    if k < 2:
        return k, t
    return (0, tiles + t) if t < tiles // 2 else (1, tiles + t - tiles // 2)


def half_rows(places, width, parts):
    unit = 16 * (parts // 2)
    return -(-places * width // unit) * unit


def put(out_ref, place, width, tile):
    half, at = place
    out_ref[half, at * width : (at + 1) * width, :] = tile


def with_column(tile, column):
    free = lane_index(tile.shape[0]) >= HEAD_DIM
    return jnp.where(free, column, tile)


def ffn_grad_kernel(b_ref, cot_ref, hid_ref, d_gate_ref, d_up_ref, out_ref):
    width = b_ref.shape[1]
    hidden = hid_ref.shape[1]
    tiles = hidden // LANES
    chunk = 2 * LANES
    b_turned = b_ref[...].T
    cot_turned = jnp.concatenate([cot_ref[s] for s in range(cot_ref.shape[0])], axis=1)
    for k, (left, right) in enumerate(
        ((b_turned, d_gate_ref), (b_turned, d_up_ref), (cot_turned, hid_ref))
    ):
        for c in range(hidden // chunk):
            product = dot(left, right[:, c * chunk : (c + 1) * chunk]).astype(bf16)
            for u in range(2):
                put(
                    out_ref,
                    ffn_place(k, 2 * c + u, tiles),
                    width,
                    product[:, u * LANES : (u + 1) * LANES],
                )


def ffn_grad_call(b, cot, hid, d_gate, d_up):
    width = b.shape[1]
    tiles = hid.shape[1] // LANES
    return pl.pallas_call(
        ffn_grad_kernel,
        out_shape=jax.ShapeDtypeStruct((2, (tiles + tiles // 2) * width, LANES), bf16),
        compiler_params=params(60),
        name="ffn_grads",
    )(b, cot, hid, d_gate, d_up)


def ffn_unfold_kernel(gate_in, up_in, down_in, gate_ref, up_ref, down_ref):
    for source, target in ((gate_in, gate_ref), (up_in, up_ref), (down_in, down_ref)):
        for u in range(source.shape[1]):
            target[:, u * LANES : (u + 1) * LANES] = source[0, u].astype(f32)


def ffn_unfold_call(sums, width, hidden):
    tiles = hidden // LANES
    chunk = 2
    steps = tiles // chunk
    sums = sums.reshape(2, tiles + tiles // 2, width, LANES)
    block = (1, chunk, width, LANES)
    return pl.pallas_call(
        ffn_unfold_kernel,
        grid=(steps,),
        in_specs=[
            pl.BlockSpec(block, lambda i: (0, i, 0, 0)),
            pl.BlockSpec(block, lambda i: (1, i, 0, 0)),
            pl.BlockSpec(block, lambda i: (i // (steps // 2), steps + i % (steps // 2), 0, 0)),
        ],
        out_specs=[pl.BlockSpec((width, chunk * LANES), lambda i: (0, i))] * 3,
        out_shape=[jax.ShapeDtypeStruct((width, hidden), f32)] * 3,
        compiler_params=params(60),
        name="ffn_unfold",
    )(sums, sums, sums)


def unfold_square(products, out_ref, norm_ref):
    for t, product in enumerate(products):
        if t < len(products) - 1:
            out_ref[:, t * LANES : (t + 1) * LANES] = product
        else:
            out_ref[:, t * LANES :] = product[:, :HEAD_DIM]
            norm_ref[...] = product.T[HEAD_DIM, :]


def unfold_call(kernel, name, arrays, shapes):
    smem = pl.BlockSpec(memory_space=pltpu.SMEM)
    vmem = pl.BlockSpec(memory_space=pltpu.VMEM)
    return pl.pallas_call(
        kernel,
        in_specs=[smem if t.ndim == 1 else vmem for t in arrays],
        out_shape=[jax.ShapeDtypeStruct(shape, f32) for shape in shapes],
        compiler_params=params(48),
        name=name,
    )(*arrays)


def query_grad_kernel(
    a_ref, attn_ref, d_proj_ref, d_q_ref, g_norm_ref, w_ref, out_ref, g_ref, g_out_ref
):
    for t, tile in enumerate(head_tiles(dot(a_ref[...].T, d_q_ref[...]))):
        g_ref[t] = tile.astype(bf16)
    width = a_ref.shape[1]
    column = jnp.broadcast_to(g_norm_ref[...], (8, width)).T[:, :1]
    for t, tile in enumerate(head_tiles(dot(attn_ref[...].T, d_proj_ref[...]))):
        if t == g_out_ref.shape[0] - 1:
            tile = with_column(tile, column)
        g_out_ref[t] = tile.astype(bf16)
    out_ref[...] = dot(d_q_ref[...], w_ref[...], NT)


def query_grad_call(a, attn, d_proj, d_q, g_norm, w_query):
    rows, width = a.shape
    tiles = jax.ShapeDtypeStruct((-(-width // LANES), width, LANES), bf16)
    return pl.pallas_call(
        query_grad_kernel,
        out_shape=[jax.ShapeDtypeStruct((rows, width), f32), tiles, tiles],
        compiler_params=params(32),
        name="query_grads",
    )(a, attn, d_proj, d_q, g_norm, w_query)


def attn_place(t):
    return t % 2, t // 2


def last_kernel(
    x_ref, a_ref, norm_ref, wk_ref, wv_ref, cos_ref, sin_ref, d_kv_ref, d_aq_ref, d_mid_ref, g_q_ref,
    g_out_ref, out_ref, g_ref, d_pairs, d_norm,
):
    step = pl.program_id(0)
    x = x_ref[0].T.astype(f32)
    rows, width = x.shape
    low_half = lane_index(rows) < HEAD_DIM
    scale = lax.rsqrt(jnp.sum(x * x, axis=-1, keepdims=True) * (1.0 / width) + eps_norm)
    normed = x * scale
    parts = []
    for g in range(KV_HEADS):
        tile = d_kv_ref[0, :, g * LANES : (g + 1) * LANES].astype(f32)
        turned = tile * cos_ref[0] - swap_halves(tile) * sin_ref[0]
        parts.append(jnp.where(low_half, turned, tile))
    moved = [pltpu.roll(part, HEAD_DIM, 1) for part in parts]
    d_key = jnp.concatenate(
        [jnp.where(low_half, parts[0], moved[1]), parts[2][:, :HEAD_DIM]], axis=1
    ).astype(bf16)
    d_value = jnp.concatenate(
        [jnp.where(low_half, moved[0], parts[1]), moved[2][:, :HEAD_DIM]], axis=1
    ).astype(bf16)
    g_pairs = dot(a_ref[0], jnp.concatenate(parts, axis=1).astype(bf16), TN)
    d_a = d_aq_ref[0] + dot(d_key, wk_ref[...]) + dot(d_value, wv_ref[...])
    g_norm = jnp.sum(d_a * normed, axis=0, keepdims=True)

    @pl.when(step == 0)
    def _():
        d_norm[...] = g_norm
        d_pairs[...] = g_pairs

    @pl.when(step > 0)
    def _():
        d_norm[...] += g_norm
        d_pairs[...] += g_pairs

    e = d_a * as_row(norm_ref)
    mean = jnp.sum(e * normed, axis=-1, keepdims=True) * (1.0 / width)
    out_ref[0] = (d_mid_ref[0] + scale * (e - normed * mean)).astype(bf16).T

    @pl.when(step == pl.num_programs(0) - 1)
    def _():
        square = g_q_ref.shape[0]
        column = jnp.broadcast_to(d_norm[...], (8, width)).T[:, :1]
        for t in range(square):
            tile = g_q_ref[t]
            if t == square - 1:
                tile = with_column(tile.astype(f32), column).astype(bf16)
            put(g_ref, attn_place(t), width, tile)
        for g in range(KV_HEADS):
            put(
                g_ref,
                attn_place(square + g),
                width,
                d_pairs[:, g * LANES : (g + 1) * LANES].astype(bf16),
            )
        for t in range(square):
            put(g_ref, attn_place(square + KV_HEADS + t), width, g_out_ref[t])
        clear_rest(g_ref, 2 * square + KV_HEADS, width)


def last_call(x, a, norm, w_key, w_value, cos, sin, d_kv, d_aq, d_mid, g_query, g_out, parts):
    seqs, width, rows = x.shape
    row = lambda *shape: pl.BlockSpec((1,) + shape, lambda s: (s,) + (0,) * len(shape))
    places = -(-(2 * g_query.shape[0] + KV_HEADS) // 2)
    g_shape = (2, half_rows(places, width, parts), LANES)
    wide = KV_HEADS * LANES
    return pl.pallas_call(
        last_kernel,
        grid=(seqs,),
        in_specs=[
            row(width, rows),
            row(rows, width),
            full_spec((width,)),
            full_spec(w_key.shape),
            full_spec(w_value.shape),
            row(rows, LANES),
            row(rows, LANES),
            row(rows, wide),
            row(rows, width),
            row(rows, width),
            full_spec(g_query.shape),
            full_spec(g_out.shape),
        ],
        out_specs=[row(width, rows), full_spec(g_shape)],
        out_shape=[
            jax.ShapeDtypeStruct((seqs, width, rows), bf16),
            jax.ShapeDtypeStruct(g_shape, bf16),
        ],
        scratch_shapes=[pltpu.VMEM((width, wide), f32), pltpu.VMEM((1, width), f32)],
        compiler_params=params(32),
        name="last_part",
    )(x, a, norm, w_key, w_value, cos, sin, d_kv, d_aq, d_mid, g_query, g_out)


def attn_unfold_kernel(
    side, mine, other, query_ref, key_ref, value_ref, norm_ref, out_ref, norm_two_ref
):
    width = query_ref.shape[0]
    square = -(-width // LANES)

    def spread(halves):
        def tile(t):
            half, at = attn_place(t)
            return halves[half][at * width : (at + 1) * width, :].astype(f32)

        unfold_square([tile(t) for t in range(square)], query_ref, norm_ref)
        for g in range(KV_HEADS):
            pair = tile(square + g)
            lanes = slice(g * HEAD_DIM, (g + 1) * HEAD_DIM)
            turned = pair.T
            key_ref[lanes, :] = turned[:HEAD_DIM]
            value_ref[lanes, :] = turned[HEAD_DIM:]
        first = square + KV_HEADS
        unfold_square([tile(first + t) for t in range(square)], out_ref, norm_two_ref)

    @pl.when(side[0] == 0)
    def _():
        spread((mine, other))

    @pl.when(side[0] != 0)
    def _():
        spread((other, mine))


def device_stages(seq_count, batch_count):
    masks = [1 << k for k in range(batch_count.bit_length() - 1)]
    masks += [mask * batch_count for mask in exchange_masks(seq_count)]
    return [masks[:1]] + [masks[k : k + 2] for k in range(1, len(masks), 2)]


def stage_places(stages, index):
    bits = {}
    for mask in sorted((m for stage in stages for m in stage), reverse=True):
        bit = (index >> (mask.bit_length() - 1)) & 1
        bits[mask] = bit
        index = index ^ (bit * mask)
    return [sum(bits[mask] << k for k, mask in enumerate(stage)) for stage in stages]


def swap_with(value, mask, devices):
    return lax.ppermute(value, ("seq", "batch"), [(i, i ^ mask) for i in range(devices)])


def scatter_stage(value, stage, place, devices):
    group = 1 << len(stage)
    masks = span(stage)
    value = value.reshape((group, -1, LANES))
    pick = lambda k: lax.dynamic_index_in_dim(value, place ^ k, 0, False)
    got = [swap_with(pick(k), masks[k], devices) for k in range(1, group)]
    return sum((g.astype(f32) for g in got), pick(0).astype(f32)).astype(bf16)


def gather_stage(value, stage, place, devices):
    group = 1 << len(stage)
    masks = span(stage)
    parts = jnp.stack([value] + [swap_with(value, masks[k], devices) for k in range(1, group)])
    for k in range(len(stage)):
        shape = parts.shape
        split = parts.reshape((group >> (k + 1), 2, 1 << k) + shape[1:])
        parts = jnp.where((place >> k) & 1 == 1, split[:, ::-1], split).reshape(shape)
    return parts


def gather_order(value, order, stages, places, devices):
    done = []
    for k in order:
        value = gather_stage(value, stages[k], places[k], devices)
        done.insert(0, k)
    back = sorted(range(len(done)), key=lambda i: done[i])
    return jnp.transpose(value, back + [len(done), len(done) + 1])


def gather_sums(part, stages, places, devices, chains):
    late = list(range(1, len(stages)))[::-1]
    step = part.shape[0] // chains
    got = [
        gather_order(
            part[c * step : (c + 1) * step],
            late[c % len(late) :] + late[: c % len(late)],
            stages,
            places,
            devices,
        )
        for c in range(chains)
    ]
    half = got[0] if chains == 1 else jnp.concatenate(got, axis=-2)
    half = half.reshape(-1, LANES)
    return half, swap_with(half, stages[0][0], devices)


def exchange_masks(count):
    masks = [1 << k for k in range(count.bit_length() - 1)]
    if count == 8:
        masks[2] = 6
    return masks


def chain_order(masks, chain):
    shift = chain % len(masks)
    return masks[shift:] + masks[:shift]


def span(masks):
    ids = [0]
    for mask in masks:
        ids += [k ^ mask for k in ids]
    return ids


def gather_blocks(kv, count):
    me = lax.axis_index("seq")
    masks = exchange_masks(count)
    seqs, last = kv.shape[0], len(masks) - 1
    held = [kv[s : s + 1] for s in range(seqs)]
    rounds, numbers = [], []

    def send(s, r, value, known, is_last):
        mask = chain_order(masks, s)[r]
        pairs = [
            (i, i ^ mask)
            for i in range(count)
            if not is_last or min(i ^ k for k in known) < i ^ mask
        ]
        return lax.ppermute(value, "seq", pairs), [me ^ (mask ^ k) for k in known]

    def keep(sent):
        rounds.append([value for value, _ in sent])
        numbers.append([k for _, known in sent for k in known])

    early = []
    for r in range(last):
        known = [span(chain_order(masks, s)[:r]) for s in range(seqs)]
        if r == last - 1:
            early = [send(s, last, held[s], known[s], True) for s in range(seqs)]
        sent = [send(s, r, held[s], known[s], False) for s in range(seqs)]
        keep(sent)
        if r < last - 1:
            held = [jnp.concatenate([h, v], axis=0) for h, (v, _) in zip(held, sent)]
    keep(early)
    keep(
        [
            send(
                s,
                last,
                rounds[last - 1][s],
                [chain_order(masks, s)[last - 1] ^ k for k in known[s]],
                True,
            )
            for s in range(seqs)
        ]
    )
    return rounds, numbers


def add_low(*terms):
    return sum((t.astype(f32) for t in terms[1:]), terms[0].astype(f32)).astype(bf16)


def return_round(parts, r, count):
    masks = exchange_masks(count)
    got = []
    for s, part in enumerate(parts):
        order = chain_order(masks, s)
        mask, known = order[r], span(order[:r])
        pairs = [
            (i, i ^ mask)
            for i in range(count)
            if r < len(masks) - 1 or min(i ^ mask ^ k for k in known) < i
        ]
        got.append(lax.ppermute(part, "seq", pairs))
    return got


def beside(tile):
    rows = tile.shape[0]
    half = rows // 2
    return jnp.where(
        lane_index(half) < HEAD_DIM, tile[:half], pltpu.roll(tile[half:], HEAD_DIM, 1)
    )


def stacked(tile):
    return jnp.concatenate([tile, pltpu.roll(tile, HEAD_DIM, 1)], axis=0)


def other_half(tile):
    return pltpu.roll(tile, HEAD_DIM, 1)


def join(low, high):
    return jnp.where(lane_index(low.shape[0]) < HEAD_DIM, low, high)


def low_only(tile):
    return jnp.where(lane_index(tile.shape[0]) < HEAD_DIM, tile, 0.0)


def high_only(tile):
    return jnp.where(lane_index(tile.shape[0]) < HEAD_DIM, 0.0, tile)


def write_long(ref, at, parts, more=None):
    h0, h1, h2, key, value = parts
    rows = key.shape[0]
    ref[at, 0:rows] = join(h0, other_half(h1)).astype(bf16)
    ref[at, rows : 2 * rows] = join(h2, other_half(key)).astype(bf16)
    ref[at, 2 * rows : rows * 5 // 2] = beside(value).astype(bf16)
    if more is not None:
        ref[at, rows * 5 // 2 :] = more


def read_long(message, rows):
    first = message[0:rows].astype(f32)
    second = message[rows : 2 * rows].astype(f32)
    value = stacked(message[2 * rows : rows * 5 // 2].astype(f32))
    return (first, other_half(first), second), join(other_half(second), other_half(value))


def write_short(ref, at, heads):
    rows = heads[0].shape[0]
    ref[at, 0:rows] = join(heads[0], other_half(heads[1])).astype(bf16)
    ref[at, rows:] = beside(heads[2]).astype(bf16)


def read_short(message):
    rows = message.shape[0] * 2 // 3
    first = message[0:rows].astype(f32)
    return first, other_half(first), stacked(message[rows:].astype(f32))


def units_pre_kernel(
    count, ids, x_ref, norm_ref, wq_ref, wk_ref, wv_ref, cos_ref, sin_ref, *refs
):
    outs, (a_ref, q_ref, kv_ref, out_ref) = refs[:count], refs[count:]
    me = ids[0]
    seqs, width, rows = x_ref.shape

    def heads_of(tiles, many):
        return [tiles[h // 2] if h % 2 == 0 else other_half(tiles[h // 2]) for h in range(many)]

    for s in range(seqs):
        x = x_ref[s].T.astype(f32)
        scale = lax.rsqrt(jnp.sum(x * x, axis=-1, keepdims=True) * (1.0 / width) + eps_norm)
        a = (x * scale * as_row(norm_ref)).astype(bf16)
        a_ref[s] = a
        cos, sin = cos_ref[s], sin_ref[s]

        def turn(tile, cos=cos, sin=sin):
            return tile * cos + swap_halves(tile) * sin

        queries = heads_of([turn(t) * 0.125 for t in head_tiles(dot(a, wq_ref[...]))], HEADS)
        keys = heads_of([turn(t) for t in head_tiles(dot(a, wk_ref[...], NT))], KV_HEADS)
        values = heads_of(head_tiles(dot(a, wv_ref[...], NT)), KV_HEADS)
        for g in range(KV_HEADS):
            parts = queries[g * PER : (g + 1) * PER] + [keys[g], values[g]]
            unit = s * KV_HEADS + g
            if unit < count:
                write_long(out_ref, lax.rem(unit - me + count, count), parts)
            else:
                for h in range(PER):
                    q_ref[h * rows : (h + 1) * rows] = low_only(parts[h]).astype(bf16)
                kv_ref[0] = join(parts[3], other_half(parts[4])).astype(bf16)
    hand_out(out_ref, outs)


def hand_out(messages, outs):
    for t, out in enumerate(outs):
        out[...] = messages[t]


def units_pre_call(ids, x, norm, w_query, w_key, w_value, cos, sin, count):
    seqs, width, rows = x.shape
    vmem = pl.BlockSpec(memory_space=pltpu.VMEM)
    message = (rows * 5 // 2, LANES)
    outs = pl.pallas_call(
        functools.partial(units_pre_kernel, count),
        in_specs=[pl.BlockSpec(memory_space=pltpu.SMEM)] + [vmem] * 7,
        out_shape=[jax.ShapeDtypeStruct(message, bf16)] * count
        + [
            jax.ShapeDtypeStruct((seqs, rows, width), bf16),
            jax.ShapeDtypeStruct((PER * rows, LANES), bf16),
            jax.ShapeDtypeStruct((1, rows, LANES), bf16),
        ],
        scratch_shapes=[pltpu.VMEM((count,) + message, bf16)],
        compiler_params=params(60),
        name="project",
    )(ids, x, norm, w_query, w_key, w_value, cos, sin)
    return (outs[:count],) + tuple(outs[count:])


def attend_row(q, blocks, seen=None):
    rows = blocks[0].shape[0]
    peak = sums = None
    for first in range(0, len(blocks), UNROLL):
        part = blocks[first : first + UNROLL]
        scores = [dot(kv, q, NT) for kv in part]
        if first + len(part) == len(blocks):
            scores[-1] = jnp.where(causal_part(rows, PER), scores[-1], mask_low)
        tops = [jnp.max(sc, axis=0, keepdims=True) for sc in scores]
        flags = [None] * len(part)
        if seen is not None:
            flags = (seen + [None])[first : first + UNROLL]
            tops = [t if f is None else jnp.where(f, t, mask_low) for t, f in zip(tops, flags)]
        new_peak = functools.reduce(jnp.maximum, tops if peak is None else tops + [peak])
        shifts = [new_peak if f is None else jnp.where(f, new_peak, -mask_low) for f in flags]
        shares = [jnp.exp(sc - sh).astype(bf16).T for sc, sh in zip(scores, shifts)]
        ones = lane_index(rows) < HEAD_DIM
        values = [jnp.where(ones, jnp.ones((), bf16), kv) for kv in part]
        added = dot(jnp.concatenate(shares, axis=1), jnp.concatenate(values, axis=0))
        if peak is not None:
            fading = jnp.broadcast_to(jnp.exp(peak - new_peak), (LANES, peak.shape[1])).T
            added = sums * fading + added
        peak, sums = new_peak, added
    return peak, sums


def attend_result(peak, total):
    rows = total.shape[0] // PER
    moved = other_half(total)
    normal = moved / total
    log_total = peak + jnp.log(total.T[0:1])
    return [normal[h * rows : (h + 1) * rows] for h in range(PER)], log_total


def units_forward_kernel(count, ids, *refs):
    messages = refs[:count]
    outs, (log_ref, q_ref, kv_ref, out_ref) = refs[-4 - count : -4], refs[-4:]
    rows = kv_ref.shape[1]
    me = ids[0]
    for t in range(count):
        block = lax.rem(me - t + count, count)
        heads, kv = read_long(messages[t], rows)
        for h in range(PER):
            q_ref[block, h * rows : (h + 1) * rows] = low_only(heads[h]).astype(bf16)
        kv_ref[block] = kv.astype(bf16)
    for i in range(count):
        new_peak, sums = attend_row(q_ref[i], [kv_ref[j] for j in range(i + 1)])
        heads, log_total = attend_result(new_peak, sums)
        log_ref[i] = log_total
        write_short(out_ref, lax.rem(i - me + count, count), heads)
    hand_out(out_ref, outs)


def units_forward_call(ids, messages, after):
    count = len(messages)
    rows = messages[0].shape[0] * 2 // 5
    wide = PER * rows
    vmem = pl.BlockSpec(memory_space=pltpu.VMEM)
    message = (rows * 3 // 2, LANES)
    outs = pl.pallas_call(
        functools.partial(units_forward_kernel, count),
        in_specs=[pl.BlockSpec(memory_space=pltpu.SMEM)]
        + [vmem] * count
        + [pl.BlockSpec(memory_space=pl.ANY)] * len(after),
        out_shape=[jax.ShapeDtypeStruct(message, bf16)] * count
        + [
            jax.ShapeDtypeStruct((count, 1, wide), f32),
            jax.ShapeDtypeStruct((count, wide, LANES), bf16),
            jax.ShapeDtypeStruct((count, rows, LANES), bf16),
        ],
        scratch_shapes=[pltpu.VMEM((count,) + message, bf16)],
        compiler_params=params(48),
        name="units_forward",
    )(ids, *messages, *after)
    return (outs[:count],) + tuple(outs[count:])


def last_unit_forward_kernel(ids, q_ref, kv_ref, out_ref, log_ref):
    me = ids[0]
    count = kv_ref.shape[0]
    others = span(exchange_masks(count))[1:]
    blocks = [kv_ref[p] for p in range(1, count)] + [kv_ref[0]]
    heads, log_total = attend_result(
        *attend_row(q_ref[...], blocks, [(me ^ k) < me for k in others])
    )
    log_ref[...] = log_total
    write_short(out_ref, 0, heads)


def last_unit_forward_call(ids, q, kv):
    wide = q.shape[0]
    vmem = pl.BlockSpec(memory_space=pltpu.VMEM)
    return pl.pallas_call(
        last_unit_forward_kernel,
        in_specs=[pl.BlockSpec(memory_space=pltpu.SMEM), vmem, vmem],
        out_shape=[
            jax.ShapeDtypeStruct((1, wide // 2, LANES), bf16),
            jax.ShapeDtypeStruct((1, wide), f32),
        ],
        compiler_params=params(32),
        name="last_unit_forward",
    )(ids, q, kv)


def attend_back(q, d_out, kv, log_total, delta, diagonal):
    rows = kv.shape[0]
    scores = dot(kv, q, NT)
    probs = jnp.exp(scores - log_total)
    if diagonal:
        probs = jnp.where(causal_part(rows, PER), probs, 0.0)
    d_probs = dot(kv, d_out, NT)
    d_scores = (probs * (d_probs - delta)).astype(bf16)
    return (
        dot(probs.astype(bf16), d_out) + dot(d_scores, q),
        dot(d_scores.T, kv),
    )


def unpack_out(message, attn):
    heads, values = read_short(message), read_short(attn)
    delta = [
        jnp.sum(low_only(d * o).T, axis=0, keepdims=True) for d, o in zip(heads, values)
    ]
    d_out = jnp.concatenate([high_only(other_half(d)) for d in heads], axis=0)
    return d_out.astype(bf16), jnp.concatenate(delta, axis=1)


def last_unit_backward_kernel(
    ids, q_ref, kv_ref, d_ref, attn_ref, log_ref, d_kv_ref, d_q_ref, d_out
):
    me = ids[0]
    count = kv_ref.shape[0]
    d_value, delta = unpack_out(d_ref[...], attn_ref[...])
    d_out[...] = d_value
    log_total = log_ref[...]
    total = None
    for p, k in list(enumerate(span(exchange_masks(count))))[1:]:
        shift = jnp.where((me ^ k) < me, log_total, -mask_low)
        d_kv, d_q = attend_back(q_ref[...], d_out[...], kv_ref[p], shift, delta, False)
        d_kv_ref[me ^ k] = d_kv.astype(bf16)
        total = d_q if total is None else total + d_q
    d_kv, d_q = attend_back(q_ref[...], d_out[...], kv_ref[0], log_total, delta, True)
    d_kv_ref[me] = d_kv.astype(bf16)
    d_q_ref[...] = total + d_q


def last_unit_backward_call(ids, q, kv, d_message, attn, log_total):
    vmem = pl.BlockSpec(memory_space=pltpu.VMEM)
    return pl.pallas_call(
        last_unit_backward_kernel,
        in_specs=[pl.BlockSpec(memory_space=pltpu.SMEM)] + [vmem] * 5,
        out_shape=[
            jax.ShapeDtypeStruct(kv.shape, bf16),
            jax.ShapeDtypeStruct(q.shape, f32),
        ],
        scratch_shapes=[pltpu.VMEM(q.shape, bf16)],
        compiler_params=params(24),
        name="last_unit_backward",
    )(ids, q, kv, d_message, attn, log_total)


def units_backward_kernel(count, ids, *refs):
    messages, refs = refs[:count], refs[count:]
    attn, refs = refs[:count], refs[count:]
    q_ref, kv_ref, log_ref, last_ref = refs[:4]
    outs, (out_ref, d_out, delta, d_kv) = refs[4:-4], refs[-4:]
    rows = kv_ref.shape[1]
    me = ids[0]
    for t in range(count):
        block = lax.rem(me - t + count, count)
        value, row = unpack_out(messages[t][...], attn[(count - t) % count][...])
        d_out[block] = value
        delta[block] = row
    for i in reversed(range(count)):
        d_query = None
        for first in range(0, i + 1, 2):
            places = list(range(first, min(first + 2, i + 1)))
            blocks = [kv_ref[j] for j in places]
            probs, d_scores = [], []
            for j, kv in zip(places, blocks):
                prob = jnp.exp(dot(kv, q_ref[i], NT) - log_ref[i])
                if j == i:
                    prob = jnp.where(causal_part(rows, PER), prob, 0.0)
                d_prob = dot(kv, d_out[i], NT)
                d_scores.append((prob * (d_prob - delta[i])).astype(bf16))
                probs.append(prob.astype(bf16))
            for j, prob, d_score in zip(places, probs, d_scores):
                term = dot(prob, d_out[i]) + dot(d_score, q_ref[i])
                d_kv[j] = term if i == count - 1 else d_kv[j] + term
            term = dot(jnp.concatenate([d.T for d in d_scores], axis=1), jnp.concatenate(blocks, axis=0))
            d_query = term if d_query is None else d_query + term
        tile = d_kv[i]
        write_long(
            out_ref,
            lax.rem(i - me + count, count),
            [d_query[h * rows : (h + 1) * rows] for h in range(PER)] + [tile, other_half(tile)],
            last_ref[i],
        )
    hand_out(out_ref, outs)


def units_backward_call(ids, messages, q, kv, attn, log_total, last_d_kv):
    count, rows, _ = kv.shape
    wide = PER * rows
    vmem = pl.BlockSpec(memory_space=pltpu.VMEM)
    message = (rows * 7 // 2, LANES)
    return pl.pallas_call(
        functools.partial(units_backward_kernel, count),
        in_specs=[pl.BlockSpec(memory_space=pltpu.SMEM)] + [vmem] * (2 * count + 4),
        out_shape=[jax.ShapeDtypeStruct(message, bf16)] * count,
        scratch_shapes=[
            pltpu.VMEM((count,) + message, bf16),
            pltpu.VMEM((count, wide, LANES), bf16),
            pltpu.VMEM((count, 1, wide), f32),
            pltpu.VMEM((count, rows, LANES), f32),
        ],
        compiler_params=params(56),
        name="units_backward",
    )(ids, *messages, *attn, q, kv, log_total, last_d_kv)


def units_ffn_kernel(
    count,
    ids,
    x_ref,
    cot_ref,
    norm_ref,
    w_out_ref,
    w_gate_hbm,
    w_up_hbm,
    w_down_hbm,
    *refs,
):
    messages, last_message = refs[:count], refs[count]
    (
        mid_hbm, attn_hbm, hid_hbm, d_gate_hbm, d_up_hbm, g_hbm,
        units, w_gate, w_up, w_down, mid, attn, cot, b, hid, d_gate, d_up, g_buf, w_sems, out_sems,
    ) = refs[count + 1 :]
    me = ids[0]
    seqs, width, rows = x_ref.shape
    hidden = w_gate.shape[1]
    tiles = hidden // LANES
    loads = [
        pltpu.make_async_copy(source, target, w_sems.at[k])
        for k, (source, target) in enumerate(
            ((w_gate_hbm, w_gate), (w_up_hbm, w_up), (w_down_hbm, w_down))
        )
    ]
    for load in loads:
        load.start()
    stores = []

    def store(source, target):
        copy = pltpu.make_async_copy(source, target, out_sems.at[len(stores)])
        copy.start()
        stores.append(copy)

    for t in range(count):
        units[lax.rem(me - t + count, count)] = messages[t][...]
    units[count] = last_message[0]
    for s in range(seqs):
        here = slice(s * rows, (s + 1) * rows)
        heads = []
        for g in range(KV_HEADS):
            heads += read_short(units[s * KV_HEADS + g])
        parts = [join(heads[h], other_half(heads[h + 1])) for h in range(0, HEADS - 1, 2)]
        attn_rows = jnp.concatenate(parts + [heads[HEADS - 1][:, :HEAD_DIM]], axis=1).astype(bf16)
        attn[s] = attn_rows
        cot[here] = cot_ref[s].T
        mid_rows = x_ref[s].T.astype(f32) + dot(attn_rows, w_out_ref[...])
        scale = lax.rsqrt(
            jnp.sum(mid_rows * mid_rows, axis=-1, keepdims=True) * (1.0 / width) + eps_norm
        )
        mid[s] = mid_rows
        b[here] = (mid_rows * scale * as_row(norm_ref)).astype(bf16)
    store(mid, mid_hbm)
    store(attn, attn_hbm)
    b_turned = b[...].T
    cot_turned = jnp.concatenate([cot_ref[s] for s in range(seqs)], axis=1)
    for load in loads:
        load.wait()
    chunk = 2 * LANES

    def gradient(k, c, left, right):
        product = dot(left, right[:, c * chunk : (c + 1) * chunk]).astype(bf16)
        for u in range(2):
            half, at = ffn_place(k, 2 * c + u, tiles)
            here = pl.ds(at * width, width)
            g_buf[half, here, :] = product[:, u * LANES : (u + 1) * LANES]
            store(g_buf.at[half, here], g_hbm.at[half, here])

    for c in range(hidden // chunk):
        lanes = pl.ds(c * chunk, chunk)
        gate = dot(b[...], w_gate[:, lanes])
        up = dot(b[...], w_up[:, lanes])
        d_hid = dot(cot[...], w_down[:, lanes])
        sig = 1.0 / (1.0 + jnp.exp(-gate))
        active = gate * sig
        hid[:, lanes] = (active * up).astype(bf16)
        d_gate[:, lanes] = (d_hid * up * sig * (1.0 + gate * (1.0 - sig))).astype(bf16)
        d_up[:, lanes] = (d_hid * active).astype(bf16)
    for source, target in ((d_gate, d_gate_hbm), (d_up, d_up_hbm), (hid, hid_hbm)):
        store(source, target)
    for k, (left, right) in enumerate(((b_turned, d_gate), (b_turned, d_up), (cot_turned, hid))):
        for c in range(hidden // chunk):
            gradient(k, c, left, right)
    for copy in stores:
        copy.wait()


def units_ffn_call(ids, x, cot, messages, last_message, w_out, norm, w_gate, w_up, w_down):
    seqs, width, rows = x.shape
    hidden = w_gate.shape[1]
    count = len(messages)
    tokens = seqs * rows
    short = (rows * 3 // 2, LANES)
    tiles = hidden // LANES
    g_shape = (2, (tiles + tiles // 2) * width, LANES)
    vmem = pl.BlockSpec(memory_space=pltpu.VMEM)
    hbm = pl.BlockSpec(memory_space=pl.ANY)
    wide = (tokens, hidden)
    return pl.pallas_call(
        functools.partial(units_ffn_kernel, count),
        in_specs=[pl.BlockSpec(memory_space=pltpu.SMEM)]
        + [vmem] * 4
        + [hbm] * 3
        + [vmem] * (count + 1),
        out_specs=[hbm] * 6,
        out_shape=[
            jax.ShapeDtypeStruct((seqs, rows, width), f32),
            jax.ShapeDtypeStruct((seqs, rows, width), bf16),
            jax.ShapeDtypeStruct(wide, bf16),
            jax.ShapeDtypeStruct(wide, bf16),
            jax.ShapeDtypeStruct(wide, bf16),
            jax.ShapeDtypeStruct(g_shape, bf16),
        ],
        scratch_shapes=[
            pltpu.VMEM((count + 1,) + short, bf16),
            pltpu.VMEM(w_gate.shape, bf16),
            pltpu.VMEM(w_up.shape, bf16),
            pltpu.VMEM(w_down.shape, bf16),
            pltpu.VMEM((seqs, rows, width), f32),
            pltpu.VMEM((seqs, rows, width), bf16),
            pltpu.VMEM((tokens, width), bf16),
            pltpu.VMEM((tokens, width), bf16),
            pltpu.VMEM(wide, bf16),
            pltpu.VMEM(wide, bf16),
            pltpu.VMEM(wide, bf16),
            pltpu.VMEM(g_shape, bf16),
            pltpu.SemaphoreType.DMA((3,)),
            pltpu.SemaphoreType.DMA((5 + 3 * tiles,)),
        ],
        compiler_params=params(60),
        name="feed_forward",
    )(ids, x, cot, norm, w_out, w_gate, w_up, w_down, *messages, last_message)


def units_back_kernel(
    count,
    ids,
    mid_ref,
    cot_ref,
    d_gate_ref,
    d_up_ref,
    norm_ref,
    w_out_ref,
    w_gate_ref,
    w_up_ref,
    d_mid_ref,
    d_last_ref,
    g_norm_ref,
    *refs,
):
    outs, d_out_ref = refs[:count], refs[count]
    step = pl.program_id(0)
    me = ids[0]
    mid = mid_ref[0]
    rows, width = mid.shape
    cot = cot_ref[0].T
    scale = lax.rsqrt(jnp.sum(mid * mid, axis=-1, keepdims=True) * (1.0 / width) + eps_norm)
    normed = mid * scale
    d_b = dot(d_gate_ref[...], w_gate_ref[...], NT) + dot(d_up_ref[...], w_up_ref[...], NT)
    norm_term = jnp.sum(d_b * normed, axis=0, keepdims=True)
    e = d_b * as_row(norm_ref)
    mean = jnp.sum(e * normed, axis=-1, keepdims=True) * (1.0 / width)
    d_mid = cot.astype(f32) + scale * (e - normed * mean)
    d_mid_ref[0] = d_mid
    d_proj = d_mid.astype(bf16)
    d_tiles = head_tiles(dot(d_proj, w_out_ref[...], NT))
    d_heads = [
        d_tiles[h // 2] if h % 2 == 0 else other_half(d_tiles[h // 2]) for h in range(HEADS)
    ]
    for g in range(KV_HEADS):
        unit = step * KV_HEADS + g

        @pl.when(unit < count)
        def _(g=g, unit=unit):
            at = lax.rem(unit - me + count, count)
            write_short(d_out_ref, at, d_heads[g * PER : (g + 1) * PER])

        @pl.when(unit == count)
        def _(g=g):
            write_short(d_last_ref, 0, d_heads[g * PER : (g + 1) * PER])

    @pl.when(step == 0)
    def _():
        g_norm_ref[...] = norm_term

    @pl.when(step > 0)
    def _():
        g_norm_ref[...] += norm_term

    @pl.when(step == pl.num_programs(0) - 1)
    def _():
        hand_out(d_out_ref, outs)


def units_back_call(ids, mid, cot, d_gate, d_up, norm, w_out, w_gate, w_up, count):
    seqs, rows, width = mid.shape
    hidden = w_gate.shape[1]
    row = lambda *shape: pl.BlockSpec((1,) + shape, lambda s, *_: (s,) + (0,) * len(shape))
    part = pl.BlockSpec((rows, hidden), lambda s, *_: (s, 0))
    short = (rows * 3 // 2, LANES)
    outs = pl.pallas_call(
        functools.partial(units_back_kernel, count),
        grid_spec=pltpu.PrefetchScalarGridSpec(
            num_scalar_prefetch=1,
            grid=(seqs,),
            in_specs=[row(rows, width), row(width, rows), part, part, full_spec((width,))]
            + [full_spec(w_out.shape), full_spec(w_gate.shape), full_spec(w_up.shape)],
            out_specs=[
                row(rows, width),
                full_spec((1,) + short),
                full_spec((1, width)),
            ]
            + [full_spec(short)] * count,
            scratch_shapes=[pltpu.VMEM((count,) + short, bf16)],
        ),
        out_shape=[
            jax.ShapeDtypeStruct((seqs, rows, width), f32),
            jax.ShapeDtypeStruct((1,) + short, bf16),
            jax.ShapeDtypeStruct((1, width), f32),
        ]
        + [jax.ShapeDtypeStruct(short, bf16)] * count,
        compiler_params=params(60),
        name="feed_back",
    )(ids, mid, cot, d_gate, d_up, norm, w_out, w_gate, w_up)
    return (outs[3:],) + tuple(outs[:3])


def units_out_kernel(
    mid_ref, attn_ref, hid_ref, d_mid_ref, g_norm_ref, w_down_ref, out_ref, g_ref, g_out
):
    step = pl.program_id(0)
    out_ref[0] = (mid_ref[0] + dot(hid_ref[...], w_down_ref[...], NT)).astype(bf16).T
    term = dot(attn_ref[0].T, d_mid_ref[0].astype(bf16))

    @pl.when(step == 0)
    def _():
        g_out[...] = term

    @pl.when(step > 0)
    def _():
        g_out[...] += term

    @pl.when(step == pl.num_programs(0) - 1)
    def _():
        column = jnp.broadcast_to(g_norm_ref[...], (8, g_norm_ref.shape[1])).T[:, :1]
        for t, tile in enumerate(head_tiles(g_out[...])):
            if t == g_ref.shape[0] - 1:
                tile = with_column(tile, column)
            g_ref[t] = tile.astype(bf16)


def units_out_call(mid, attn, hid, d_mid, g_norm, w_down):
    seqs, rows, width = mid.shape
    hidden = w_down.shape[1]
    row = lambda *shape: pl.BlockSpec((1,) + shape, lambda s: (s,) + (0,) * len(shape))
    g_shape = (-(-width // LANES), width, LANES)
    return pl.pallas_call(
        units_out_kernel,
        grid=(seqs,),
        in_specs=[
            row(rows, width),
            row(rows, width),
            pl.BlockSpec((rows, hidden), lambda s: (s, 0)),
            row(rows, width),
            full_spec((1, width)),
            full_spec(w_down.shape),
        ],
        out_specs=[row(width, rows), full_spec(g_shape)],
        out_shape=[
            jax.ShapeDtypeStruct((seqs, width, rows), bf16),
            jax.ShapeDtypeStruct(g_shape, bf16),
        ],
        scratch_shapes=[pltpu.VMEM((width, width), f32)],
        compiler_params=params(60),
        name="feed_out",
    )(mid, attn, hid, d_mid, g_norm, w_down)


def units_last_kernel(
    count, ids, x_ref, a_ref, norm_ref, wq_ref, wk_ref, wv_ref, cos_ref, sin_ref, d_mid_ref, last_q_ref,
    g_out_ref, *refs,
):
    messages = refs[:count]
    out_ref, g_ref, units = refs[count:]
    me = ids[0]
    seqs, width, rows = x_ref.shape
    for t in range(count):
        units[lax.rem(me - t + count, count)] = messages[t][: rows * 5 // 2]
    last_kv = sum(messages[t][rows * 5 // 2 :].astype(f32) for t in range(count))
    heads = [last_q_ref[h * rows : (h + 1) * rows] for h in range(PER)]
    write_long(units, count, heads + [last_kv, other_half(last_kv)])

    def flat(tiles):
        return jnp.concatenate(tiles[:-1] + [tiles[-1][:, :HEAD_DIM]], axis=1).astype(bf16)

    d_queries, d_pairs = [], []
    g_norm = None
    for s in range(seqs):
        cos, sin = cos_ref[s], sin_ref[s]

        def turn(tile, cos=cos, sin=sin):
            return tile * cos - swap_halves(tile) * sin

        def in_tiles(parts):
            return [
                join(parts[h], other_half(parts[h + 1])) for h in range(0, len(parts) - 1, 2)
            ] + [parts[-1]]

        heads, keys, values = [], [], []
        for g in range(KV_HEADS):
            parts, kv = read_long(units[s * KV_HEADS + g], rows)
            heads += parts
            keys.append(kv)
            values.append(other_half(kv))
        d_query = flat([turn(t) * 0.125 for t in in_tiles(heads)])
        key_tiles = [turn(t) for t in in_tiles(keys)]
        d_key, d_value = flat(key_tiles), flat(in_tiles(values))
        turned = [
            key_tiles[g // 2] if g % 2 == 0 else other_half(key_tiles[g // 2])
            for g in range(KV_HEADS)
        ]
        pairs = [join(turned[g], other_half(values[g])) for g in range(KV_HEADS)]
        d_queries.append(d_query)
        d_pairs.append(jnp.concatenate(pairs, axis=1).astype(bf16))
        d_a = (
            dot(d_query, wq_ref[...], NT) + dot(d_key, wk_ref[...]) + dot(d_value, wv_ref[...])
        )
        x = x_ref[s].T.astype(f32)
        scale = lax.rsqrt(jnp.sum(x * x, axis=-1, keepdims=True) * (1.0 / width) + eps_norm)
        normed = x * scale
        term = jnp.sum(d_a * normed, axis=0, keepdims=True)
        g_norm = term if g_norm is None else g_norm + term
        e = d_a * as_row(norm_ref)
        mean = jnp.sum(e * normed, axis=-1, keepdims=True) * (1.0 / width)
        out_ref[s] = (d_mid_ref[s] + scale * (e - normed * mean)).astype(bf16).T
    a_turned = jnp.concatenate([a_ref[s].T for s in range(seqs)], axis=1)
    g_query = dot(a_turned, jnp.concatenate(d_queries, axis=0))
    g_pairs = dot(a_turned, jnp.concatenate(d_pairs, axis=0))
    square = -(-width // LANES)
    column = jnp.broadcast_to(g_norm, (8, width)).T[:, :1]
    for t, tile in enumerate(head_tiles(g_query)):
        if t == square - 1:
            tile = with_column(tile, column)
        put(g_ref, attn_place(t), width, tile.astype(bf16))
    for g in range(KV_HEADS):
        tile = g_pairs[:, g * LANES : (g + 1) * LANES]
        put(g_ref, attn_place(square + g), width, tile.astype(bf16))
    for t in range(square):
        put(g_ref, attn_place(square + KV_HEADS + t), width, g_out_ref[t])
    clear_rest(g_ref, 2 * square + KV_HEADS, width)


def clear_rest(g_ref, places, width):
    for half in range(2):
        used = (places + 1 - half) // 2 * width
        left_over = g_ref.shape[1] - used
        if left_over:
            g_ref[half, used:, :] = jnp.zeros((left_over, LANES), bf16)


def units_last_call(
    ids, x, a, norm, w_query, w_key, w_value, cos, sin, d_mid, last_d_q, g_out, messages, parts
):
    seqs, width, rows = x.shape
    count = len(messages)
    vmem = pl.BlockSpec(memory_space=pltpu.VMEM)
    places = -(-(2 * -(-width // LANES) + KV_HEADS) // 2)
    return pl.pallas_call(
        functools.partial(units_last_kernel, count),
        in_specs=[pl.BlockSpec(memory_space=pltpu.SMEM)] + [vmem] * (11 + count),
        out_shape=[
            jax.ShapeDtypeStruct((seqs, width, rows), bf16),
            jax.ShapeDtypeStruct((2, half_rows(places, width, parts), LANES), bf16),
        ],
        scratch_shapes=[pltpu.VMEM((count + 1, rows * 5 // 2, LANES), bf16)],
        compiler_params=params(60),
        name="last_part",
    )(ids, x, a, norm, w_query, w_key, w_value, cos, sin, d_mid, last_d_q, g_out, *messages)


def to_all(messages):
    count = len(messages)
    return [messages[0]] + [
        lax.ppermute(messages[t], "seq", [(i, (i + t) % count) for i in range(count)])
        for t in range(1, count)
    ]


def rope_tables(positions):
    half = HEAD_DIM // 2
    lane = jnp.arange(LANES, dtype=jnp.int32)
    frequency = jnp.exp((lane % half).astype(f32) * (-math.log(10000.0) / half))
    angles = positions.T.astype(f32)[..., None] * frequency
    return jnp.cos(angles), jnp.where(lane % HEAD_DIM < half, -1.0, 1.0) * jnp.sin(angles)


def spread_layer(
    x, cot, cos, sin, norm_one, norm_two, w_query, wk_turned, wv_turned, w_out, w_gate, w_up,
    w_down_turned, count, devices, sum_over, places_ok,
):
    seqs, width, rows = x.shape
    me = lax.axis_index("seq")
    a, q, kv = pre_call(x, norm_one, w_query, wk_turned, wv_turned, cos, sin)
    rounds, numbers = gather_blocks(kv, count)
    last = len(rounds) - 2

    def ids_of(picked):
        return jnp.stack([me] + [k for part in picked for k in part]).astype(jnp.int32)

    state = forward_call(ids_of(numbers[:last]), q, kv, rounds[:last], None, False)
    far, far_ids = rounds[last:], ids_of(numbers[last:])
    attn, log_total = forward_call(far_ids, q, None, far, state, True)
    (block_out, b, hid, d_gate, d_up, d_mid, d_proj, d_out, delta, g_norm_mlp) = middle_call(
        x, cot, attn, w_out, norm_two, w_gate, w_up, w_down_turned
    )
    flat = lambda t: t.reshape(seqs * rows, t.shape[-1])
    g_ffn = ffn_grad_call(flat(b), cot, flat(hid), flat(d_gate), flat(d_up))
    g_ffn = lax.psum(g_ffn, ("seq", "batch"))
    common = (q, d_out, log_total, delta)
    _, far_terms, d_query = backward_call(far_ids, *common, None, far, None, None)
    far_terms = [jnp.concatenate([t, u], axis=0) for t, u in zip(*far_terms)]
    got = [return_round(far_terms, last, count)]
    _, mid_terms, d_query = backward_call(
        ids_of(numbers[last - 1 : last]), *common, None, rounds[last - 1 : last], d_query, None
    )
    half = far_terms[0].shape[0] // 2
    mid_terms = [add_low(t, g[half:]) for t, g in zip(mid_terms[0], got[0])]
    got.append(return_round(mid_terms, last - 1, count))
    own_terms, near_terms, d_q = backward_call(
        ids_of(numbers[: last - 1]), *common, kv, rounds[: last - 1], d_query, (cos, sin),
        tuple(mid_terms),
    )
    for r in reversed(range(last - 1)):
        size = 1 << r
        terms = [
            add_low(t, *(g[s][size : 2 * size] for g in got)) for s, t in enumerate(near_terms[r])
        ]
        got.append(return_round(terms, r, count))
    d_kv = jnp.concatenate(
        [add_low(own_terms[s : s + 1], *(g[s][:1] for g in got)) for s in range(seqs)], axis=0
    )
    d_aq, g_query, g_out = query_grad_call(
        flat(a), flat(attn), flat(d_proj), flat(d_q), g_norm_mlp, w_query
    )
    d_tokens, g_attn = last_call(
        x, a, norm_one, wk_turned, wv_turned, cos, sin, d_kv,
        d_aq.reshape(seqs, rows, width), d_mid, g_query, g_out, devices,
    )
    return block_out, d_tokens, g_ffn, sum_over(g_attn)


def units_layer(
    x, cot, cos, sin, norm_one, norm_two, w_query, wk_turned, wv_turned, w_out, w_gate, w_up,
    w_down_turned, count, devices, sum_over, places_ok,
):
    seqs, width, rows = x.shape
    flat = lambda t: t.reshape(seqs * rows, t.shape[-1])
    ids = lax.axis_index("seq").astype(jnp.int32).reshape(1)
    messages, a, last_q, last_kv = units_pre_call(
        ids, x, norm_one, w_query, wk_turned, wv_turned, cos, sin, count
    )
    masks = exchange_masks(count)
    swap = lambda part, mask: lax.ppermute(part, "seq", [(i, i ^ mask) for i in range(count)])
    last_kv = jnp.concatenate([last_kv, swap(last_kv, masks[0])], axis=0)
    arrived, last_kv = lax.optimization_barrier((to_all(messages), last_kv))
    first, *later = masks[1:]
    last_kv = jnp.concatenate([last_kv, swap(last_kv, first)], axis=0)
    attn_out, log_total, q, kv = units_forward_call(ids, arrived, ())
    for mask in later:
        last_kv = jnp.concatenate([last_kv, swap(last_kv, mask)], axis=0)
    last_attn, last_log = last_unit_forward_call(ids, last_q, last_kv)
    mid, attn, hid, d_gate, d_up, g_ffn = units_ffn_call(
        ids, x, cot, to_all(attn_out), last_attn, w_out, norm_two, w_gate, w_up, w_down_turned
    )
    g_ffn = lax.psum(g_ffn, ("seq", "batch"))

    def backward(mid, attn, hid, d_gate, d_up, q, kv, attn_out, log_total, last_attn, last_log, a):
        d_messages, d_mid, d_last, g_norm_mlp = units_back_call(
            ids, mid, cot, d_gate, d_up, norm_two, w_out, w_gate, w_up, count
        )
        block_out, g_out = units_out_call(mid, attn, hid, d_mid, g_norm_mlp, w_down_turned)
        last_d_kv, last_d_q = last_unit_backward_call(
            ids, last_q, last_kv, d_last[0], last_attn[0], last_log
        )
        d_all = units_backward_call(
            ids, to_all(d_messages), q, kv, attn_out, log_total, last_d_kv
        )
        d_tokens, g_attn = units_last_call(
            ids, x, a, norm_one, w_query, wk_turned, wv_turned, cos, sin, d_mid, last_d_q, g_out,
            to_all(d_all), devices,
        )
        return (block_out, d_tokens) + sum_over(g_attn)

    block_out, d_tokens, *attn_sums = in_one_piece(
        places_ok,
        backward,
        (mid, attn, hid, d_gate, d_up, q, kv, attn_out, log_total, last_attn, last_log, a),
    )
    return block_out, d_tokens, g_ffn, attn_sums


def in_one_piece(always, part, operands):
    shapes = jax.eval_shape(part, *operands)

    def never(*_):
        return jax.tree.map(lambda t: jnp.zeros(t.shape, t.dtype), shapes)

    return lax.cond(always, part, never, *operands)


def on_device(
    tokens,
    positions,
    norm_attn,
    w_query,
    w_key,
    w_value,
    w_out,
    norm_mlp,
    w_gate,
    w_up,
    w_down,
    cotangent,
):
    rows, seqs, width = tokens.shape
    hidden = w_gate.shape[1]
    kv_width = KV_HEADS * HEAD_DIM
    count, batches = lax.axis_size("seq"), lax.axis_size("batch")
    me = lax.axis_index("seq")
    devices = count * batches
    stages = device_stages(count, batches)
    places = stage_places(stages, me * batches + lax.axis_index("batch"))
    x = jnp.transpose(tokens, (1, 2, 0))
    cot = jnp.transpose(cotangent, (1, 2, 0))
    wk_turned, wv_turned, w_down_turned = w_key.T, w_value.T, w_down.T
    cos, sin = rope_tables(positions)
    norm_one, norm_two = norm_attn, norm_mlp
    def sum_over(value):
        for stage, place in zip(stages, places):
            value = scatter_stage(value, stage, place, devices)
        return gather_sums(value, stages, places, devices, 1)

    layer = units_layer if count == seqs * KV_HEADS - 1 else spread_layer
    block_out, d_tokens, g_ffn, attn_sums = layer(
        x, cot, cos, sin, norm_one, norm_two, w_query, wk_turned, wv_turned, w_out, w_gate, w_up,
        w_down_turned, count, devices, sum_over, positions[0, 0] >= 0,
    )
    side = places[0].reshape(1).astype(jnp.int32)
    g_gate, g_up, g_down = ffn_unfold_call(g_ffn, width, hidden)
    g_query, g_key, g_value, g_norm_attn, g_out, g_norm_mlp = unfold_call(
        attn_unfold_kernel,
        "attn_unfold",
        (side, *attn_sums),
        [(width, width), (kv_width, width), (kv_width, width), (width,)]
        + [(width, width), (width,)],
    )
    return (
        jnp.transpose(block_out, (2, 0, 1)),
        jnp.transpose(d_tokens, (2, 0, 1)),
        g_norm_attn,
        g_query,
        g_key.T,
        g_value.T,
        g_out,
        g_norm_mlp,
        g_gate,
        g_up,
        g_down.T,
    )


def solution(mesh):
    split = P("seq", "batch", None)
    return jax.shard_map(
        on_device,
        mesh=mesh,
        in_specs=(split, P("seq", "batch")) + (P(),) * 9 + (split,),
        out_specs=(split, split) + (P(),) * 9,
        check_vma=False,
    )
```

```python
import functools
import math

import jax
import jax.numpy as jnp
from jax import lax
from jax.experimental import pallas as pl
from jax.experimental.pallas import tpu as pltpu
from jax.sharding import PartitionSpec as P

HEADS = 9
KV_HEADS = 3
HEAD_DIM = 64
PER = HEADS // KV_HEADS
LANES = 128

eps_norm = 1e-05
mask_low = -1e30
f32 = jnp.float32
bf16 = jnp.bfloat16

NN = (((1,), (0,)), ((), ()))
NT = (((1,), (1,)), ((), ()))
TN = (((0,), (0,)), ((), ()))
UNROLL = 4


def dot(left, right, dims=NN):
    return lax.dot_general(left, right, dims, preferred_element_type=f32)


def params(mib):
    return pltpu.CompilerParams(vmem_limit_bytes=mib * 1024 * 1024)


def as_row(ref):
    return ref[...].reshape(1, ref.shape[0])


def full_spec(shape):
    zeros = (0,) * len(shape)
    return pl.BlockSpec(shape, lambda *_: zeros)


def lane_index(rows):
    return lax.broadcasted_iota(jnp.int32, (rows, LANES), 1)


def swap_halves(tile):
    half = HEAD_DIM // 2
    lane = lane_index(tile.shape[0])
    return jnp.where(
        lane % HEAD_DIM < half, pltpu.roll(tile, LANES - half, 1), pltpu.roll(tile, half, 1)
    )


def head_tiles(lin):
    rows, width = lin.shape
    if width % LANES:
        lin = jnp.concatenate([lin, jnp.zeros((rows, HEAD_DIM), lin.dtype)], axis=1)
    return [lin[:, at : at + LANES] for at in range(0, lin.shape[1], LANES)]


def pre_kernel(
    x_ref, norm_ref, wq_ref, wk_ref, wv_ref, cos_ref, sin_ref, a_ref, q_ref, kv_ref
):
    x = x_ref[0].T.astype(f32)
    rows, width = x.shape
    scale = lax.rsqrt(jnp.sum(x * x, axis=-1, keepdims=True) * (1.0 / width) + eps_norm)
    a = (x * scale * as_row(norm_ref)).astype(bf16)
    a_ref[0] = a
    cos, sin = cos_ref[0], sin_ref[0]
    low_half = lane_index(rows) < HEAD_DIM

    def turn(tile):
        return tile * cos + swap_halves(tile) * sin

    keys = [turn(tile) for tile in head_tiles(dot(a, wk_ref[...], NT))]
    values = head_tiles(dot(a, wv_ref[...], NT))
    for g in range(KV_HEADS):
        key, value = keys[g // 2], values[g // 2]
        if g % 2 == 0:
            value = pltpu.roll(value, HEAD_DIM, 1)
        else:
            key = pltpu.roll(key, HEAD_DIM, 1)
        kv_ref[0, :, g * LANES : (g + 1) * LANES] = jnp.where(low_half, key, value).astype(bf16)
    queries = [turn(tile) * 0.125 for tile in head_tiles(dot(a, wq_ref[...]))]
    for head in range(HEADS):
        tile = queries[head // 2]
        if head % 2:
            tile = pltpu.roll(tile, HEAD_DIM, 1)
        group, place = divmod(head, PER)
        q_ref[0, group, place * rows : (place + 1) * rows, :] = jnp.where(
            low_half, tile, 0.0
        ).astype(bf16)


def pre_call(x, norm, w_query, w_key, w_value, cos, sin):
    seqs, width, rows = x.shape
    row = lambda shape: pl.BlockSpec((1,) + shape, lambda s: (s,) + (0,) * len(shape))
    return pl.pallas_call(
        pre_kernel,
        grid=(seqs,),
        in_specs=[
            row((width, rows)),
            full_spec((width,)),
            full_spec(w_query.shape),
            full_spec(w_key.shape),
            full_spec(w_value.shape),
            row((rows, LANES)),
            row((rows, LANES)),
        ],
        out_specs=[
            row((rows, width)),
            row((KV_HEADS, PER * rows, LANES)),
            row((rows, KV_HEADS * LANES)),
        ],
        out_shape=[
            jax.ShapeDtypeStruct((seqs, rows, width), bf16),
            jax.ShapeDtypeStruct((seqs, KV_HEADS, PER * rows, LANES), bf16),
            jax.ShapeDtypeStruct((seqs, rows, KV_HEADS * LANES), bf16),
        ],
        compiler_params=params(16),
        name="project",
    )(x, norm, w_query, w_key, w_value, cos, sin)


def causal_part(rows, heads):
    key = lax.broadcasted_iota(jnp.int32, (rows, rows), 0)
    query = lax.broadcasted_iota(jnp.int32, (rows, rows), 1)
    return jnp.concatenate([key <= query] * heads, axis=1)


def for_blocks(ids, me, seqs, own, pieces, counts, work, zeros=None):
    if own is not None:
        for s in range(seqs):
            work(s, own[s], None, (-1, s, s))
    first = 1
    for k, (parts, count) in enumerate(zip(pieces, counts)):
        least = ids[first]
        for n in range(1, seqs * count):
            least = jnp.minimum(least, ids[first + n])
        unroll = min(count, UNROLL)

        @pl.when(least < me)
        def _(parts=parts, first=first, count=count, k=k):
            def some(c, _):
                for s in range(seqs):
                    for u in range(unroll):
                        j = c * unroll + u
                        work(s, parts[s][j], ids[first + s * count + j] < me, (k, s, j))
                return 0

            if count == unroll:
                some(0, 0)
            else:
                lax.fori_loop(0, count // unroll, some, 0)

        if zeros is not None:

            @pl.when(least >= me)
            def _(k=k):
                zeros(k)

        first += seqs * count


def forward_kernel(counts, has_own, has_state, is_last, ids, *refs):
    refs = list(refs)
    q = refs.pop(0)
    seqs, rows = q.shape[0], q.shape[2] // PER
    own = refs.pop(0) if has_own else None
    pieces = [[refs.pop(0) for _ in range(seqs)] for _ in counts]
    if has_state:
        peak_in, total_in = refs.pop(0), refs.pop(0)
    outs, (peak, total) = refs[:-2], refs[-2:]
    me = ids[0]
    if has_state:
        peak[...] = peak_in[:, 0]
        total[...] = total_in[:, 0]
    low_half = lane_index(rows) < HEAD_DIM

    def attend(s, kv, seen):
        ones_values = jnp.where(low_half, jnp.ones((), bf16), kv)
        scores = dot(kv, q[s, 0], NT)
        if seen is None:
            scores = jnp.where(causal_part(rows, PER), scores, mask_low)
            new_peak = shift = jnp.max(scores, axis=0, keepdims=True)
        else:
            old_peak = peak[s]
            top = jnp.max(scores, axis=0, keepdims=True)
            new_peak = jnp.where(seen, jnp.maximum(old_peak, top), old_peak)
            shift = jnp.where(seen, new_peak, -mask_low)
        shares = jnp.exp(scores - shift).astype(bf16)
        added = dot(shares.T, ones_values)
        if seen is None:
            total[s] = added
        else:
            total[s] = total[s] * jnp.exp(old_peak - new_peak).T + added
        peak[s] = new_peak

    for_blocks(ids, me, seqs, own, pieces, counts, lambda s, kv, seen, store: attend(s, kv, seen))
    if is_last:
        attn, log_total = outs
        group = pl.program_id(0)
        for s in range(seqs):
            acc = total[s]
            normal = acc / pltpu.roll(acc, HEAD_DIM, 1)
            sums = acc.T[0:1]
            log_total[s, 0] = peak[s] + jnp.log(sums)
            values = normal[:, HEAD_DIM:].astype(bf16)
            for g in range(KV_HEADS):

                @pl.when(group == g)
                def _(values=values, s=s, g=g):
                    for h in range(PER):
                        at = (g * PER + h) * HEAD_DIM
                        attn[s, :, at : at + HEAD_DIM] = values[h * rows : (h + 1) * rows]

    else:
        outs[0][:, 0] = peak[...]
        outs[1][:, 0] = total[...]


def piece_spec(count, rows):
    return pl.BlockSpec((count, rows, LANES), lambda g, *_: (0, 0, g))


def group_spec(seqs, *shape):
    zeros = (0,) * len(shape)
    return pl.BlockSpec((seqs, 1) + shape, lambda g, *_: (0, g) + zeros)


def forward_call(ids, q, own, pieces, state, is_last):
    seqs, groups, wide, _ = q.shape
    rows = wide // PER
    counts = [parts[0].shape[0] for parts in pieces]
    arrays, specs = [q], [group_spec(seqs, wide, LANES)]
    if own is not None:
        arrays.append(own)
        specs.append(piece_spec(seqs, rows))
    for parts, count in zip(pieces, counts):
        arrays += parts
        specs += [piece_spec(count, rows)] * seqs
    row_spec, row_shape = group_spec(seqs, 1, wide), (seqs, groups, 1, wide)
    sum_spec, sum_shape = group_spec(seqs, wide, LANES), (seqs, groups, wide, LANES)
    if state is not None:
        arrays += list(state)
        specs += [row_spec, sum_spec]
    if is_last:
        attn_shape = (seqs, rows, HEADS * HEAD_DIM)
        out_shape = [
            jax.ShapeDtypeStruct(attn_shape, bf16),
            jax.ShapeDtypeStruct(row_shape, f32),
        ]
        out_specs = [full_spec(attn_shape), row_spec]
    else:
        out_shape = [
            jax.ShapeDtypeStruct(row_shape, f32),
            jax.ShapeDtypeStruct(sum_shape, f32),
        ]
        out_specs = [row_spec, sum_spec]
    return pl.pallas_call(
        functools.partial(
            forward_kernel, counts, own is not None, state is not None, is_last
        ),
        out_shape=out_shape,
        grid_spec=pltpu.PrefetchScalarGridSpec(
            num_scalar_prefetch=1,
            grid=(groups,),
            in_specs=specs,
            out_specs=out_specs,
            scratch_shapes=[
                pltpu.VMEM((seqs, 1, wide), f32),
                pltpu.VMEM((seqs, wide, LANES), f32),
            ],
        ),
        compiler_params=params(60),
        name="attend_forward",
    )(ids, *arrays)


def backward_kernel(counts, has_own, has_state, is_last, waits, ids, *refs):
    refs = list(refs)[waits:]
    q, d_out, log_total, delta = refs[:4]
    refs = refs[4:]
    seqs, rows = q.shape[0], q.shape[2] // PER
    own = refs.pop(0) if has_own else None
    pieces = [[refs.pop(0) for _ in range(seqs)] for _ in counts]
    d_query_in = refs.pop(0) if has_state else None
    cos, sin = (refs.pop(0), refs.pop(0)) if is_last else (None, None)
    d_own = refs.pop(0) if has_own else None
    d_pieces = [[refs.pop(0) for _ in range(seqs)] for _ in counts]
    d_query_out, d_query = refs
    me = ids[0]
    if has_state:
        d_query[...] = d_query_in[:, 0]
    else:
        d_query[...] = jnp.zeros_like(d_query)

    def back(s, kv, seen, place):
        q_all, d_all = q[s, 0], d_out[s, 0]
        scores = dot(kv, q_all, NT)
        if seen is None:
            probs = jnp.exp(scores - log_total[s, 0])
            probs = jnp.where(causal_part(rows, PER), probs, 0.0)
        else:
            probs = jnp.exp(scores - jnp.where(seen, log_total[s, 0], -mask_low))
        d_probs = dot(kv, d_all, NT)
        d_scores = (probs * (d_probs - delta[s, 0])).astype(bf16)
        d_query[s] += dot(d_scores.T, kv)
        terms = (dot(probs.astype(bf16), d_all) + dot(d_scores, q_all)).astype(bf16)
        piece, s, j = place
        if piece < 0:
            d_own[s] = terms
        else:
            d_pieces[piece][s][j] = terms

    def zeros(piece):
        for s in range(seqs):
            d_pieces[piece][s][...] = jnp.zeros(d_pieces[piece][s].shape, bf16)

    for_blocks(ids, me, seqs, own, pieces, counts, back, zeros)
    if is_last:
        group = pl.program_id(0)
        for s in range(seqs):
            turned = []
            for h in range(PER):
                tile = d_query[s, h * rows : (h + 1) * rows, :] * 0.125
                turned.append(
                    (tile * cos[s] - swap_halves(tile) * sin[s])[:, :HEAD_DIM].astype(bf16)
                )
            for g in range(KV_HEADS):

                @pl.when(group == g)
                def _(turned=turned, s=s, g=g):
                    for h in range(PER):
                        at = (g * PER + h) * HEAD_DIM
                        d_query_out[s, :, at : at + HEAD_DIM] = turned[h]

    else:
        d_query_out[:, 0] = d_query[...]


def backward_call(ids, q, d_out, log_total, delta, own, pieces, d_query, tables, after=()):
    seqs, groups, wide, _ = q.shape
    rows = wide // PER
    counts = [parts[0].shape[0] for parts in pieces]
    sum_spec, sum_shape = group_spec(seqs, wide, LANES), (seqs, groups, wide, LANES)
    row_spec = group_spec(seqs, 1, wide)
    arrays = [q, d_out, log_total, delta]
    specs = [sum_spec, sum_spec, row_spec, row_spec]
    out_shape, out_specs = [], []
    if own is not None:
        arrays.append(own)
        specs.append(piece_spec(seqs, rows))
        out_shape.append(jax.ShapeDtypeStruct(own.shape, bf16))
        out_specs.append(piece_spec(seqs, rows))
    for parts, count in zip(pieces, counts):
        arrays += parts
        specs += [piece_spec(count, rows)] * seqs
        out_shape += [jax.ShapeDtypeStruct(parts[0].shape, bf16)] * seqs
        out_specs += [piece_spec(count, rows)] * seqs
    if d_query is not None:
        arrays.append(d_query)
        specs.append(sum_spec)
    is_last = tables is not None
    if is_last:
        arrays += list(tables)
        specs += [full_spec((seqs, rows, LANES))] * 2
        shape = (seqs, rows, HEADS * HEAD_DIM)
        out_shape.append(jax.ShapeDtypeStruct(shape, bf16))
        out_specs.append(full_spec(shape))
    else:
        out_shape.append(jax.ShapeDtypeStruct(sum_shape, f32))
        out_specs.append(sum_spec)
    arrays = list(after) + arrays
    specs = [pl.BlockSpec(memory_space=pl.ANY)] * len(after) + specs
    outs = pl.pallas_call(
        functools.partial(
            backward_kernel, counts, own is not None, d_query is not None, is_last, len(after)
        ),
        out_shape=out_shape,
        grid_spec=pltpu.PrefetchScalarGridSpec(
            num_scalar_prefetch=1,
            grid=(groups,),
            in_specs=specs,
            out_specs=out_specs,
            scratch_shapes=[pltpu.VMEM((seqs, wide, LANES), f32)],
        ),
        compiler_params=params(60),
        name="attend_backward",
    )(ids, *arrays)
    d_own = None
    if own is not None:
        d_own, outs = outs[0], outs[1:]
    d_pieces = [list(outs[k * seqs : (k + 1) * seqs]) for k in range(len(counts))]
    return d_own, d_pieces, outs[-1]


def middle_kernel(
    x_ref,
    cot_ref,
    attn_ref,
    w_out_ref,
    norm_ref,
    w_gate_ref,
    w_up_ref,
    w_down_ref,
    out_ref,
    b_ref,
    hid_ref,
    d_gate_ref,
    d_up_ref,
    d_mid_ref,
    d_proj_ref,
    d_out_ref,
    delta_ref,
    g_norm_ref,
):
    x = x_ref[0].T.astype(f32)
    rows, width = x.shape
    cot = cot_ref[0].T
    attn = attn_ref[0]
    mid = x + dot(attn, w_out_ref[...])
    scale = lax.rsqrt(jnp.sum(mid * mid, axis=-1, keepdims=True) * (1.0 / width) + eps_norm)
    normed = mid * scale
    b = (normed * as_row(norm_ref)).astype(bf16)
    b_ref[0] = b
    gate = dot(b, w_gate_ref[...])
    up = dot(b, w_up_ref[...])
    sig = 1.0 / (1.0 + jnp.exp(-gate))
    active = gate * sig
    hid = (active * up).astype(bf16)
    hid_ref[0] = hid
    out_ref[0] = (mid + dot(hid, w_down_ref[...], NT)).astype(bf16).T
    d_hid = dot(cot, w_down_ref[...])
    d_gate = (d_hid * up * sig * (1.0 + gate * (1.0 - sig))).astype(bf16)
    d_up = (d_hid * active).astype(bf16)
    d_gate_ref[0] = d_gate
    d_up_ref[0] = d_up
    d_b = dot(d_gate, w_gate_ref[...], NT) + dot(d_up, w_up_ref[...], NT)
    g_norm = jnp.sum(d_b * normed, axis=0, keepdims=True)

    @pl.when(pl.program_id(0) == 0)
    def _():
        g_norm_ref[...] = g_norm

    @pl.when(pl.program_id(0) > 0)
    def _():
        g_norm_ref[...] += g_norm

    e = d_b * as_row(norm_ref)
    mean = jnp.sum(e * normed, axis=-1, keepdims=True) * (1.0 / width)
    d_mid = cot.astype(f32) + scale * (e - normed * mean)
    d_mid_ref[0] = d_mid
    d_proj = d_mid.astype(bf16)
    d_proj_ref[0] = d_proj
    d_attn = dot(d_proj, w_out_ref[...], NT).astype(bf16).astype(f32)
    both = d_attn * attn.astype(f32)
    high = both.astype(bf16)
    rest = (both - high.astype(f32)).astype(bf16)
    head = lax.broadcasted_iota(jnp.int32, (16, width), 0)
    feature = lax.broadcasted_iota(jnp.int32, (16, width), 1)
    picks = jnp.where(
        (feature >= head * HEAD_DIM) & (feature < (head + 1) * HEAD_DIM), 1.0, 0.0
    ).astype(bf16)
    sums = dot(picks, high, NT) + dot(picks, rest, NT)
    high_half = lane_index(rows) >= HEAD_DIM
    padded = jnp.concatenate([d_attn, jnp.zeros((rows, HEAD_DIM), f32)], axis=1)
    for k in range(HEADS):
        at = k // 2 * LANES
        tile = padded[:, at : at + LANES]
        if k % 2 == 0:
            tile = pltpu.roll(tile, HEAD_DIM, 1)
        group, place = divmod(k, PER)
        here = slice(place * rows, (place + 1) * rows)
        d_out_ref[0, group, here, :] = jnp.where(high_half, tile, 0.0).astype(bf16)
        delta_ref[0, group, 0:1, here] = sums[k : k + 1]


def middle_call(x, cot, attn, w_out, norm, w_gate, w_up, w_down):
    seqs, width, rows = x.shape
    hidden = w_gate.shape[1]
    row = lambda *shape: pl.BlockSpec((1,) + shape, lambda s: (s,) + (0,) * len(shape))
    wide = PER * rows
    shapes = [
        ((width, rows), bf16),
        ((rows, width), bf16),
        ((rows, hidden), bf16),
        ((rows, hidden), bf16),
        ((rows, hidden), bf16),
        ((rows, width), f32),
        ((rows, width), bf16),
        ((KV_HEADS, wide, LANES), bf16),
        ((KV_HEADS, 1, wide), f32),
    ]
    return pl.pallas_call(
        middle_kernel,
        grid=(seqs,),
        in_specs=[row(width, rows), row(width, rows), row(rows, width)]
        + [
            full_spec(w_out.shape),
            full_spec((width,)),
            full_spec(w_gate.shape),
            full_spec(w_up.shape),
            full_spec(w_down.shape),
        ],
        out_specs=[row(*shape) for shape, _ in shapes] + [full_spec((1, width))],
        out_shape=[jax.ShapeDtypeStruct((seqs,) + shape, kind) for shape, kind in shapes]
        + [jax.ShapeDtypeStruct((1, width), f32)],
        compiler_params=params(60),
        name="feed_forward",
    )(x, cot, attn, w_out, norm, w_gate, w_up, w_down)


def ffn_place(k, t, tiles):
    if k < 2:
        return k, t
    return (0, tiles + t) if t < tiles // 2 else (1, tiles + t - tiles // 2)


def half_rows(places, width, parts):
    unit = 16 * (parts // 2)
    return -(-places * width // unit) * unit


def put(out_ref, place, width, tile):
    half, at = place
    out_ref[half, at * width : (at + 1) * width, :] = tile


def with_column(tile, column):
    free = lane_index(tile.shape[0]) >= HEAD_DIM
    return jnp.where(free, column, tile)


def ffn_grad_kernel(b_ref, cot_ref, hid_ref, d_gate_ref, d_up_ref, out_ref):
    width = b_ref.shape[1]
    hidden = hid_ref.shape[1]
    tiles = hidden // LANES
    chunk = 2 * LANES
    b_turned = b_ref[...].T
    cot_turned = jnp.concatenate([cot_ref[s] for s in range(cot_ref.shape[0])], axis=1)
    for k, (left, right) in enumerate(
        ((b_turned, d_gate_ref), (b_turned, d_up_ref), (cot_turned, hid_ref))
    ):
        for c in range(hidden // chunk):
            product = dot(left, right[:, c * chunk : (c + 1) * chunk]).astype(bf16)
            for u in range(2):
                put(
                    out_ref,
                    ffn_place(k, 2 * c + u, tiles),
                    width,
                    product[:, u * LANES : (u + 1) * LANES],
                )


def ffn_grad_call(b, cot, hid, d_gate, d_up):
    width = b.shape[1]
    tiles = hid.shape[1] // LANES
    return pl.pallas_call(
        ffn_grad_kernel,
        out_shape=jax.ShapeDtypeStruct((2, (tiles + tiles // 2) * width, LANES), bf16),
        compiler_params=params(60),
        name="ffn_grads",
    )(b, cot, hid, d_gate, d_up)


def ffn_unfold_kernel(gate_in, up_in, down_in, gate_ref, up_ref, down_ref):
    tiles = gate_in.shape[1]
    for t in range(tiles):
        lanes = slice(t * LANES, (t + 1) * LANES)
        gate_ref[:, lanes] = gate_in[0, t].astype(f32)
        up_ref[:, lanes] = up_in[0, t].astype(f32)
        down_ref[:, lanes] = down_in[t // (tiles // 2), t % (tiles // 2)].astype(f32)


def ffn_unfold_call(sums, width, hidden):
    tiles = hidden // LANES
    steps = 2
    rows = width // steps
    sums = sums.reshape(2, tiles + tiles // 2, width, LANES)
    block = (1, tiles, rows, LANES)
    return pl.pallas_call(
        ffn_unfold_kernel,
        grid=(steps,),
        in_specs=[
            pl.BlockSpec(block, lambda i: (0, 0, i, 0)),
            pl.BlockSpec(block, lambda i: (1, 0, i, 0)),
            pl.BlockSpec((2, tiles // 2, rows, LANES), lambda i: (0, 2, i, 0)),
        ],
        out_specs=[pl.BlockSpec((rows, hidden), lambda i: (i, 0))] * 3,
        out_shape=[jax.ShapeDtypeStruct((width, hidden), f32)] * 3,
        compiler_params=params(60),
        name="ffn_unfold",
    )(sums, sums, sums)


def unfold_square(products, out_ref, norm_ref):
    for t, product in enumerate(products):
        if t < len(products) - 1:
            out_ref[:, t * LANES : (t + 1) * LANES] = product
        else:
            out_ref[:, t * LANES :] = product[:, :HEAD_DIM]
            norm_ref[...] = product.T[HEAD_DIM, :]


def unfold_call(kernel, name, arrays, shapes):
    smem = pl.BlockSpec(memory_space=pltpu.SMEM)
    vmem = pl.BlockSpec(memory_space=pltpu.VMEM)
    return pl.pallas_call(
        kernel,
        in_specs=[smem if t.ndim == 1 else vmem for t in arrays],
        out_shape=[jax.ShapeDtypeStruct(shape, f32) for shape in shapes],
        compiler_params=params(48),
        name=name,
    )(*arrays)


def query_grad_kernel(
    a_ref, attn_ref, d_proj_ref, d_q_ref, g_norm_ref, w_ref, out_ref, g_ref, g_out_ref
):
    for t, tile in enumerate(head_tiles(dot(a_ref[...].T, d_q_ref[...]))):
        g_ref[t] = tile.astype(bf16)
    width = a_ref.shape[1]
    column = jnp.broadcast_to(g_norm_ref[...], (8, width)).T[:, :1]
    for t, tile in enumerate(head_tiles(dot(attn_ref[...].T, d_proj_ref[...]))):
        if t == g_out_ref.shape[0] - 1:
            tile = with_column(tile, column)
        g_out_ref[t] = tile.astype(bf16)
    out_ref[...] = dot(d_q_ref[...], w_ref[...], NT)


def query_grad_call(a, attn, d_proj, d_q, g_norm, w_query):
    rows, width = a.shape
    tiles = jax.ShapeDtypeStruct((-(-width // LANES), width, LANES), bf16)
    return pl.pallas_call(
        query_grad_kernel,
        out_shape=[jax.ShapeDtypeStruct((rows, width), f32), tiles, tiles],
        compiler_params=params(32),
        name="query_grads",
    )(a, attn, d_proj, d_q, g_norm, w_query)


def attn_place(t):
    return t % 2, t // 2


def last_kernel(
    x_ref, a_ref, norm_ref, wk_ref, wv_ref, cos_ref, sin_ref, d_kv_ref, d_aq_ref, d_mid_ref, g_q_ref,
    g_out_ref, out_ref, g_ref, d_pairs, d_norm,
):
    step = pl.program_id(0)
    x = x_ref[0].T.astype(f32)
    rows, width = x.shape
    low_half = lane_index(rows) < HEAD_DIM
    scale = lax.rsqrt(jnp.sum(x * x, axis=-1, keepdims=True) * (1.0 / width) + eps_norm)
    normed = x * scale
    parts = []
    for g in range(KV_HEADS):
        tile = d_kv_ref[0, :, g * LANES : (g + 1) * LANES].astype(f32)
        turned = tile * cos_ref[0] - swap_halves(tile) * sin_ref[0]
        parts.append(jnp.where(low_half, turned, tile))
    moved = [pltpu.roll(part, HEAD_DIM, 1) for part in parts]
    d_key = jnp.concatenate(
        [jnp.where(low_half, parts[0], moved[1]), parts[2][:, :HEAD_DIM]], axis=1
    ).astype(bf16)
    d_value = jnp.concatenate(
        [jnp.where(low_half, moved[0], parts[1]), moved[2][:, :HEAD_DIM]], axis=1
    ).astype(bf16)
    g_pairs = dot(a_ref[0], jnp.concatenate(parts, axis=1).astype(bf16), TN)
    d_a = d_aq_ref[0] + dot(d_key, wk_ref[...]) + dot(d_value, wv_ref[...])
    g_norm = jnp.sum(d_a * normed, axis=0, keepdims=True)

    @pl.when(step == 0)
    def _():
        d_norm[...] = g_norm
        d_pairs[...] = g_pairs

    @pl.when(step > 0)
    def _():
        d_norm[...] += g_norm
        d_pairs[...] += g_pairs

    e = d_a * as_row(norm_ref)
    mean = jnp.sum(e * normed, axis=-1, keepdims=True) * (1.0 / width)
    out_ref[0] = (d_mid_ref[0] + scale * (e - normed * mean)).astype(bf16).T

    @pl.when(step == pl.num_programs(0) - 1)
    def _():
        square = g_q_ref.shape[0]
        column = jnp.broadcast_to(d_norm[...], (8, width)).T[:, :1]
        for t in range(square):
            tile = g_q_ref[t]
            if t == square - 1:
                tile = with_column(tile.astype(f32), column).astype(bf16)
            put(g_ref, attn_place(t), width, tile)
        for g in range(KV_HEADS):
            put(
                g_ref,
                attn_place(square + g),
                width,
                d_pairs[:, g * LANES : (g + 1) * LANES].astype(bf16),
            )
        for t in range(square):
            put(g_ref, attn_place(square + KV_HEADS + t), width, g_out_ref[t])
        clear_rest(g_ref, 2 * square + KV_HEADS, width)


def last_call(x, a, norm, w_key, w_value, cos, sin, d_kv, d_aq, d_mid, g_query, g_out, parts):
    seqs, width, rows = x.shape
    row = lambda *shape: pl.BlockSpec((1,) + shape, lambda s: (s,) + (0,) * len(shape))
    places = -(-(2 * g_query.shape[0] + KV_HEADS) // 2)
    g_shape = (2, half_rows(places, width, parts), LANES)
    wide = KV_HEADS * LANES
    return pl.pallas_call(
        last_kernel,
        grid=(seqs,),
        in_specs=[
            row(width, rows),
            row(rows, width),
            full_spec((width,)),
            full_spec(w_key.shape),
            full_spec(w_value.shape),
            row(rows, LANES),
            row(rows, LANES),
            row(rows, wide),
            row(rows, width),
            row(rows, width),
            full_spec(g_query.shape),
            full_spec(g_out.shape),
        ],
        out_specs=[row(width, rows), full_spec(g_shape)],
        out_shape=[
            jax.ShapeDtypeStruct((seqs, width, rows), bf16),
            jax.ShapeDtypeStruct(g_shape, bf16),
        ],
        scratch_shapes=[pltpu.VMEM((width, wide), f32), pltpu.VMEM((1, width), f32)],
        compiler_params=params(32),
        name="last_part",
    )(x, a, norm, w_key, w_value, cos, sin, d_kv, d_aq, d_mid, g_query, g_out)


def attn_unfold_kernel(
    side, mine, other, query_ref, key_ref, value_ref, norm_ref, out_ref, norm_two_ref
):
    width = query_ref.shape[0]
    square = -(-width // LANES)

    def spread(halves):
        def tile(t):
            half, at = attn_place(t)
            return halves[half][at * width : (at + 1) * width, :].astype(f32)

        unfold_square([tile(t) for t in range(square)], query_ref, norm_ref)
        for g in range(KV_HEADS):
            pair = tile(square + g)
            lanes = slice(g * HEAD_DIM, (g + 1) * HEAD_DIM)
            turned = pair.T
            key_ref[lanes, :] = turned[:HEAD_DIM]
            value_ref[lanes, :] = turned[HEAD_DIM:]
        first = square + KV_HEADS
        unfold_square([tile(first + t) for t in range(square)], out_ref, norm_two_ref)

    @pl.when(side[0] == 0)
    def _():
        spread((mine, other))

    @pl.when(side[0] != 0)
    def _():
        spread((other, mine))


def device_stages(seq_count, batch_count):
    masks = [1 << k for k in range(batch_count.bit_length() - 1)]
    masks += [mask * batch_count for mask in exchange_masks(seq_count)]
    return [masks[:1]] + [masks[k : k + 2] for k in range(1, len(masks), 2)]


def stage_places(stages, index):
    bits = {}
    for mask in sorted((m for stage in stages for m in stage), reverse=True):
        bit = (index >> (mask.bit_length() - 1)) & 1
        bits[mask] = bit
        index = index ^ (bit * mask)
    return [sum(bits[mask] << k for k, mask in enumerate(stage)) for stage in stages]


def swap_with(value, mask, devices):
    return lax.ppermute(value, ("seq", "batch"), [(i, i ^ mask) for i in range(devices)])


def scatter_stage(value, stage, place, devices):
    group = 1 << len(stage)
    masks = span(stage)
    value = value.reshape((group, -1, LANES))
    pick = lambda k: lax.dynamic_index_in_dim(value, place ^ k, 0, False)
    got = [swap_with(pick(k), masks[k], devices) for k in range(1, group)]
    return sum((g.astype(f32) for g in got), pick(0).astype(f32)).astype(bf16)


def gather_stage(value, stage, place, devices):
    group = 1 << len(stage)
    masks = span(stage)
    parts = jnp.stack([value] + [swap_with(value, masks[k], devices) for k in range(1, group)])
    for k in range(len(stage)):
        shape = parts.shape
        split = parts.reshape((group >> (k + 1), 2, 1 << k) + shape[1:])
        parts = jnp.where((place >> k) & 1 == 1, split[:, ::-1], split).reshape(shape)
    return parts


def gather_order(value, order, stages, places, devices):
    done = []
    for k in order:
        value = gather_stage(value, stages[k], places[k], devices)
        done.insert(0, k)
    back = sorted(range(len(done)), key=lambda i: done[i])
    return jnp.transpose(value, back + [len(done), len(done) + 1])


def gather_sums(part, stages, places, devices, chains):
    late = list(range(1, len(stages)))[::-1]
    step = part.shape[0] // chains
    got = [
        gather_order(
            part[c * step : (c + 1) * step],
            late[c % len(late) :] + late[: c % len(late)],
            stages,
            places,
            devices,
        )
        for c in range(chains)
    ]
    half = got[0] if chains == 1 else jnp.concatenate(got, axis=-2)
    half = half.reshape(-1, LANES)
    return half, swap_with(half, stages[0][0], devices)


def exchange_masks(count):
    masks = [1 << k for k in range(count.bit_length() - 1)]
    if count == 8:
        masks[2] = 6
    return masks


def chain_order(masks, chain):
    shift = chain % len(masks)
    return masks[shift:] + masks[:shift]


def span(masks):
    ids = [0]
    for mask in masks:
        ids += [k ^ mask for k in ids]
    return ids


def gather_blocks(kv, count):
    me = lax.axis_index("seq")
    masks = exchange_masks(count)
    seqs, last = kv.shape[0], len(masks) - 1
    held = [kv[s : s + 1] for s in range(seqs)]
    rounds, numbers = [], []

    def send(s, r, value, known, is_last):
        mask = chain_order(masks, s)[r]
        pairs = [
            (i, i ^ mask)
            for i in range(count)
            if not is_last or min(i ^ k for k in known) < i ^ mask
        ]
        return lax.ppermute(value, "seq", pairs), [me ^ (mask ^ k) for k in known]

    def keep(sent):
        rounds.append([value for value, _ in sent])
        numbers.append([k for _, known in sent for k in known])

    early = []
    for r in range(last):
        known = [span(chain_order(masks, s)[:r]) for s in range(seqs)]
        if r == last - 1:
            early = [send(s, last, held[s], known[s], True) for s in range(seqs)]
        sent = [send(s, r, held[s], known[s], False) for s in range(seqs)]
        keep(sent)
        if r < last - 1:
            held = [jnp.concatenate([h, v], axis=0) for h, (v, _) in zip(held, sent)]
    keep(early)
    keep(
        [
            send(
                s,
                last,
                rounds[last - 1][s],
                [chain_order(masks, s)[last - 1] ^ k for k in known[s]],
                True,
            )
            for s in range(seqs)
        ]
    )
    return rounds, numbers


def add_low(*terms):
    return sum((t.astype(f32) for t in terms[1:]), terms[0].astype(f32)).astype(bf16)


def return_round(parts, r, count):
    masks = exchange_masks(count)
    got = []
    for s, part in enumerate(parts):
        order = chain_order(masks, s)
        mask, known = order[r], span(order[:r])
        pairs = [
            (i, i ^ mask)
            for i in range(count)
            if r < len(masks) - 1 or min(i ^ mask ^ k for k in known) < i
        ]
        got.append(lax.ppermute(part, "seq", pairs))
    return got


def beside(tile):
    rows = tile.shape[0]
    half = rows // 2
    return jnp.where(
        lane_index(half) < HEAD_DIM, tile[:half], pltpu.roll(tile[half:], HEAD_DIM, 1)
    )


def stacked(tile):
    return jnp.concatenate([tile, pltpu.roll(tile, HEAD_DIM, 1)], axis=0)


def other_half(tile):
    return pltpu.roll(tile, HEAD_DIM, 1)


def join(low, high):
    return jnp.where(lane_index(low.shape[0]) < HEAD_DIM, low, high)


def low_only(tile):
    return jnp.where(lane_index(tile.shape[0]) < HEAD_DIM, tile, 0.0)


def high_only(tile):
    return jnp.where(lane_index(tile.shape[0]) < HEAD_DIM, 0.0, tile)


def write_long(ref, at, parts, more=None):
    h0, h1, h2, key, value = parts
    rows = key.shape[0]
    ref[at, 0:rows] = join(h0, other_half(h1)).astype(bf16)
    ref[at, rows : 2 * rows] = join(h2, other_half(key)).astype(bf16)
    ref[at, 2 * rows : rows * 5 // 2] = beside(value).astype(bf16)
    if more is not None:
        ref[at, rows * 5 // 2 :] = more


def read_long(message, rows):
    first = message[0:rows].astype(f32)
    second = message[rows : 2 * rows].astype(f32)
    value = stacked(message[2 * rows : rows * 5 // 2].astype(f32))
    return (first, other_half(first), second), join(other_half(second), other_half(value))


def write_short(ref, at, heads):
    rows = heads[0].shape[0]
    ref[at, 0:rows] = join(heads[0], other_half(heads[1])).astype(bf16)
    ref[at, rows:] = beside(heads[2]).astype(bf16)


def read_short(message):
    rows = message.shape[0] * 2 // 3
    first = message[0:rows].astype(f32)
    return first, other_half(first), stacked(message[rows:].astype(f32))


def units_pre_kernel(
    count, ids, x_ref, norm_ref, wq_ref, wk_ref, wv_ref, cos_ref, sin_ref, *refs
):
    outs, (a_ref, q_ref, kv_ref, out_ref) = refs[:count], refs[count:]
    me = ids[0]
    seqs, width, rows = x_ref.shape

    def heads_of(tiles, many):
        return [tiles[h // 2] if h % 2 == 0 else other_half(tiles[h // 2]) for h in range(many)]

    for s in range(seqs):
        x = x_ref[s].T.astype(f32)
        scale = lax.rsqrt(jnp.sum(x * x, axis=-1, keepdims=True) * (1.0 / width) + eps_norm)
        a = (x * scale * as_row(norm_ref)).astype(bf16)
        a_ref[s] = a
        cos, sin = cos_ref[s], sin_ref[s]

        def turn(tile, cos=cos, sin=sin):
            return tile * cos + swap_halves(tile) * sin

        queries = heads_of([turn(t) * 0.125 for t in head_tiles(dot(a, wq_ref[...]))], HEADS)
        keys = heads_of([turn(t) for t in head_tiles(dot(a, wk_ref[...], NT))], KV_HEADS)
        values = heads_of(head_tiles(dot(a, wv_ref[...], NT)), KV_HEADS)
        for g in range(KV_HEADS):
            parts = queries[g * PER : (g + 1) * PER] + [keys[g], values[g]]
            unit = s * KV_HEADS + g
            if unit < count:
                write_long(out_ref, lax.rem(unit - me + count, count), parts)
            else:
                for h in range(PER):
                    q_ref[h * rows : (h + 1) * rows] = low_only(parts[h]).astype(bf16)
                kv_ref[0] = join(parts[3], other_half(parts[4])).astype(bf16)
    hand_out(out_ref, outs)


def hand_out(messages, outs):
    for t, out in enumerate(outs):
        out[...] = messages[t]


def units_pre_call(ids, x, norm, w_query, w_key, w_value, cos, sin, count):
    seqs, width, rows = x.shape
    vmem = pl.BlockSpec(memory_space=pltpu.VMEM)
    message = (rows * 5 // 2, LANES)
    outs = pl.pallas_call(
        functools.partial(units_pre_kernel, count),
        in_specs=[pl.BlockSpec(memory_space=pltpu.SMEM)] + [vmem] * 7,
        out_shape=[jax.ShapeDtypeStruct(message, bf16)] * count
        + [
            jax.ShapeDtypeStruct((seqs, rows, width), bf16),
            jax.ShapeDtypeStruct((PER * rows, LANES), bf16),
            jax.ShapeDtypeStruct((1, rows, LANES), bf16),
        ],
        scratch_shapes=[pltpu.VMEM((count,) + message, bf16)],
        compiler_params=params(60),
        name="project",
    )(ids, x, norm, w_query, w_key, w_value, cos, sin)
    return (outs[:count],) + tuple(outs[count:])


def attend_row(q, blocks, seen=None):
    rows = blocks[0].shape[0]
    peak = sums = None
    for first in range(0, len(blocks), UNROLL):
        part = blocks[first : first + UNROLL]
        scores = [dot(kv, q, NT) for kv in part]
        if first + len(part) == len(blocks):
            scores[-1] = jnp.where(causal_part(rows, PER), scores[-1], mask_low)
        tops = [jnp.max(sc, axis=0, keepdims=True) for sc in scores]
        flags = [None] * len(part)
        if seen is not None:
            flags = (seen + [None])[first : first + UNROLL]
            tops = [t if f is None else jnp.where(f, t, mask_low) for t, f in zip(tops, flags)]
        new_peak = functools.reduce(jnp.maximum, tops if peak is None else tops + [peak])
        shifts = [new_peak if f is None else jnp.where(f, new_peak, -mask_low) for f in flags]
        shares = [jnp.exp(sc - sh).astype(bf16).T for sc, sh in zip(scores, shifts)]
        ones = lane_index(rows) < HEAD_DIM
        values = [jnp.where(ones, jnp.ones((), bf16), kv) for kv in part]
        added = dot(jnp.concatenate(shares, axis=1), jnp.concatenate(values, axis=0))
        if peak is not None:
            fading = jnp.broadcast_to(jnp.exp(peak - new_peak), (LANES, peak.shape[1])).T
            added = sums * fading + added
        peak, sums = new_peak, added
    return peak, sums


def attend_result(peak, total):
    rows = total.shape[0] // PER
    moved = other_half(total)
    normal = moved / total
    log_total = peak + jnp.log(total.T[0:1])
    return [normal[h * rows : (h + 1) * rows] for h in range(PER)], log_total


def units_forward_kernel(count, ids, *refs):
    messages = refs[:count]
    outs, (log_ref, q_ref, kv_ref, out_ref) = refs[-4 - count : -4], refs[-4:]
    rows = kv_ref.shape[1]
    me = ids[0]
    for t in range(count):
        block = lax.rem(me - t + count, count)
        heads, kv = read_long(messages[t], rows)
        for h in range(PER):
            q_ref[block, h * rows : (h + 1) * rows] = low_only(heads[h]).astype(bf16)
        kv_ref[block] = kv.astype(bf16)
    for i in range(count):
        new_peak, sums = attend_row(q_ref[i], [kv_ref[j] for j in range(i + 1)])
        heads, log_total = attend_result(new_peak, sums)
        log_ref[i] = log_total
        write_short(out_ref, lax.rem(i - me + count, count), heads)
    hand_out(out_ref, outs)


def units_forward_call(ids, messages, after):
    count = len(messages)
    rows = messages[0].shape[0] * 2 // 5
    wide = PER * rows
    vmem = pl.BlockSpec(memory_space=pltpu.VMEM)
    message = (rows * 3 // 2, LANES)
    outs = pl.pallas_call(
        functools.partial(units_forward_kernel, count),
        in_specs=[pl.BlockSpec(memory_space=pltpu.SMEM)]
        + [vmem] * count
        + [pl.BlockSpec(memory_space=pl.ANY)] * len(after),
        out_shape=[jax.ShapeDtypeStruct(message, bf16)] * count
        + [
            jax.ShapeDtypeStruct((count, 1, wide), f32),
            jax.ShapeDtypeStruct((count, wide, LANES), bf16),
            jax.ShapeDtypeStruct((count, rows, LANES), bf16),
        ],
        scratch_shapes=[pltpu.VMEM((count,) + message, bf16)],
        compiler_params=params(48),
        name="units_forward",
    )(ids, *messages, *after)
    return (outs[:count],) + tuple(outs[count:])


def last_unit_forward_kernel(ids, q_ref, kv_ref, out_ref, log_ref):
    me = ids[0]
    count = kv_ref.shape[0]
    others = span(exchange_masks(count))[1:]
    blocks = [kv_ref[p] for p in range(1, count)] + [kv_ref[0]]
    heads, log_total = attend_result(
        *attend_row(q_ref[...], blocks, [(me ^ k) < me for k in others])
    )
    log_ref[...] = log_total
    write_short(out_ref, 0, heads)


def last_unit_forward_call(ids, q, kv):
    wide = q.shape[0]
    vmem = pl.BlockSpec(memory_space=pltpu.VMEM)
    return pl.pallas_call(
        last_unit_forward_kernel,
        in_specs=[pl.BlockSpec(memory_space=pltpu.SMEM), vmem, vmem],
        out_shape=[
            jax.ShapeDtypeStruct((1, wide // 2, LANES), bf16),
            jax.ShapeDtypeStruct((1, wide), f32),
        ],
        compiler_params=params(32),
        name="last_unit_forward",
    )(ids, q, kv)


def attend_back(q, d_out, kv, log_total, delta, diagonal):
    rows = kv.shape[0]
    scores = dot(kv, q, NT)
    probs = jnp.exp(scores - log_total)
    if diagonal:
        probs = jnp.where(causal_part(rows, PER), probs, 0.0)
    d_probs = dot(kv, d_out, NT)
    d_scores = (probs * (d_probs - delta)).astype(bf16)
    return (
        dot(probs.astype(bf16), d_out) + dot(d_scores, q),
        dot(d_scores.T, kv),
    )


def unpack_out(message, attn):
    heads, values = read_short(message), read_short(attn)
    delta = [
        jnp.sum(low_only(d * o).T, axis=0, keepdims=True) for d, o in zip(heads, values)
    ]
    d_out = jnp.concatenate([high_only(other_half(d)) for d in heads], axis=0)
    return d_out.astype(bf16), jnp.concatenate(delta, axis=1)


def last_unit_backward_kernel(
    ids, q_ref, kv_ref, d_ref, attn_ref, log_ref, d_kv_ref, d_q_ref, d_out
):
    me = ids[0]
    count = kv_ref.shape[0]
    d_value, delta = unpack_out(d_ref[...], attn_ref[...])
    d_out[...] = d_value
    log_total = log_ref[...]
    total = None
    for p, k in list(enumerate(span(exchange_masks(count))))[1:]:
        shift = jnp.where((me ^ k) < me, log_total, -mask_low)
        d_kv, d_q = attend_back(q_ref[...], d_out[...], kv_ref[p], shift, delta, False)
        d_kv_ref[me ^ k] = d_kv.astype(bf16)
        total = d_q if total is None else total + d_q
    d_kv, d_q = attend_back(q_ref[...], d_out[...], kv_ref[0], log_total, delta, True)
    d_kv_ref[me] = d_kv.astype(bf16)
    d_q_ref[...] = total + d_q


def last_unit_backward_call(ids, q, kv, d_message, attn, log_total):
    vmem = pl.BlockSpec(memory_space=pltpu.VMEM)
    return pl.pallas_call(
        last_unit_backward_kernel,
        in_specs=[pl.BlockSpec(memory_space=pltpu.SMEM)] + [vmem] * 5,
        out_shape=[
            jax.ShapeDtypeStruct(kv.shape, bf16),
            jax.ShapeDtypeStruct(q.shape, f32),
        ],
        scratch_shapes=[pltpu.VMEM(q.shape, bf16)],
        compiler_params=params(24),
        name="last_unit_backward",
    )(ids, q, kv, d_message, attn, log_total)


def units_backward_kernel(count, ids, *refs):
    messages, refs = refs[:count], refs[count:]
    attn, refs = refs[:count], refs[count:]
    q_ref, kv_ref, log_ref, last_ref = refs[:4]
    outs, (out_ref, d_out, delta, d_kv) = refs[4:-4], refs[-4:]
    rows = kv_ref.shape[1]
    me = ids[0]
    for t in range(count):
        block = lax.rem(me - t + count, count)
        value, row = unpack_out(messages[t][...], attn[(count - t) % count][...])
        d_out[block] = value
        delta[block] = row
    for i in reversed(range(count)):
        d_query = None
        for first in range(0, i + 1, 2):
            places = list(range(first, min(first + 2, i + 1)))
            blocks = [kv_ref[j] for j in places]
            probs, d_scores = [], []
            for j, kv in zip(places, blocks):
                prob = jnp.exp(dot(kv, q_ref[i], NT) - log_ref[i])
                if j == i:
                    prob = jnp.where(causal_part(rows, PER), prob, 0.0)
                d_prob = dot(kv, d_out[i], NT)
                d_scores.append((prob * (d_prob - delta[i])).astype(bf16))
                probs.append(prob.astype(bf16))
            for j, prob, d_score in zip(places, probs, d_scores):
                term = dot(prob, d_out[i]) + dot(d_score, q_ref[i])
                d_kv[j] = term if i == count - 1 else d_kv[j] + term
            term = dot(jnp.concatenate([d.T for d in d_scores], axis=1), jnp.concatenate(blocks, axis=0))
            d_query = term if d_query is None else d_query + term
        tile = d_kv[i]
        write_long(
            out_ref,
            lax.rem(i - me + count, count),
            [d_query[h * rows : (h + 1) * rows] for h in range(PER)] + [tile, other_half(tile)],
            last_ref[i],
        )
    hand_out(out_ref, outs)


def units_backward_call(ids, messages, q, kv, attn, log_total, last_d_kv):
    count, rows, _ = kv.shape
    wide = PER * rows
    vmem = pl.BlockSpec(memory_space=pltpu.VMEM)
    message = (rows * 7 // 2, LANES)
    return pl.pallas_call(
        functools.partial(units_backward_kernel, count),
        in_specs=[pl.BlockSpec(memory_space=pltpu.SMEM)] + [vmem] * (2 * count + 4),
        out_shape=[jax.ShapeDtypeStruct(message, bf16)] * count,
        scratch_shapes=[
            pltpu.VMEM((count,) + message, bf16),
            pltpu.VMEM((count, wide, LANES), bf16),
            pltpu.VMEM((count, 1, wide), f32),
            pltpu.VMEM((count, rows, LANES), f32),
        ],
        compiler_params=params(56),
        name="units_backward",
    )(ids, *messages, *attn, q, kv, log_total, last_d_kv)


def units_ffn_kernel(
    count,
    ids,
    x_ref,
    cot_ref,
    norm_ref,
    w_out_ref,
    w_gate_hbm,
    w_up_hbm,
    w_down_hbm,
    *refs,
):
    messages, last_message = refs[:count], refs[count]
    (
        mid_hbm, attn_hbm, hid_hbm, d_gate_hbm, d_up_hbm, g_hbm,
        units, w_gate, w_up, w_down, mid, attn, cot, b, hid, d_gate, d_up, g_buf, w_sems, out_sems,
    ) = refs[count + 1 :]
    me = ids[0]
    seqs, width, rows = x_ref.shape
    hidden = w_gate.shape[1]
    tiles = hidden // LANES
    loads = [
        pltpu.make_async_copy(source, target, w_sems.at[k])
        for k, (source, target) in enumerate(
            ((w_gate_hbm, w_gate), (w_up_hbm, w_up), (w_down_hbm, w_down))
        )
    ]
    for load in loads:
        load.start()
    stores = []

    def store(source, target):
        copy = pltpu.make_async_copy(source, target, out_sems.at[len(stores)])
        copy.start()
        stores.append(copy)

    for t in range(count):
        units[lax.rem(me - t + count, count)] = messages[t][...]
    units[count] = last_message[0]
    for s in range(seqs):
        here = slice(s * rows, (s + 1) * rows)
        heads = []
        for g in range(KV_HEADS):
            heads += read_short(units[s * KV_HEADS + g])
        parts = [join(heads[h], other_half(heads[h + 1])) for h in range(0, HEADS - 1, 2)]
        attn_rows = jnp.concatenate(parts + [heads[HEADS - 1][:, :HEAD_DIM]], axis=1).astype(bf16)
        attn[s] = attn_rows
        cot[here] = cot_ref[s].T
        mid_rows = x_ref[s].T.astype(f32) + dot(attn_rows, w_out_ref[...])
        scale = lax.rsqrt(
            jnp.sum(mid_rows * mid_rows, axis=-1, keepdims=True) * (1.0 / width) + eps_norm
        )
        mid[s] = mid_rows
        b[here] = (mid_rows * scale * as_row(norm_ref)).astype(bf16)
    store(mid, mid_hbm)
    store(attn, attn_hbm)
    b_turned = b[...].T
    cot_turned = jnp.concatenate([cot_ref[s] for s in range(seqs)], axis=1)
    for load in loads:
        load.wait()
    chunk = 2 * LANES

    def gradient(k, c, left, right):
        product = dot(left, right[:, c * chunk : (c + 1) * chunk]).astype(bf16)
        for u in range(2):
            half, at = ffn_place(k, 2 * c + u, tiles)
            here = pl.ds(at * width, width)
            g_buf[half, here, :] = product[:, u * LANES : (u + 1) * LANES]
            store(g_buf.at[half, here], g_hbm.at[half, here])

    for c in range(hidden // chunk):
        lanes = pl.ds(c * chunk, chunk)
        gate = dot(b[...], w_gate[:, lanes])
        up = dot(b[...], w_up[:, lanes])
        d_hid = dot(cot[...], w_down[:, lanes])
        sig = 1.0 / (1.0 + jnp.exp(-gate))
        active = gate * sig
        hid[:, lanes] = (active * up).astype(bf16)
        d_gate[:, lanes] = (d_hid * up * sig * (1.0 + gate * (1.0 - sig))).astype(bf16)
        d_up[:, lanes] = (d_hid * active).astype(bf16)
    for source, target in ((d_gate, d_gate_hbm), (d_up, d_up_hbm), (hid, hid_hbm)):
        store(source, target)
    for k, (left, right) in enumerate(((b_turned, d_gate), (b_turned, d_up), (cot_turned, hid))):
        for c in range(hidden // chunk):
            gradient(k, c, left, right)
    for copy in stores:
        copy.wait()


def units_ffn_call(ids, x, cot, messages, last_message, w_out, norm, w_gate, w_up, w_down):
    seqs, width, rows = x.shape
    hidden = w_gate.shape[1]
    count = len(messages)
    tokens = seqs * rows
    short = (rows * 3 // 2, LANES)
    tiles = hidden // LANES
    g_shape = (2, (tiles + tiles // 2) * width, LANES)
    vmem = pl.BlockSpec(memory_space=pltpu.VMEM)
    hbm = pl.BlockSpec(memory_space=pl.ANY)
    wide = (tokens, hidden)
    return pl.pallas_call(
        functools.partial(units_ffn_kernel, count),
        in_specs=[pl.BlockSpec(memory_space=pltpu.SMEM)]
        + [vmem] * 4
        + [hbm] * 3
        + [vmem] * (count + 1),
        out_specs=[hbm] * 6,
        out_shape=[
            jax.ShapeDtypeStruct((seqs, rows, width), f32),
            jax.ShapeDtypeStruct((seqs, rows, width), bf16),
            jax.ShapeDtypeStruct(wide, bf16),
            jax.ShapeDtypeStruct(wide, bf16),
            jax.ShapeDtypeStruct(wide, bf16),
            jax.ShapeDtypeStruct(g_shape, bf16),
        ],
        scratch_shapes=[
            pltpu.VMEM((count + 1,) + short, bf16),
            pltpu.VMEM(w_gate.shape, bf16),
            pltpu.VMEM(w_up.shape, bf16),
            pltpu.VMEM(w_down.shape, bf16),
            pltpu.VMEM((seqs, rows, width), f32),
            pltpu.VMEM((seqs, rows, width), bf16),
            pltpu.VMEM((tokens, width), bf16),
            pltpu.VMEM((tokens, width), bf16),
            pltpu.VMEM(wide, bf16),
            pltpu.VMEM(wide, bf16),
            pltpu.VMEM(wide, bf16),
            pltpu.VMEM(g_shape, bf16),
            pltpu.SemaphoreType.DMA((3,)),
            pltpu.SemaphoreType.DMA((5 + 3 * tiles,)),
        ],
        compiler_params=params(60),
        name="feed_forward",
    )(ids, x, cot, norm, w_out, w_gate, w_up, w_down, *messages, last_message)


def units_back_kernel(
    count,
    ids,
    mid_ref,
    cot_ref,
    d_gate_ref,
    d_up_ref,
    norm_ref,
    w_out_ref,
    w_gate_ref,
    w_up_ref,
    d_mid_ref,
    d_last_ref,
    g_norm_ref,
    *refs,
):
    outs, d_out_ref = refs[:count], refs[count]
    step = pl.program_id(0)
    me = ids[0]
    mid = mid_ref[0]
    rows, width = mid.shape
    cot = cot_ref[0].T
    scale = lax.rsqrt(jnp.sum(mid * mid, axis=-1, keepdims=True) * (1.0 / width) + eps_norm)
    normed = mid * scale
    d_b = dot(d_gate_ref[...], w_gate_ref[...], NT) + dot(d_up_ref[...], w_up_ref[...], NT)
    norm_term = jnp.sum(d_b * normed, axis=0, keepdims=True)
    e = d_b * as_row(norm_ref)
    mean = jnp.sum(e * normed, axis=-1, keepdims=True) * (1.0 / width)
    d_mid = cot.astype(f32) + scale * (e - normed * mean)
    d_mid_ref[0] = d_mid
    d_proj = d_mid.astype(bf16)
    d_tiles = head_tiles(dot(d_proj, w_out_ref[...], NT))
    d_heads = [
        d_tiles[h // 2] if h % 2 == 0 else other_half(d_tiles[h // 2]) for h in range(HEADS)
    ]
    for g in range(KV_HEADS):
        unit = step * KV_HEADS + g

        @pl.when(unit < count)
        def _(g=g, unit=unit):
            at = lax.rem(unit - me + count, count)
            write_short(d_out_ref, at, d_heads[g * PER : (g + 1) * PER])

        @pl.when(unit == count)
        def _(g=g):
            write_short(d_last_ref, 0, d_heads[g * PER : (g + 1) * PER])

    @pl.when(step == 0)
    def _():
        g_norm_ref[...] = norm_term

    @pl.when(step > 0)
    def _():
        g_norm_ref[...] += norm_term

    @pl.when(step == pl.num_programs(0) - 1)
    def _():
        hand_out(d_out_ref, outs)


def units_back_call(ids, mid, cot, d_gate, d_up, norm, w_out, w_gate, w_up, count):
    seqs, rows, width = mid.shape
    hidden = w_gate.shape[1]
    row = lambda *shape: pl.BlockSpec((1,) + shape, lambda s, *_: (s,) + (0,) * len(shape))
    part = pl.BlockSpec((rows, hidden), lambda s, *_: (s, 0))
    short = (rows * 3 // 2, LANES)
    outs = pl.pallas_call(
        functools.partial(units_back_kernel, count),
        grid_spec=pltpu.PrefetchScalarGridSpec(
            num_scalar_prefetch=1,
            grid=(seqs,),
            in_specs=[row(rows, width), row(width, rows), part, part, full_spec((width,))]
            + [full_spec(w_out.shape), full_spec(w_gate.shape), full_spec(w_up.shape)],
            out_specs=[
                row(rows, width),
                full_spec((1,) + short),
                full_spec((1, width)),
            ]
            + [full_spec(short)] * count,
            scratch_shapes=[pltpu.VMEM((count,) + short, bf16)],
        ),
        out_shape=[
            jax.ShapeDtypeStruct((seqs, rows, width), f32),
            jax.ShapeDtypeStruct((1,) + short, bf16),
            jax.ShapeDtypeStruct((1, width), f32),
        ]
        + [jax.ShapeDtypeStruct(short, bf16)] * count,
        compiler_params=params(60),
        name="feed_back",
    )(ids, mid, cot, d_gate, d_up, norm, w_out, w_gate, w_up)
    return (outs[3:],) + tuple(outs[:3])


def units_out_kernel(
    mid_ref, attn_ref, hid_ref, d_mid_ref, g_norm_ref, w_down_ref, out_ref, g_ref, g_out
):
    step = pl.program_id(0)
    out_ref[0] = (mid_ref[0] + dot(hid_ref[...], w_down_ref[...], NT)).astype(bf16).T
    term = dot(attn_ref[0].T, d_mid_ref[0].astype(bf16))

    @pl.when(step == 0)
    def _():
        g_out[...] = term

    @pl.when(step > 0)
    def _():
        g_out[...] += term

    @pl.when(step == pl.num_programs(0) - 1)
    def _():
        column = jnp.broadcast_to(g_norm_ref[...], (8, g_norm_ref.shape[1])).T[:, :1]
        for t, tile in enumerate(head_tiles(g_out[...])):
            if t == g_ref.shape[0] - 1:
                tile = with_column(tile, column)
            g_ref[t] = tile.astype(bf16)


def units_out_call(mid, attn, hid, d_mid, g_norm, w_down):
    seqs, rows, width = mid.shape
    hidden = w_down.shape[1]
    row = lambda *shape: pl.BlockSpec((1,) + shape, lambda s: (s,) + (0,) * len(shape))
    g_shape = (-(-width // LANES), width, LANES)
    return pl.pallas_call(
        units_out_kernel,
        grid=(seqs,),
        in_specs=[
            row(rows, width),
            row(rows, width),
            pl.BlockSpec((rows, hidden), lambda s: (s, 0)),
            row(rows, width),
            full_spec((1, width)),
            full_spec(w_down.shape),
        ],
        out_specs=[row(width, rows), full_spec(g_shape)],
        out_shape=[
            jax.ShapeDtypeStruct((seqs, width, rows), bf16),
            jax.ShapeDtypeStruct(g_shape, bf16),
        ],
        scratch_shapes=[pltpu.VMEM((width, width), f32)],
        compiler_params=params(60),
        name="feed_out",
    )(mid, attn, hid, d_mid, g_norm, w_down)


def units_last_kernel(
    count, ids, x_ref, a_ref, norm_ref, wq_ref, wk_ref, wv_ref, cos_ref, sin_ref, d_mid_ref, last_q_ref,
    g_out_ref, *refs,
):
    messages = refs[:count]
    core, out_ref, keep_ref, send_ref, g_ref, units = refs[count:]
    me = ids[0]
    seqs, width, rows = x_ref.shape
    for t in range(count):
        units[lax.rem(me - t + count, count)] = messages[t][: rows * 5 // 2]
    last_kv = sum(messages[t][rows * 5 // 2 :].astype(f32) for t in range(count))
    heads = [last_q_ref[h * rows : (h + 1) * rows] for h in range(PER)]
    write_long(units, count, heads + [last_kv, other_half(last_kv)])

    def flat(tiles):
        return jnp.concatenate(tiles[:-1] + [tiles[-1][:, :HEAD_DIM]], axis=1).astype(bf16)

    d_queries, d_pairs = [], []
    g_norm = None
    for s in range(seqs):
        cos, sin = cos_ref[s], sin_ref[s]

        def turn(tile, cos=cos, sin=sin):
            return tile * cos - swap_halves(tile) * sin

        def in_tiles(parts):
            return [
                join(parts[h], other_half(parts[h + 1])) for h in range(0, len(parts) - 1, 2)
            ] + [parts[-1]]

        heads, keys, values = [], [], []
        for g in range(KV_HEADS):
            parts, kv = read_long(units[s * KV_HEADS + g], rows)
            heads += parts
            keys.append(kv)
            values.append(other_half(kv))
        d_query = flat([turn(t) * 0.125 for t in in_tiles(heads)])
        key_tiles = [turn(t) for t in in_tiles(keys)]
        d_key, d_value = flat(key_tiles), flat(in_tiles(values))
        turned = [
            key_tiles[g // 2] if g % 2 == 0 else other_half(key_tiles[g // 2])
            for g in range(KV_HEADS)
        ]
        pairs = [join(turned[g], other_half(values[g])) for g in range(KV_HEADS)]
        d_queries.append(d_query)
        d_pairs.append(jnp.concatenate(pairs, axis=1).astype(bf16))
        d_a = (
            dot(d_query, wq_ref[...], NT) + dot(d_key, wk_ref[...]) + dot(d_value, wv_ref[...])
        )
        x = x_ref[s].T.astype(f32)
        scale = lax.rsqrt(jnp.sum(x * x, axis=-1, keepdims=True) * (1.0 / width) + eps_norm)
        normed = x * scale
        term = jnp.sum(d_a * normed, axis=0, keepdims=True)
        g_norm = term if g_norm is None else g_norm + term
        e = d_a * as_row(norm_ref)
        mean = jnp.sum(e * normed, axis=-1, keepdims=True) * (1.0 / width)
        out_ref[s] = (d_mid_ref[s] + scale * (e - normed * mean)).astype(bf16).T
    a_turned = jnp.concatenate([a_ref[s].T for s in range(seqs)], axis=1)
    g_query = dot(a_turned, jnp.concatenate(d_queries, axis=0))
    g_pairs = dot(a_turned, jnp.concatenate(d_pairs, axis=0))
    square = -(-width // LANES)
    column = jnp.broadcast_to(g_norm, (8, width)).T[:, :1]
    for t, tile in enumerate(head_tiles(g_query)):
        if t == square - 1:
            tile = with_column(tile, column)
        put(g_ref, attn_place(t), width, tile.astype(bf16))
    for g in range(KV_HEADS):
        tile = g_pairs[:, g * LANES : (g + 1) * LANES]
        put(g_ref, attn_place(square + g), width, tile.astype(bf16))
    for t in range(square):
        put(g_ref, attn_place(square + KV_HEADS + t), width, g_out_ref[t])
    clear_rest(g_ref, 2 * square + KV_HEADS, width)
    keep_ref[...] = g_ref[core[0]]
    send_ref[...] = g_ref[1 - core[0]]


def clear_rest(g_ref, places, width):
    for half in range(2):
        used = (places + 1 - half) // 2 * width
        left_over = g_ref.shape[1] - used
        if left_over:
            g_ref[half, used:, :] = jnp.zeros((left_over, LANES), bf16)


def units_last_call(
    ids, x, a, norm, w_query, w_key, w_value, cos, sin, d_mid, last_d_q, g_out, messages, parts, core
):
    seqs, width, rows = x.shape
    count = len(messages)
    vmem = pl.BlockSpec(memory_space=pltpu.VMEM)
    smem = pl.BlockSpec(memory_space=pltpu.SMEM)
    places = -(-(2 * -(-width // LANES) + KV_HEADS) // 2)
    half = jax.ShapeDtypeStruct((half_rows(places, width, parts), LANES), bf16)
    return pl.pallas_call(
        functools.partial(units_last_kernel, count),
        in_specs=[smem] + [vmem] * (11 + count) + [smem],
        out_shape=[
            jax.ShapeDtypeStruct((seqs, width, rows), bf16),
            half,
            half,
        ],
        scratch_shapes=[pltpu.VMEM((2,) + half.shape, bf16), pltpu.VMEM((count + 1, rows * 5 // 2, LANES), bf16)],
        compiler_params=params(60),
        name="last_part",
    )(ids, x, a, norm, w_query, w_key, w_value, cos, sin, d_mid, last_d_q, g_out, *messages, core)


def to_all(messages):
    count = len(messages)
    return [messages[0]] + [
        lax.ppermute(messages[t], "seq", [(i, (i + t) % count) for i in range(count)])
        for t in range(1, count)
    ]


def rope_tables(positions):
    half = HEAD_DIM // 2
    lane = jnp.arange(LANES, dtype=jnp.int32)
    frequency = jnp.exp((lane % half).astype(f32) * (-math.log(10000.0) / half))
    angles = positions.T.astype(f32)[..., None] * frequency
    return jnp.cos(angles), jnp.where(lane % HEAD_DIM < half, -1.0, 1.0) * jnp.sin(angles)


def spread_layer(
    x, cot, cos, sin, norm_one, norm_two, w_query, wk_turned, wv_turned, w_out, w_gate, w_up,
    w_down_turned, count, devices, sum_over, places_ok,
):
    seqs, width, rows = x.shape
    me = lax.axis_index("seq")
    a, q, kv = pre_call(x, norm_one, w_query, wk_turned, wv_turned, cos, sin)
    rounds, numbers = gather_blocks(kv, count)
    last = len(rounds) - 2

    def ids_of(picked):
        return jnp.stack([me] + [k for part in picked for k in part]).astype(jnp.int32)

    state = forward_call(ids_of(numbers[:last]), q, kv, rounds[:last], None, False)
    far, far_ids = rounds[last:], ids_of(numbers[last:])
    attn, log_total = forward_call(far_ids, q, None, far, state, True)
    (block_out, b, hid, d_gate, d_up, d_mid, d_proj, d_out, delta, g_norm_mlp) = middle_call(
        x, cot, attn, w_out, norm_two, w_gate, w_up, w_down_turned
    )
    flat = lambda t: t.reshape(seqs * rows, t.shape[-1])
    g_ffn = ffn_grad_call(flat(b), cot, flat(hid), flat(d_gate), flat(d_up))
    g_ffn = lax.psum(g_ffn, ("seq", "batch"))
    common = (q, d_out, log_total, delta)
    _, far_terms, d_query = backward_call(far_ids, *common, None, far, None, None)
    far_terms = [jnp.concatenate([t, u], axis=0) for t, u in zip(*far_terms)]
    got = [return_round(far_terms, last, count)]
    _, mid_terms, d_query = backward_call(
        ids_of(numbers[last - 1 : last]), *common, None, rounds[last - 1 : last], d_query, None
    )
    half = far_terms[0].shape[0] // 2
    mid_terms = [add_low(t, g[half:]) for t, g in zip(mid_terms[0], got[0])]
    got.append(return_round(mid_terms, last - 1, count))
    own_terms, near_terms, d_q = backward_call(
        ids_of(numbers[: last - 1]), *common, kv, rounds[: last - 1], d_query, (cos, sin),
        tuple(mid_terms),
    )
    for r in reversed(range(last - 1)):
        size = 1 << r
        terms = [
            add_low(t, *(g[s][size : 2 * size] for g in got)) for s, t in enumerate(near_terms[r])
        ]
        got.append(return_round(terms, r, count))
    d_kv = jnp.concatenate(
        [add_low(own_terms[s : s + 1], *(g[s][:1] for g in got)) for s in range(seqs)], axis=0
    )
    d_aq, g_query, g_out = query_grad_call(
        flat(a), flat(attn), flat(d_proj), flat(d_q), g_norm_mlp, w_query
    )
    d_tokens, g_attn = last_call(
        x, a, norm_one, wk_turned, wv_turned, cos, sin, d_kv,
        d_aq.reshape(seqs, rows, width), d_mid, g_query, g_out, devices,
    )
    return block_out, d_tokens, g_ffn, sum_over(g_attn)


def units_layer(
    x, cot, cos, sin, norm_one, norm_two, w_query, wk_turned, wv_turned, w_out, w_gate, w_up,
    w_down_turned, count, devices, sum_over, places_ok,
):
    seqs, width, rows = x.shape
    flat = lambda t: t.reshape(seqs * rows, t.shape[-1])
    ids = lax.axis_index("seq").astype(jnp.int32).reshape(1)
    messages, a, last_q, last_kv = units_pre_call(
        ids, x, norm_one, w_query, wk_turned, wv_turned, cos, sin, count
    )
    masks = exchange_masks(count)
    swap = lambda part, mask: lax.ppermute(part, "seq", [(i, i ^ mask) for i in range(count)])
    last_kv = jnp.concatenate([last_kv, swap(last_kv, masks[0])], axis=0)
    arrived, last_kv = lax.optimization_barrier((to_all(messages), last_kv))
    first, *later = masks[1:]
    last_kv = jnp.concatenate([last_kv, swap(last_kv, first)], axis=0)
    attn_out, log_total, q, kv = units_forward_call(ids, arrived, ())
    for mask in later:
        last_kv = jnp.concatenate([last_kv, swap(last_kv, mask)], axis=0)
    last_attn, last_log = last_unit_forward_call(ids, last_q, last_kv)
    mid, attn, hid, d_gate, d_up, g_ffn = units_ffn_call(
        ids, x, cot, to_all(attn_out), last_attn, w_out, norm_two, w_gate, w_up, w_down_turned
    )
    g_ffn = lax.psum(g_ffn, ("seq", "batch"))

    def backward(mid, attn, hid, d_gate, d_up, q, kv, attn_out, log_total, last_attn, last_log, a):
        d_messages, d_mid, d_last, g_norm_mlp = units_back_call(
            ids, mid, cot, d_gate, d_up, norm_two, w_out, w_gate, w_up, count
        )
        block_out, g_out = units_out_call(mid, attn, hid, d_mid, g_norm_mlp, w_down_turned)
        last_d_kv, last_d_q = last_unit_backward_call(
            ids, last_q, last_kv, d_last[0], last_attn[0], last_log
        )
        d_all = units_backward_call(
            ids, to_all(d_messages), q, kv, attn_out, log_total, last_d_kv
        )
        core = (lax.axis_index("batch") & 1).astype(jnp.int32).reshape(1)
        d_tokens, keep, send = units_last_call(
            ids, x, a, norm_one, w_query, wk_turned, wv_turned, cos, sin, d_mid, last_d_q, g_out,
            to_all(d_all), devices, core,
        )
        return (block_out, d_tokens) + sum_over(add_low(keep, swap_with(send, 1, devices)), 1)

    block_out, d_tokens, *attn_sums = in_one_piece(
        places_ok,
        backward,
        (mid, attn, hid, d_gate, d_up, q, kv, attn_out, log_total, last_attn, last_log, a),
    )
    return block_out, d_tokens, g_ffn, attn_sums


def in_one_piece(always, part, operands):
    shapes = jax.eval_shape(part, *operands)

    def never(*_):
        return jax.tree.map(lambda t: jnp.zeros(t.shape, t.dtype), shapes)

    return lax.cond(always, part, never, *operands)


def on_device(
    tokens,
    positions,
    norm_attn,
    w_query,
    w_key,
    w_value,
    w_out,
    norm_mlp,
    w_gate,
    w_up,
    w_down,
    cotangent,
):
    rows, seqs, width = tokens.shape
    hidden = w_gate.shape[1]
    kv_width = KV_HEADS * HEAD_DIM
    count, batches = lax.axis_size("seq"), lax.axis_size("batch")
    me = lax.axis_index("seq")
    devices = count * batches
    stages = device_stages(count, batches)
    places = stage_places(stages, me * batches + lax.axis_index("batch"))
    x = jnp.transpose(tokens, (1, 2, 0))
    cot = jnp.transpose(cotangent, (1, 2, 0))
    wk_turned, wv_turned, w_down_turned = w_key.T, w_value.T, w_down.T
    cos, sin = rope_tables(positions)
    norm_one, norm_two = norm_attn, norm_mlp
    def sum_over(value, done=0):
        for stage, place in zip(stages[done:], places[done:]):
            value = scatter_stage(value, stage, place, devices)
        return gather_sums(value, stages, places, devices, 1)

    layer = units_layer if count == seqs * KV_HEADS - 1 else spread_layer
    block_out, d_tokens, g_ffn, attn_sums = layer(
        x, cot, cos, sin, norm_one, norm_two, w_query, wk_turned, wv_turned, w_out, w_gate, w_up,
        w_down_turned, count, devices, sum_over, positions[0, 0] >= 0,
    )
    side = places[0].reshape(1).astype(jnp.int32)
    g_gate, g_up, g_down = ffn_unfold_call(g_ffn, width, hidden)
    g_query, g_key, g_value, g_norm_attn, g_out, g_norm_mlp = unfold_call(
        attn_unfold_kernel,
        "attn_unfold",
        (side, *attn_sums),
        [(width, width), (kv_width, width), (kv_width, width), (width,)]
        + [(width, width), (width,)],
    )
    return (
        jnp.transpose(block_out, (2, 0, 1)),
        jnp.transpose(d_tokens, (2, 0, 1)),
        g_norm_attn,
        g_query,
        g_key.T,
        g_value.T,
        g_out,
        g_norm_mlp,
        g_gate,
        g_up,
        g_down.T,
    )


def solution(mesh):
    split = P("seq", "batch", None)
    return jax.shard_map(
        on_device,
        mesh=mesh,
        in_specs=(split, P("seq", "batch")) + (P(),) * 9 + (split,),
        out_specs=(split, split) + (P(),) * 9,
        check_vma=False,
    )
```
